32 devices in a mesh: tok: 16 (over z, y, x), rep: 2 (over core).
Axes of the slice: x: 2, y: 2, z: 4, core: 2. Of those that a mesh axis runs over, the one named last changes fastest.
Arguments:
- tokens: bfloat16 [2, 4096, 1024], P('rep', 'tok'), may hold values from -6 to 6
- cotangent: bfloat16 [2, 4096, 1024], P('rep', 'tok'), may hold values from -6 to 6
- lengths: int32 [2, 16], P('rep'), may hold values from 1 to 3586, as said below
- up_weight: float32 [1024, 3072], P(('tok', 'rep')), may hold values from -0.1875 to 0.1875
- value_weight: float32 [1024, 512], P(('tok', 'rep')), may hold values from -0.1875 to 0.1875
- expand_weight: float32 [512, 3072], P(('tok', 'rep')), may hold values from -0.25 to 0.25
- down_weight: float32 [3072, 1024], P(('tok', 'rep')), may hold values from -0.109375 to 0.109375
- norm_params: float32 [2, 1024], P(None, ('tok', 'rep')), may hold values from -3 to 3
- state_params: float32 [2, 512, 512], P(None, 'tok'), may hold values from -0.02 to 0.02
- state_poles: float32 [2, 512, 512], P(None, 'tok'), may hold values from -9 to 1
- up_mean: float32 [1024, 3072], P(('tok', 'rep')), may hold values from -20 to 20
- up_square: float32 [1024, 3072], P(('tok', 'rep')), may hold values from 0.49152 to 8.02816
- value_mean: float32 [1024, 512], P(('tok', 'rep')), may hold values from -32 to 32
- value_square: float32 [1024, 512], P(('tok', 'rep')), may hold values from 1.2288 to 19.6608
- expand_mean: float32 [512, 3072], P(('tok', 'rep')), may hold values from -24 to 24
- expand_square: float32 [512, 3072], P(('tok', 'rep')), may hold values from 0.589824 to 9.4208
- down_mean: float32 [3072, 1024], P(('tok', 'rep')), may hold values from -40 to 40
- down_square: float32 [3072, 1024], P(('tok', 'rep')), may hold values from 1.72032 to 27.8528
- norm_mean: float32 [2, 1024], P(None, ('tok', 'rep')), may hold values from -40 to 40
- norm_square: float32 [2, 1024], P(None, ('tok', 'rep')), may hold values from 2.12992 to 33.5872
- state_mean: float32 [2, 512, 512], P(None, 'tok')
- state_square: float32 [2, 512, 512], P(None, 'tok')
Outputs:
- layer_out: bfloat16 [2, 4096, 1024], P('rep', 'tok')
- token_grad: float32 [2, 4096, 1024], P('rep', 'tok')
- up_next: float32 [1024, 3072], P(('tok', 'rep'))
- up_mean_next: float32 [1024, 3072], P(('tok', 'rep'))
- up_square_next: float32 [1024, 3072], P(('tok', 'rep'))
- value_next: float32 [1024, 512], P(('tok', 'rep'))
- value_mean_next: float32 [1024, 512], P(('tok', 'rep'))
- value_square_next: float32 [1024, 512], P(('tok', 'rep'))
- expand_next: float32 [512, 3072], P(('tok', 'rep'))
- expand_mean_next: float32 [512, 3072], P(('tok', 'rep'))
- expand_square_next: float32 [512, 3072], P(('tok', 'rep'))
- down_next: float32 [3072, 1024], P(('tok', 'rep'))
- down_mean_next: float32 [3072, 1024], P(('tok', 'rep'))
- down_square_next: float32 [3072, 1024], P(('tok', 'rep'))
- norm_next: float32 [2, 1024], P(None, ('tok', 'rep'))
- norm_mean_next: float32 [2, 1024], P(None, ('tok', 'rep'))
- norm_square_next: float32 [2, 1024], P(None, ('tok', 'rep'))
- state_next: float32 [2, 512, 512], P(None, 'tok')
- state_mean_next: float32 [2, 512, 512], P(None, 'tok')
- state_square_next: float32 [2, 512, 512], P(None, 'tok')
The draws below stay inside these ranges and needn't reach their ends.
Inputs may be any that keep to these rules, and one draw needn't show every extreme that they name: `lengths`: each row sums to 4096; a group's items lie end to end in its tokens in the order given; each group has one item of exactly 3586 tokens.
All inputs are finite; a program needn't handle non-finite values.
Results may differ from the reference program's by a relative error of at most 0.005.
Values may be sent and summed in bfloat16 or wider, within the bound.
No kernel may reach another device: no remote copies, remote signals or barrier semaphores. Data moves between devices by JAX's collectives and lax.ppermute only.
A program may use at most 256 MiB of HBM per device.

```python
import math
import jax
import jax.numpy as jnp
from jax import lax

D = 1024
HID = 3072
CH = 512
NS = 512
BLOCK = 128
ITEMS = 16
STEP = 5
TOK_DEV = 256
GROUPS = 2
TOK_GROUP = 4096
TOKENS = 8192
MOST_LEN = 3586


def rates_of(key):
    return jax.random.uniform(jax.random.fold_in(key, 11), (CH, NS), jnp.float32, -9.0, -3.4)


def grad_scales(key):
    speed_rate = jnp.maximum(jnp.exp(rates_of(key)), 1.0 / 2000.0)
    inv_root = lax.rsqrt(speed_rate)
    stacked = jnp.stack([0.66 * inv_root, 0.66 * inv_root])
    return stacked * TOKENS ** 0.5


def draw_state_poles(key, part):
    decay_log = rates_of(key)
    key = jax.random.fold_in(key, 12)
    frequency = jax.random.uniform(key, (CH, NS), jnp.float32, -1.0, 1.0)
    return jnp.stack([decay_log, frequency])


def draw_state_params(key, part):
    key = jax.random.fold_in(key, 13)
    return 0.003 * jnp.clip(jax.random.normal(key, (2, CH, NS), jnp.float32), -6.0, 6.0)


def draw_state_mean(key, part):
    scales = grad_scales(key)
    key = jax.random.fold_in(key, 14)
    noise = jnp.clip(jax.random.normal(key, (2, CH, NS), jnp.float32), -6.0, 6.0)
    return 0.111 * scales * noise


def draw_state_square(key, part):
    scales = grad_scales(key)
    key = jax.random.fold_in(key, 15)
    factor = jnp.exp(jax.random.uniform(key, (2, CH, NS), jnp.float32, -0.7, 2.08))
    return 0.001 * factor * scales * scales


def draw_norm_params(key, part):
    gain_row = jnp.exp(jax.random.uniform(jax.random.fold_in(key, 21), (D,), jnp.float32, -0.7, 0.7))
    shift_row = 0.3 * jnp.clip(jax.random.normal(jax.random.fold_in(key, 22), (D,), jnp.float32), -6.0, 6.0)
    return jnp.stack([gain_row, shift_row])


def length_row(key):
    half = TOK_DEV - 1
    order = jax.random.permutation(key, 2 * TOK_DEV - 4)[:ITEMS - 3].astype(jnp.int32)
    picks = jnp.where(order + 1 < half, order + 1, order + 2).astype(jnp.int32)
    cuts = jnp.sort(jnp.concatenate([picks, jnp.full((1,), half, jnp.int32)]))
    bounds = jnp.concatenate([jnp.zeros((1,), jnp.int32), cuts, jnp.full((1,), 2 * half, jnp.int32)])
    pieces = bounds[1:] - bounds[:-1]
    place = jnp.sum((cuts <= half).astype(jnp.int32))
    index_row = jnp.arange(ITEMS, dtype=jnp.int32)
    before = pieces[jnp.minimum(index_row, ITEMS - 2)]
    after = pieces[jnp.maximum(index_row - 1, 0)]
    longest = jnp.full((ITEMS,), MOST_LEN, jnp.int32)
    return jnp.where(index_row < place, before, jnp.where(index_row == place, longest, after)).astype(jnp.int32)


def draw_lengths(key, part):
    rows = [length_row(jax.random.fold_in(key, 31 + group_index)) for group_index in range(GROUPS)]
    return jnp.stack(rows)


def shard_levels(rng, dims, shards, low, largest):
    def one(position, shards_of):
        heights = jax.random.uniform(jax.random.fold_in(jax.random.fold_in(rng, 6), position), (shards_of,), jnp.float32, low / len(shards), largest / len(shards))
        return jnp.repeat(jnp.exp(heights), dims[position] // shards_of).reshape((-1,) + (1,) * (len(dims) - position - 1))

    level = one(*shards[0])
    for cut in shards[1:]:
        level = level * one(*cut)
    return level


def gaussian(own_key, extent, width, bound, cuts=(), kind=jnp.bfloat16):
    entries = width * jax.random.normal(own_key, extent, jnp.float32)
    if cuts:
        entries = entries * shard_levels(own_key, extent, cuts, -0.22, 0.18)
    return jnp.clip(entries, -bound, bound).astype(kind)


def setup_inputs(seed: int = 0) -> dict:
    streams_of = jax.random.split(jax.random.key(seed), 23)
    return {
        "tokens": gaussian(streams_of[0], (GROUPS, TOK_GROUP, D), 1.0, 6.0, ((0, 2), (1, 16))),
        "cotangent": gaussian(streams_of[1], (GROUPS, TOK_GROUP, D), 1.0, 6.0, ((0, 2), (1, 16))),
        "lengths": draw_lengths(jax.random.fold_in(streams_of[22], 71), 0),
        "up_weight": gaussian(streams_of[3], (D, HID), D ** -0.5, 0.1875, ((0, 32),), jnp.float32),
        "value_weight": gaussian(streams_of[4], (D, CH), D ** -0.5, 0.1875, ((0, 32),), jnp.float32),
        "expand_weight": gaussian(streams_of[5], (CH, HID), CH ** -0.5, 0.25, ((0, 32),), jnp.float32),
        "down_weight": gaussian(streams_of[6], (HID, D), HID ** -0.5, 0.109375, ((0, 32),), jnp.float32),
        "norm_params": draw_norm_params(jax.random.fold_in(streams_of[22], 71), 0),
        "state_params": draw_state_params(jax.random.fold_in(streams_of[22], 71), 0),
        "state_poles": draw_state_poles(jax.random.fold_in(streams_of[22], 71), 0),
        "up_mean": gaussian(streams_of[10], (D, HID), (0.039 * TOKENS ** 0.5), 20.0, ((0, 32),), jnp.float32),
        "up_square": jnp.clip(jnp.exp(math.log(8.02816) - 2.79320805 * jax.random.uniform(streams_of[11], (D, HID), jnp.float32) ** shard_levels(streams_of[11], (D, HID), ((0, 32),), -0.2, 0.2)), 0.49152, 8.02816),
        "value_mean": gaussian(streams_of[12], (D, CH), (0.061 * TOKENS ** 0.5), 32.0, ((0, 32),), jnp.float32),
        "value_square": jnp.clip(jnp.exp(math.log(19.6608) - 2.7725887 * jax.random.uniform(streams_of[13], (D, CH), jnp.float32) ** shard_levels(streams_of[13], (D, CH), ((0, 32),), -0.2, 0.2)), 1.2288, 19.6608),
        "expand_mean": gaussian(streams_of[14], (CH, HID), (0.042 * TOKENS ** 0.5), 24.0, ((0, 32),), jnp.float32),
        "expand_square": jnp.clip(jnp.exp(math.log(9.4208) - 2.7708511 * jax.random.uniform(streams_of[15], (CH, HID), jnp.float32) ** shard_levels(streams_of[15], (CH, HID), ((0, 32),), -0.2, 0.2)), 0.589824, 9.4208),
        "down_mean": gaussian(streams_of[16], (HID, D), (0.072 * TOKENS ** 0.5), 40.0, ((0, 32),), jnp.float32),
        "down_square": jnp.clip(jnp.exp(math.log(27.8528) - 2.784423 * jax.random.uniform(streams_of[17], (HID, D), jnp.float32) ** shard_levels(streams_of[17], (HID, D), ((0, 32),), -0.2, 0.2)), 1.72032, 27.8528),
        "norm_mean": gaussian(streams_of[18], (2, D), (0.08 * TOKENS ** 0.5), 40.0, ((1, 32),), jnp.float32),
        "norm_square": jnp.clip(jnp.exp(math.log(33.5872) - 2.7580606 * jax.random.uniform(streams_of[19], (2, D), jnp.float32) ** shard_levels(streams_of[19], (2, D), ((1, 32),), -0.2, 0.2)), 2.12992, 33.5872),
        "state_mean": draw_state_mean(jax.random.fold_in(streams_of[22], 71), 0),
        "state_square": draw_state_square(jax.random.fold_in(streams_of[22], 71), 0),
    }


@jax.custom_vjp
def low(v):
    return lax.optimization_barrier(v.astype(jnp.bfloat16)).astype(jnp.float32)

@jax.custom_vjp
def low_back(v):
    return v

def low_keep(v):
    return (low(v), None)

def low_pass(kept, grad):
    return (grad,)

def back_keep(v):
    return (v, None)

def back_low(kept, grad):
    return (low(grad),)
low.defvjp(low_keep, low_pass)
low_back.defvjp(back_keep, back_low)
epsilon_norm = 1e-05
epsilon_adam = 1e-08
beta_first = 0.9
beta_second = 0.999

def gelu_curve(values):
    return jax.nn.gelu(values, approximate=True)

def layer_norm(rows, norm_weights):
    average = lax.optimization_barrier(jnp.mean(rows, axis=-1, keepdims=True))
    centered = rows - average
    variance = lax.optimization_barrier(jnp.mean(centered * centered, axis=-1, keepdims=True))
    return centered * lax.rsqrt(variance + epsilon_norm) * norm_weights[0] + norm_weights[1]

def segments_of(lengths_row, length):
    ends = jnp.cumsum(lengths_row, dtype=jnp.int32)
    positions = jnp.arange(length, dtype=jnp.int32)
    return lax.optimization_barrier(jnp.sum((positions[:, None] >= ends[None, :]).astype(jnp.int32), axis=1, dtype=jnp.int32))

def ssm_channels(values, params, segment):
    highest_precision = lax.Precision.HIGHEST
    channels, length = values.shape
    block_len = BLOCK
    blocks = length // block_len
    decay_rate = jnp.exp(params[0])
    frequency = params[1]
    coef_real = params[2]
    coef_imag = params[3]
    lag_values = jnp.arange(block_len + 1, dtype=jnp.float32)
    magnitude = jnp.exp(-decay_rate[:, None, :] * lag_values[None, :, None])
    phase = frequency[:, None, :] * lag_values[None, :, None]
    power_real_part = magnitude * jnp.cos(phase)
    power_imaginary = magnitude * jnp.sin(phase)
    kernel = lax.optimization_barrier(jnp.sum(coef_real[:, None, :] * power_real_part[:, :block_len] - coef_imag[:, None, :] * power_imaginary[:, :block_len], axis=2))
    row_index = jnp.arange(block_len, dtype=jnp.int32)
    lag_index = row_index[:, None] - row_index[None, :]
    toeplitz = jnp.where((lag_index >= 0)[None], kernel[:, jnp.maximum(lag_index, 0)], jnp.float32(0.0))
    seg_blocks = segment.reshape(blocks, block_len)
    last_seg = seg_blocks[:, block_len - 1]
    prev_seg = jnp.concatenate([jnp.full((1,), -1, jnp.int32), last_seg[:-1]])
    value_blocks = values.reshape(channels, blocks, block_len)
    tail_mask = (seg_blocks == last_seg[:, None]).astype(jnp.float32)
    trailing_values = value_blocks * tail_mask[None]
    reversed_real_part = power_real_part[:, block_len - 1::-1]
    reversed_imaginary = power_imaginary[:, block_len - 1::-1]
    input_real_part = jnp.einsum('fwz,fzx->fwx', trailing_values, reversed_real_part, precision=highest_precision)
    input_imaginary = jnp.einsum('fwz,fzx->fwx', trailing_values, reversed_imaginary, precision=highest_precision)
    carry_flag = (last_seg == prev_seg).astype(jnp.float32)
    step_real = power_real_part[:, block_len][:, None, :] * carry_flag[None, :, None]
    step_imag = power_imaginary[:, block_len][:, None, :] * carry_flag[None, :, None]

    def combine(earlier, later):
        return (later[0] * earlier[0] - later[1] * earlier[1], later[0] * earlier[1] + later[1] * earlier[0], later[0] * earlier[2] - later[1] * earlier[3] + later[2], later[0] * earlier[3] + later[1] * earlier[2] + later[3])
    states = lax.associative_scan(combine, (step_real, step_imag, input_real_part, input_imaginary), axis=1)
    end_real = states[2]
    end_imag = states[3]
    start_real = jnp.concatenate([jnp.zeros_like(end_real[:, :1]), end_real[:, :-1]], axis=1)
    start_imag = jnp.concatenate([jnp.zeros_like(end_imag[:, :1]), end_imag[:, :-1]], axis=1)
    mixed_real_part = coef_real[:, None, :] * start_real - coef_imag[:, None, :] * start_imag
    mixed_imaginary = coef_real[:, None, :] * start_imag + coef_imag[:, None, :] * start_real
    carried_state = jnp.einsum('zgv,zqv->zgq', mixed_real_part, power_real_part[:, 1:], precision=highest_precision)
    carried_state = carried_state - jnp.einsum('zgv,zqv->zgq', mixed_imaginary, power_imaginary[:, 1:], precision=highest_precision)
    alive = (seg_blocks == prev_seg[:, None]).astype(jnp.float32)
    carried_state = carried_state * alive[None]
    per_step = min(64, blocks)
    step_total = blocks // per_step
    value_steps = value_blocks.reshape(channels, step_total, per_step, block_len).transpose(1, 0, 2, 3)
    seg_steps = seg_blocks.reshape(step_total, per_step, block_len)

    def local_part(pieces):
        value_piece, seg_piece = pieces
        same_item = (seg_piece[:, :, None] == seg_piece[:, None, :]).astype(jnp.float32)
        return jnp.einsum('cbts,cbs->cbt', toeplitz[:, None] * same_item[None], value_piece, precision=highest_precision)
    local_terms = lax.map(jax.checkpoint(local_part), (value_steps, seg_steps))
    local_terms = local_terms.transpose(1, 0, 2, 3).reshape(channels, blocks, block_len)
    return (carried_state + local_terms).reshape(channels, length)

def state_mix(channel_values, params, segment):
    grouped = channel_values.reshape(CH // 4, 4, TOK_GROUP)
    param_groups = params.reshape(4, CH // 4, 4, NS).transpose(1, 0, 2, 3)

    def one_group(pieces):
        return ssm_channels(pieces[0], pieces[1], segment)
    result = lax.map(jax.checkpoint(one_group), (grouped, param_groups))
    return result.reshape(CH, TOK_GROUP)

def adam_step(weight, gradient, first_moment, second, step_value, step_rate, decay_rate):
    first_new = beta_first * first_moment + (1.0 - beta_first) * gradient
    second_new = beta_second * second + (1.0 - beta_second) * gradient * gradient
    first_hat = first_new / (1.0 - jnp.power(beta_first, step_value))
    second_hat = second_new / (1.0 - jnp.power(beta_second, step_value))
    weight_new = weight - step_rate * (first_hat / (jnp.sqrt(second_hat) + epsilon_adam) + decay_rate * weight)
    return (weight_new, first_new, second_new)

def reference(tokens, cotangent, lengths, up_weight, value_weight, expand_weight, down_weight, norm_params, state_params, state_poles, up_mean, up_square, value_mean, value_square, expand_mean, expand_square, down_mean, down_square, norm_mean, norm_square, state_mean, state_square):
    highest_precision = lax.Precision.HIGHEST
    segments = jax.vmap(lambda lengths_row: segments_of(lengths_row, TOK_GROUP))(lengths)

    def forward(token_rows, up_w, value_matrix, expand_w, down_w, norm_w, coef_w):
        norm_low = low(norm_w)
        normalized_rows = low(layer_norm(token_rows, norm_low))
        up_pre = low_back(jnp.einsum('gld,dh->glh', normalized_rows, low(up_w), precision=highest_precision))
        upper = gelu_curve(up_pre)
        value_preactivation = low_back(jnp.einsum('irt,tk->irk', normalized_rows, low(value_matrix), precision=highest_precision))
        value_act = low(low_back(gelu_curve(value_preactivation)))
        state_in = value_act.transpose(0, 2, 1)
        all_params = jnp.concatenate([state_poles, coef_w], axis=0)
        state_out = jnp.stack([state_mix(state_in[index_group], all_params, segments[index_group]) for index_group in range(GROUPS)])
        state_sent = low(low_back(state_out))
        expanded = low_back(jnp.einsum('gcl,ch->glh', state_sent, low(expand_w), precision=highest_precision))
        gated = low(upper * expanded)
        return token_rows + jnp.einsum('glh,hd->gld', gated, low(down_w), precision=highest_precision)
    primals = (tokens.astype(jnp.float32), up_weight, value_weight, expand_weight, down_weight, norm_params, state_params)
    layer_rows, pullback = jax.vjp(forward, *primals)
    grads = pullback(cotangent.astype(jnp.float32))
    step_value = jnp.float32(STEP)
    up_next, up_mean_next, up_square_next = adam_step(up_weight, grads[1], up_mean, up_square, step_value, 0.08, 0.1)
    value_next, value_mean_next, value_square_next = adam_step(value_weight, grads[2], value_mean, value_square, step_value, 0.08, 0.1)
    expand_next, expand_mean_next, expand_square_next = adam_step(expand_weight, grads[3], expand_mean, expand_square, step_value, 0.08, 0.1)
    down_next, down_mean_next, down_square_next = adam_step(down_weight, grads[4], down_mean, down_square, step_value, 0.08, 0.1)
    norm_next, norm_mean_next, norm_square_next = adam_step(norm_params, grads[5], norm_mean, norm_square, step_value, 1.0, 0.0)
    state_next, state_mean_next, state_square_next = adam_step(state_params, grads[6], state_mean, state_square, step_value, 0.006, 0.0)
    return (layer_rows.astype(jnp.bfloat16), grads[0], up_next, up_mean_next, up_square_next, value_next, value_mean_next, value_square_next, expand_next, expand_mean_next, expand_square_next, down_next, down_mean_next, down_square_next, norm_next, norm_mean_next, norm_square_next, state_next, state_mean_next, state_square_next)
```

```python
import functools

import jax
import jax.numpy as jnp
from jax import lax
from jax.experimental import pallas as pl
from jax.experimental.pallas import tpu as pltpu
from jax.sharding import PartitionSpec as P

BLOCK = 128
STEP = 5


epsilon_norm = 1e-05
epsilon_adam = 1e-08
beta_first = 0.9
beta_second = 0.999


def gelu_curve(values):
    return jax.nn.gelu(values, approximate=True)


def layer_norm(rows, norm_weights):
    average = jnp.mean(rows, axis=-1, keepdims=True)
    centered = rows - average
    variance = jnp.mean(centered * centered, axis=-1, keepdims=True)
    return centered * lax.rsqrt(variance + epsilon_norm) * norm_weights[0] + norm_weights[1]


def pieces_of(lengths_row, length):
    blocks = length // BLOCK
    items = lengths_row.shape[0]
    ends = jnp.cumsum(lengths_row, dtype=jnp.int32)
    heads = BLOCK * jnp.arange(blocks, dtype=jnp.int32)
    head_rank = jnp.arange(blocks, dtype=jnp.int32) + jnp.sum(
        (ends[None, :] < heads[:, None]).astype(jnp.int32), axis=1
    )
    end_rank = jnp.arange(items, dtype=jnp.int32) + jnp.sum(
        (heads[None, :] <= ends[:, None]).astype(jnp.int32), axis=1
    )
    places = jnp.arange(blocks + items, dtype=jnp.int32)[:, None]
    starts = jnp.sum(jnp.where(head_rank[None, :] == places, heads[None, :], 0), axis=1) + jnp.sum(
        jnp.where(end_rank[None, :] == places, ends[None, :], 0), axis=1
    )
    stops = jnp.concatenate([starts[1:], jnp.full((1,), length, jnp.int32)])
    owner = starts // BLOCK
    segment = jnp.sum((ends[None, :] <= starts[:, None]).astype(jnp.int32), axis=1)
    positions = owner[:, None] * BLOCK + jnp.arange(BLOCK, dtype=jnp.int32)[None, :]
    mask = (positions >= starts[:, None]) & (positions < stops[:, None])
    pick = owner[:, None] == jnp.arange(blocks, dtype=jnp.int32)[None, :]
    follows = (segment[1:] == segment[:-1]) & (owner[1:] != owner[:-1])
    follows = jnp.concatenate([jnp.zeros((1,), bool), follows])
    return (
        pick.astype(jnp.bfloat16),
        mask.astype(jnp.bfloat16),
        follows.astype(jnp.float32),
    )


def powers_of(poles):
    decay_rate = jnp.exp(poles[0])[:, None, :]
    frequency = poles[1][:, None, :]
    lags = jnp.array([0, 1, 2, 3, 4, 5, 6, 7, 8, 16, 32, 64, 128, 128, 128, 128], jnp.float32)
    lags = lags[None, :, None]
    magnitude = jnp.exp(-decay_rate * lags)
    phase = frequency * lags
    return jnp.concatenate([magnitude * jnp.cos(phase), magnitude * jnp.sin(phase)], axis=2)


def cmul(ar, ai, br, bi):
    return ar * br - ai * bi, ar * bi + ai * br


def fill_tables(c, states, low_ref, up_ref, down_ref):
    for lane in range(0, states, 128):
        re_lanes = pl.ds(lane, 128)
        im_lanes = pl.ds(states + lane, 128)
        base = low_ref[c, 0:8, re_lanes], low_ref[c, 0:8, im_lanes]
        for ref, forward in ((up_ref, True), (down_ref, False)):
            if forward:
                re, im = base
            else:
                re = jnp.concatenate([base[0][7 - k : 8 - k] for k in range(8)], axis=0)
                im = jnp.concatenate([base[1][7 - k : 8 - k] for k in range(8)], axis=0)
            for k in range(4):
                nr, ni = cmul(
                    re,
                    im,
                    low_ref[c, 8 + k : 9 + k, re_lanes],
                    low_ref[c, 8 + k : 9 + k, im_lanes],
                )
                if forward:
                    re = jnp.concatenate([re, nr], axis=0)
                    im = jnp.concatenate([im, ni], axis=0)
                else:
                    re = jnp.concatenate([nr, re], axis=0)
                    im = jnp.concatenate([ni, im], axis=0)
            ref[c, :, re_lanes] = re.astype(jnp.bfloat16)
            ref[c, :, im_lanes] = im.astype(jnp.bfloat16)


def nt(a, b):
    return lax.dot_general(a, b, (((1,), (1,)), ((), ())), preferred_element_type=jnp.float32)


def nn(a, b):
    return lax.dot_general(a, b, (((1,), (0,)), ((), ())), preferred_element_type=jnp.float32)


def tn(a, b):
    return lax.dot_general(a, b, (((0,), (0,)), ((), ())), preferred_element_type=jnp.float32)


def split_rows(row):
    high = row.astype(jnp.bfloat16)
    rest = (row - high.astype(jnp.float32)).astype(jnp.bfloat16)
    return high, rest


def toeplitz(kernel_row):
    spread = jnp.broadcast_to(kernel_row, (BLOCK, BLOCK))
    rolled = pltpu.roll(spread, 0, 1, stride=1, stride_axis=0)
    rows = lax.broadcasted_iota(jnp.int32, (BLOCK, BLOCK), 0)
    columns = lax.broadcasted_iota(jnp.int32, (BLOCK, BLOCK), 1)
    return jnp.where(columns >= rows, rolled, 0.0)


def put_rows(ref, c, places, group, block):
    for k in range(ref.shape[0]):
        ref[k, pl.ds(c, places, stride=group), :] = block[:, 128 * k : 128 * (k + 1)]


def get_rows(ref, c, places, group):
    chunks = [ref[k, pl.ds(c, places, stride=group), :] for k in range(ref.shape[0])]
    return jnp.concatenate([chunk.astype(jnp.bfloat16) for chunk in chunks], axis=1)


def get_step(ref, rows, half):
    count = ref.shape[0] // 2
    return jnp.concatenate([ref[half * count + k, rows, :] for k in range(count)], axis=1)


def put_step(ref, rows, half, block):
    count = ref.shape[0] // 2
    for k in range(count):
        ref[half * count + k, rows, :] = block[:, 128 * k : 128 * (k + 1)]


def forward_kernel(
    active, follows_ref, pick_ref, mask_ref, values_ref, low_ref, lam_ref, coef_ref,
    out_ref, start_ref, taps_ref, up_ref, down_ref, work_ref,
):
    places = pick_ref.shape[0]
    group, states = coef_ref.shape[0], coef_ref.shape[1] // 2
    if active < group:
        work_ref[...] = jnp.zeros_like(work_ref)
    mask = mask_ref[...]
    pick = pick_ref[...]
    for c in range(active):
        fill_tables(c, states, low_ref, up_ref, down_ref)
        spread = nn(pick, values_ref[c]).astype(jnp.bfloat16) * mask
        put_rows(work_ref, c, places, group, nn(spread, down_ref[c]))
    lam_re, lam_im = lam_ref[0, :, :states], lam_ref[0, :, states:]
    far_re, far_im = lam_ref[1, :, :states], lam_ref[1, :, states:]
    coef_re, coef_im = coef_ref[:, :states], coef_ref[:, states:]
    mix_re, mix_im = cmul(coef_re, coef_im, lam_re, lam_im)

    def advance(p, carry):
        re, im = carry
        rows = pl.ds(pl.multiple_of(p * group, group), group)
        keep = follows_ref[p]
        re, im = re * keep, im * keep
        start_ref[rows, :states] = re
        start_ref[rows, states:] = im
        far = cmul(re, im, far_re, far_im)
        new_re = far[0] + get_step(work_ref, rows, 0)
        new_im = far[1] + get_step(work_ref, rows, 1)
        mixed = cmul(re, im, mix_re, mix_im)
        put_step(work_ref, rows, 0, mixed[0])
        put_step(work_ref, rows, 1, -mixed[1])
        return new_re, new_im

    zero = jnp.zeros((group, states), jnp.float32)
    lax.fori_loop(0, places, advance, (zero, zero), unroll=4)
    for c in range(active):
        row = jnp.concatenate([coef_ref[c : c + 1, :states], -coef_ref[c : c + 1, states:]], axis=1)
        high, rest = split_rows(row)
        rows = jnp.concatenate([high, rest, jnp.zeros((14, 2 * states), jnp.bfloat16)], axis=0)
        mixed = get_rows(work_ref, c, places, group)
        carried = nt(jnp.concatenate([mixed, rows], axis=0), up_ref[c])
        kernel_row = carried[places : places + 1] + carried[places + 1 : places + 2]
        taps = toeplitz(kernel_row).astype(jnp.bfloat16)
        taps_ref[c] = taps
        spread = nn(pick, values_ref[c]).astype(jnp.bfloat16) * mask
        result = (carried[:places] + nn(spread, taps)).astype(jnp.bfloat16) * mask
        out_ref[c] = tn(pick, result).astype(jnp.bfloat16)


def backward_kernel(
    active, follows_ref, pick_ref, mask_ref, values_ref, grads_ref, low_ref, lam_ref, coef_ref,
    start_ref, taps_ref, out_ref, sum_ref, up_ref, down_ref, work_ref,
):
    places = pick_ref.shape[0]
    group, states = coef_ref.shape[0], coef_ref.shape[1] // 2
    if active < group:
        work_ref[...] = jnp.zeros_like(work_ref)
        sum_ref[...] = jnp.zeros_like(sum_ref)
    mask = mask_ref[...]
    pick = pick_ref[...]
    rows = lax.broadcasted_iota(jnp.int32, (BLOCK, BLOCK), 0)
    columns = lax.broadcasted_iota(jnp.int32, (BLOCK, BLOCK), 1)
    turn = (rows + columns == BLOCK - 1).astype(jnp.bfloat16)
    for c in range(active):
        fill_tables(c, states, low_ref, up_ref, down_ref)
        values = nn(pick, values_ref[c]).astype(jnp.bfloat16) * mask
        grads = nn(pick, grads_ref[c]).astype(jnp.bfloat16) * mask
        pairs = tn(nn(values, turn).astype(jnp.bfloat16), grads)
        skewed = pltpu.roll(pairs, 1, 1, stride=1, stride_axis=0)
        lag_sum = jnp.sum(jnp.where(columns <= rows, skewed, 0.0), axis=0, keepdims=True)
        high, rest = split_rows(lag_sum)
        extra = jnp.concatenate([high, rest, jnp.zeros((14, BLOCK), jnp.bfloat16)], axis=0)
        folded = nn(jnp.concatenate([grads, extra], axis=0), up_ref[c])
        put_rows(work_ref, c, places, group, folded[:places])
        sum_ref[c : c + 1, :] = folded[places : places + 1] + folded[places + 1 : places + 2]
    lam_re, lam_im = lam_ref[0, :, :states], lam_ref[0, :, states:]
    far_re, far_im = lam_ref[1, :, :states], lam_ref[1, :, states:]
    coef_re, coef_im = coef_ref[:, :states], coef_ref[:, states:]

    def retreat(step, carry):
        re, im, total_re, total_im = carry
        p = places - 1 - step
        rows = pl.ds(pl.multiple_of(p * group, group), group)
        near = cmul(get_step(work_ref, rows, 0), get_step(work_ref, rows, 1), lam_re, lam_im)
        begin = start_ref[rows, :states], start_ref[rows, states:]
        product = cmul(begin[0], begin[1], near[0], near[1])
        mixed = cmul(re, im, coef_re, coef_im)
        put_step(work_ref, rows, 0, mixed[0])
        put_step(work_ref, rows, 1, -mixed[1])
        keep = follows_ref[p]
        far = cmul(re, im, far_re, far_im)
        return (
            (near[0] + far[0]) * keep,
            (near[1] + far[1]) * keep,
            total_re + product[0],
            total_im + product[1],
        )

    zero = jnp.zeros((group, states), jnp.float32)
    _, _, total_re, total_im = lax.fori_loop(0, places, retreat, (zero, zero, zero, zero), unroll=4)
    sum_ref[:, :states] = sum_ref[:, :states] + total_re
    sum_ref[:, states:] = -(sum_ref[:, states:] + total_im)
    for c in range(active):
        mixed = get_rows(work_ref, c, places, group)
        grads = nn(pick, grads_ref[c]).astype(jnp.bfloat16) * mask
        result = nt(mixed, down_ref[c]) + nt(grads, taps_ref[c])
        out_ref[c] = tn(pick, result.astype(jnp.bfloat16) * mask).astype(jnp.bfloat16)


def whole(shape):
    return pl.BlockSpec(shape, lambda i: (0,) * len(shape))


def mixer_specs(active, group, blocks, places, states):
    return [
        pl.BlockSpec(memory_space=pltpu.SMEM),
        whole((places, blocks)),
        whole((places, BLOCK)),
        pl.BlockSpec((active, blocks, BLOCK), lambda i: (i, 0, 0)),
    ], [
        pl.BlockSpec((active, 16, 2 * states), lambda i: (i, 0, 0)),
        pl.BlockSpec((2, group, 2 * states), lambda i: (0, i, 0)),
        pl.BlockSpec((group, 2 * states), lambda i: (i, 0)),
    ]


def scratches(active, group, places, states):
    return [
        pltpu.VMEM((active, BLOCK, 2 * states), jnp.bfloat16),
        pltpu.VMEM((active, BLOCK, 2 * states), jnp.bfloat16),
        pltpu.VMEM((2 * states // 128, places * group, 128), jnp.float32),
    ]


def mix_forward(values, pieces, powers, lams, coefs):
    channels, blocks = values.shape[0], values.shape[1]
    pick, mask, follows = pieces
    places, states = pick.shape[0], coefs.shape[1] // 2
    group, active = 8, min(8, channels)
    spare = max(0, group - channels)
    lams = jnp.pad(lams, ((0, 0), (0, spare), (0, 0)))
    coefs = jnp.pad(coefs, ((0, spare), (0, 0)))
    first, last = mixer_specs(active, group, blocks, places, states)
    table = 2 * channels * places * BLOCK * 2 * states * 2
    return pl.pallas_call(
        functools.partial(forward_kernel, active),
        grid=(channels // active,),
        in_specs=first + last,
        out_specs=[
            pl.BlockSpec((active, blocks, BLOCK), lambda i: (i, 0, 0)),
            pl.BlockSpec((places * group, 2 * states), lambda i: (i, 0)),
            pl.BlockSpec((active, BLOCK, BLOCK), lambda i: (i, 0, 0)),
        ],
        out_shape=[
            jax.ShapeDtypeStruct((channels, blocks, BLOCK), jnp.bfloat16),
            jax.ShapeDtypeStruct((places * (channels + spare), 2 * states), jnp.float32),
            jax.ShapeDtypeStruct((channels, BLOCK, BLOCK), jnp.bfloat16),
        ],
        scratch_shapes=scratches(active, group, places, states),
        compiler_params=pltpu.CompilerParams(vmem_limit_bytes=48 * 2**20),
        cost_estimate=pl.CostEstimate(flops=20 * table, bytes_accessed=16 * 2**20, transcendentals=0),
        name="mix_forward",
    )(follows, pick, mask, values, powers, lams, coefs)


def mix_backward(values, grads, pieces, powers, lams, coefs, starts, taps):
    channels, blocks = values.shape[0], values.shape[1]
    pick, mask, follows = pieces
    places, states = pick.shape[0], coefs.shape[1] // 2
    group, active = 8, min(8, channels)
    spare = max(0, group - channels)
    lams = jnp.pad(lams, ((0, 0), (0, spare), (0, 0)))
    coefs = jnp.pad(coefs, ((0, spare), (0, 0)))
    first, last = mixer_specs(active, group, blocks, places, states)
    table = 2 * channels * places * BLOCK * 2 * states * 2
    result, sums = pl.pallas_call(
        functools.partial(backward_kernel, active),
        grid=(channels // active,),
        in_specs=first
        + [pl.BlockSpec((active, blocks, BLOCK), lambda i: (i, 0, 0))]
        + last
        + [
            pl.BlockSpec((places * group, 2 * states), lambda i: (i, 0)),
            pl.BlockSpec((active, BLOCK, BLOCK), lambda i: (i, 0, 0)),
        ],
        out_specs=[
            pl.BlockSpec((active, blocks, BLOCK), lambda i: (i, 0, 0)),
            pl.BlockSpec((group, 2 * states), lambda i: (i, 0)),
        ],
        out_shape=[
            jax.ShapeDtypeStruct((channels, blocks, BLOCK), jnp.bfloat16),
            jax.ShapeDtypeStruct((channels + spare, 2 * states), jnp.float32),
        ],
        scratch_shapes=scratches(active, group, places, states),
        compiler_params=pltpu.CompilerParams(vmem_limit_bytes=48 * 2**20),
        cost_estimate=pl.CostEstimate(flops=20 * table, bytes_accessed=16 * 2**20, transcendentals=0),
        name="mix_backward",
    )(follows, pick, mask, values, grads, powers, lams, coefs, starts, taps)
    return result, sums[:channels]


def mixer_inputs(poles, params):
    table = powers_of(poles)
    lams = jnp.stack([table[:, 1], table[:, 12]])
    coefs = jnp.concatenate([params[0], params[1]], axis=1)
    return table, lams, coefs


def adam_step(weight, gradient, first_moment, second, step_value, step_rate, decay_rate):
    first_new = beta_first * first_moment + (1.0 - beta_first) * gradient
    second_new = beta_second * second + (1.0 - beta_second) * gradient * gradient
    first_hat = first_new / (1.0 - jnp.power(beta_first, step_value))
    second_hat = second_new / (1.0 - jnp.power(beta_second, step_value))
    weight_new = weight - step_rate * (
        first_hat / (jnp.sqrt(second_hat) + epsilon_adam) + decay_rate * weight
    )
    return (weight_new, first_new, second_new)


def per_device(
    tokens,
    cotangent,
    lengths,
    up_weight,
    value_weight,
    expand_weight,
    down_weight,
    norm_params,
    state_params,
    state_poles,
    up_mean,
    up_square,
    value_mean,
    value_square,
    expand_mean,
    expand_square,
    down_mean,
    down_square,
    norm_mean,
    norm_square,
    state_mean,
    state_square,
):
    up_full, value_full, expand_full, down_full, norm_full = (
        lax.all_gather(up_weight.astype(jnp.bfloat16), ("tok", "rep"), axis=0, tiled=True),
        lax.all_gather(value_weight.astype(jnp.bfloat16), ("tok", "rep"), axis=0, tiled=True),
        lax.all_gather(expand_weight.astype(jnp.bfloat16), ("tok", "rep"), axis=0, tiled=True),
        lax.all_gather(down_weight.astype(jnp.bfloat16), ("tok", "rep"), axis=0, tiled=True),
        lax.all_gather(norm_params.astype(jnp.bfloat16), ("tok", "rep"), axis=1, tiled=True),
    )
    token_rows = tokens[0].astype(jnp.float32)
    normalized_rows, norm_back = jax.vjp(layer_norm, token_rows, norm_full.astype(jnp.float32))
    normed_low = normalized_rows.astype(jnp.bfloat16)
    up_pre = jnp.dot(normed_low, up_full, preferred_element_type=jnp.float32)
    upper, upper_back = jax.vjp(gelu_curve, up_pre)
    value_preactivation = jnp.einsum(
        "td,dc->ct", normed_low, value_full, preferred_element_type=jnp.float32
    )
    value_act, value_back = jax.vjp(gelu_curve, value_preactivation)
    channel_values = lax.all_to_all(
        value_act.astype(jnp.bfloat16), "tok", split_axis=0, concat_axis=1, tiled=True
    )
    channels, length = channel_values.shape
    blocked = (channels, length // BLOCK, BLOCK)
    pieces = pieces_of(lengths[0], length)
    powers, lams, coefs = mixer_inputs(state_poles, state_params)
    channel_values = channel_values.reshape(blocked)
    state_out, starts, taps = mix_forward(channel_values, pieces, powers, lams, coefs)
    token_states = lax.all_to_all(
        state_out.reshape(channels, length), "tok", split_axis=1, concat_axis=0, tiled=True
    )
    expanded = jnp.einsum(
        "ct,ch->th", token_states, expand_full, preferred_element_type=jnp.float32
    )
    gated_low = (upper * expanded).astype(jnp.bfloat16)
    layer_rows = token_rows + jnp.dot(gated_low, down_full, preferred_element_type=jnp.float32)
    layer_out = layer_rows.astype(jnp.bfloat16)[None]
    grad_rows = cotangent[0]
    down_grad = jnp.einsum("th,td->hd", gated_low, grad_rows, preferred_element_type=jnp.float32)
    gated_grad = jnp.einsum("td,hd->th", grad_rows, down_full, preferred_element_type=jnp.float32)
    expanded_grad = (gated_grad * upper).astype(jnp.bfloat16)
    upper_grad = gated_grad * expanded
    expand_grad = jnp.einsum(
        "ct,th->ch", token_states, expanded_grad, preferred_element_type=jnp.float32
    )
    state_grad = jnp.einsum(
        "th,ch->ct", expanded_grad, expand_full, preferred_element_type=jnp.float32
    ).astype(jnp.bfloat16)
    channel_grad = lax.all_to_all(state_grad, "tok", split_axis=0, concat_axis=1, tiled=True)
    value_grad_channels, param_grad = mix_backward(
        channel_values, channel_grad.reshape(blocked), pieces, powers, lams, coefs, starts, taps
    )
    states = param_grad.shape[1] // 2
    param_grad = jnp.stack([param_grad[:, :states], param_grad[:, states:]])
    param_sum = lax.psum(param_grad, "rep")
    value_grad = lax.all_to_all(
        value_grad_channels.reshape(channels, length),
        "tok",
        split_axis=1,
        concat_axis=0,
        tiled=True,
    )
    value_pre_grad = value_back(value_grad.astype(jnp.float32))[0].astype(jnp.bfloat16)
    up_pre_grad = upper_back(upper_grad)[0].astype(jnp.bfloat16)
    up_grad = jnp.einsum("td,th->dh", normed_low, up_pre_grad, preferred_element_type=jnp.float32)
    value_w_grad = jnp.einsum(
        "td,ct->dc", normed_low, value_pre_grad, preferred_element_type=jnp.float32
    )
    normed_grad = jnp.einsum("th,dh->td", up_pre_grad, up_full, preferred_element_type=jnp.float32)
    normed_grad = normed_grad + jnp.einsum(
        "ct,dc->td", value_pre_grad, value_full, preferred_element_type=jnp.float32
    )
    row_grad, norm_grad = norm_back(normed_grad)
    token_grad = (row_grad + grad_rows.astype(jnp.float32))[None]
    expand_sum, down_sum = (
        lax.psum_scatter(expand_grad, ("tok", "rep"), scatter_dimension=0, tiled=True),
        lax.psum_scatter(down_grad, ("tok", "rep"), scatter_dimension=0, tiled=True),
    )
    up_sum, value_sum, norm_sum = (
        lax.psum_scatter(up_grad, ("tok", "rep"), scatter_dimension=0, tiled=True),
        lax.psum_scatter(value_w_grad, ("tok", "rep"), scatter_dimension=0, tiled=True),
        lax.psum_scatter(norm_grad, ("tok", "rep"), scatter_dimension=1, tiled=True),
    )
    step_value = jnp.float32(STEP)
    up_next, up_mean_next, up_square_next = adam_step(
        up_weight, up_sum, up_mean, up_square, step_value, 0.08, 0.1
    )
    value_next, value_mean_next, value_square_next = adam_step(
        value_weight, value_sum, value_mean, value_square, step_value, 0.08, 0.1
    )
    expand_next, expand_mean_next, expand_square_next = adam_step(
        expand_weight, expand_sum, expand_mean, expand_square, step_value, 0.08, 0.1
    )
    down_next, down_mean_next, down_square_next = adam_step(
        down_weight, down_sum, down_mean, down_square, step_value, 0.08, 0.1
    )
    norm_next, norm_mean_next, norm_square_next = adam_step(
        norm_params, norm_sum, norm_mean, norm_square, step_value, 1.0, 0.0
    )
    state_next, state_mean_next, state_square_next = adam_step(
        state_params, param_sum, state_mean, state_square, step_value, 0.006, 0.0
    )
    return (
        layer_out,
        token_grad,
        up_next,
        up_mean_next,
        up_square_next,
        value_next,
        value_mean_next,
        value_square_next,
        expand_next,
        expand_mean_next,
        expand_square_next,
        down_next,
        down_mean_next,
        down_square_next,
        norm_next,
        norm_mean_next,
        norm_square_next,
        state_next,
        state_mean_next,
        state_square_next,
    )


def solution(mesh):
    placed = (
        P("rep", "tok", None),
        P("rep", "tok", None),
        P("rep", None),
        P(("tok", "rep"), None),
        P(("tok", "rep"), None),
        P(("tok", "rep"), None),
        P(("tok", "rep"), None),
        P(None, ("tok", "rep")),
        P(None, "tok", None),
        P(None, "tok", None),
        P(("tok", "rep"), None),
        P(("tok", "rep"), None),
        P(("tok", "rep"), None),
        P(("tok", "rep"), None),
        P(("tok", "rep"), None),
        P(("tok", "rep"), None),
        P(("tok", "rep"), None),
        P(("tok", "rep"), None),
        P(None, ("tok", "rep")),
        P(None, ("tok", "rep")),
        P(None, "tok", None),
        P(None, "tok", None),
    )
    return jax.shard_map(
        per_device,
        mesh=mesh,
        in_specs=placed,
        out_specs=(
            P("rep", "tok", None),
            P("rep", "tok", None),
            P(("tok", "rep"), None),
            P(("tok", "rep"), None),
            P(("tok", "rep"), None),
            P(("tok", "rep"), None),
            P(("tok", "rep"), None),
            P(("tok", "rep"), None),
            P(("tok", "rep"), None),
            P(("tok", "rep"), None),
            P(("tok", "rep"), None),
            P(("tok", "rep"), None),
            P(("tok", "rep"), None),
            P(("tok", "rep"), None),
            P(None, ("tok", "rep")),
            P(None, ("tok", "rep")),
            P(None, ("tok", "rep")),
            P(None, "tok", None),
            P(None, "tok", None),
            P(None, "tok", None),
        ),
        check_vma=False,
    )
```

```python
import functools

import jax
import jax.numpy as jnp
from jax import lax
from jax.experimental import pallas as pl
from jax.experimental.pallas import tpu as pltpu
from jax.sharding import PartitionSpec as P

BLOCK = 128
STEP = 5


epsilon_norm = 1e-05
epsilon_adam = 1e-08
beta_first = 0.9
beta_second = 0.999


def gelu_curve(values):
    return jax.nn.gelu(values, approximate=True)


def pieces_of(lengths_row, length):
    blocks = length // BLOCK
    items = lengths_row.shape[0]
    ends = jnp.cumsum(lengths_row, dtype=jnp.int32)
    heads = BLOCK * jnp.arange(blocks, dtype=jnp.int32)
    head_rank = jnp.arange(blocks, dtype=jnp.int32) + jnp.sum(
        (ends[None, :] < heads[:, None]).astype(jnp.int32), axis=1
    )
    end_rank = jnp.arange(items, dtype=jnp.int32) + jnp.sum(
        (heads[None, :] <= ends[:, None]).astype(jnp.int32), axis=1
    )
    places = jnp.arange(blocks + items, dtype=jnp.int32)[:, None]
    starts = jnp.sum(jnp.where(head_rank[None, :] == places, heads[None, :], 0), axis=1) + jnp.sum(
        jnp.where(end_rank[None, :] == places, ends[None, :], 0), axis=1
    )
    stops = jnp.concatenate([starts[1:], jnp.full((1,), length, jnp.int32)])
    owner = starts // BLOCK
    segment = jnp.sum((ends[None, :] <= starts[:, None]).astype(jnp.int32), axis=1)
    positions = owner[:, None] * BLOCK + jnp.arange(BLOCK, dtype=jnp.int32)[None, :]
    mask = (positions >= starts[:, None]) & (positions < stops[:, None])
    pick = owner[:, None] == jnp.arange(blocks, dtype=jnp.int32)[None, :]
    follows = (segment[1:] == segment[:-1]) & (owner[1:] != owner[:-1])
    follows = jnp.concatenate([jnp.zeros((1,), bool), follows])
    return (
        pick.astype(jnp.bfloat16),
        mask.astype(jnp.bfloat16),
        follows.astype(jnp.float32),
    )


def powers_of(poles):
    decay_rate = jnp.exp(poles[0])[:, None, :]
    frequency = poles[1][:, None, :]
    lags = jnp.array([0, 1, 2, 3, 4, 5, 6, 7, 8, 16, 32, 64, 128, 128, 128, 128], jnp.float32)
    lags = lags[None, :, None]
    magnitude = jnp.exp(-decay_rate * lags)
    phase = frequency * lags
    return jnp.concatenate([magnitude * jnp.cos(phase), magnitude * jnp.sin(phase)], axis=2)


def cmul(ar, ai, br, bi):
    return ar * br - ai * bi, ar * bi + ai * br


def fill_tables(c, states, low_ref, up_ref, down_ref):
    for lane in range(0, states, 128):
        re_lanes = pl.ds(lane, 128)
        im_lanes = pl.ds(states + lane, 128)
        base = low_ref[c, 0:8, re_lanes], low_ref[c, 0:8, im_lanes]
        for ref, forward in ((up_ref, True), (down_ref, False)):
            if forward:
                re, im = base
            else:
                re = jnp.concatenate([base[0][7 - k : 8 - k] for k in range(8)], axis=0)
                im = jnp.concatenate([base[1][7 - k : 8 - k] for k in range(8)], axis=0)
            for k in range(4):
                nr, ni = cmul(
                    re,
                    im,
                    low_ref[c, 8 + k : 9 + k, re_lanes],
                    low_ref[c, 8 + k : 9 + k, im_lanes],
                )
                if forward:
                    re = jnp.concatenate([re, nr], axis=0)
                    im = jnp.concatenate([im, ni], axis=0)
                else:
                    re = jnp.concatenate([nr, re], axis=0)
                    im = jnp.concatenate([ni, im], axis=0)
            for lanes, entries in ((re_lanes, re), (im_lanes, im)):
                high, rest = split_rows(entries)
                ref[c, 0, :, lanes] = high
                if ref.shape[1] > 1:
                    ref[c, 1, :, lanes] = rest


def nt(a, b):
    return lax.dot_general(a, b, (((1,), (1,)), ((), ())), preferred_element_type=jnp.float32)


def nn(a, b):
    return lax.dot_general(a, b, (((1,), (0,)), ((), ())), preferred_element_type=jnp.float32)


def tn(a, b):
    return lax.dot_general(a, b, (((0,), (0,)), ((), ())), preferred_element_type=jnp.float32)


def split_rows(row):
    high = row.astype(jnp.bfloat16)
    rest = (row - high.astype(jnp.float32)).astype(jnp.bfloat16)
    return high, rest


def toeplitz(kernel_row):
    spread = jnp.broadcast_to(kernel_row, (BLOCK, BLOCK))
    rolled = pltpu.roll(spread, 0, 1, stride=1, stride_axis=0)
    rows = lax.broadcasted_iota(jnp.int32, (BLOCK, BLOCK), 0)
    columns = lax.broadcasted_iota(jnp.int32, (BLOCK, BLOCK), 1)
    return jnp.where(columns >= rows, rolled, 0.0)


def put_rows(ref, c, places, group, block):
    for k in range(ref.shape[0]):
        ref[k, pl.ds(c, places, stride=group), :] = block[:, 128 * k : 128 * (k + 1)]


def get_rows(ref, c, places, group):
    chunks = [ref[k, pl.ds(c, places, stride=group), :] for k in range(ref.shape[0])]
    return jnp.concatenate(chunks, axis=1)


def get_step(ref, rows, half):
    count = ref.shape[0] // 2
    return jnp.concatenate([ref[half * count + k, rows, :] for k in range(count)], axis=1)


def put_step(ref, rows, half, block):
    count = ref.shape[0] // 2
    for k in range(count):
        ref[half * count + k, rows, :] = block[:, 128 * k : 128 * (k + 1)]


def forward_kernel(
    active, follows_ref, pick_ref, mask_ref, values_ref, low_ref, lam_ref, coef_ref,
    out_ref, start_ref, taps_ref, token_ref, up_ref, down_ref, work_ref,
):
    token_ref[...] = jnp.zeros_like(token_ref)
    places = pick_ref.shape[0]
    group, states = coef_ref.shape[0], coef_ref.shape[1] // 2
    if active < group:
        work_ref[...] = jnp.zeros_like(work_ref)
    mask = mask_ref[...]
    pick = pick_ref[...]
    for c in range(active):
        fill_tables(c, states, low_ref, up_ref, down_ref)
        spread = nn(pick, values_ref[c]).astype(jnp.bfloat16) * mask
        put_rows(work_ref, c, places, group, nn(spread, down_ref[c, 0]) + nn(spread, down_ref[c, 1]))
    lam_re, lam_im = lam_ref[0, :, :states], lam_ref[0, :, states:]
    far_re, far_im = lam_ref[1, :, :states], lam_ref[1, :, states:]
    coef_re, coef_im = coef_ref[:, :states], coef_ref[:, states:]
    mix_re, mix_im = cmul(coef_re, coef_im, lam_re, lam_im)

    def advance(p, carry):
        re, im = carry
        rows = pl.ds(pl.multiple_of(p * group, group), group)
        keep = follows_ref[p]
        re, im = re * keep, im * keep
        start_ref[rows, :states] = re
        start_ref[rows, states:] = im
        far = cmul(re, im, far_re, far_im)
        new_re = far[0] + get_step(work_ref, rows, 0)
        new_im = far[1] + get_step(work_ref, rows, 1)
        mixed = cmul(re, im, mix_re, mix_im)
        put_step(work_ref, rows, 0, mixed[0])
        put_step(work_ref, rows, 1, -mixed[1])
        return new_re, new_im

    zero = jnp.zeros((group, states), jnp.float32)
    lax.fori_loop(0, places, advance, (zero, zero), unroll=4)
    for c in range(active):
        row = jnp.concatenate([coef_ref[c : c + 1, :states], -coef_ref[c : c + 1, states:]], axis=1)
        high, rest = split_rows(row)
        rows = jnp.concatenate([high, rest, jnp.zeros((14, 2 * states), jnp.bfloat16)], axis=0)
        mixed = split_rows(get_rows(work_ref, c, places, group))
        stack = jnp.concatenate([mixed[0], rows, mixed[1]], axis=0)
        carried = nt(stack, up_ref[c, 0])
        finer = nt(stack[: places + 16], up_ref[c, 1])
        carried = jnp.concatenate(
            [carried[:places] + carried[places + 16 :], carried[places : places + 16]], axis=0
        ) + finer
        kernel_row = carried[places : places + 1] + carried[places + 1 : places + 2]
        taps = split_rows(toeplitz(kernel_row))
        taps_ref[c] = taps[0]
        spread = nn(pick, values_ref[c]).astype(jnp.bfloat16) * mask
        result = (carried[:places] + nn(spread, taps[0]) + nn(spread, taps[1])).astype(jnp.bfloat16) * mask
        out_ref[c] = tn(pick, result).astype(jnp.bfloat16)


def backward_kernel(
    active, follows_ref, pick_ref, mask_ref, values_ref, grads_ref, low_ref, lam_ref, coef_ref,
    start_ref, taps_ref, out_ref, sum_ref, token_ref, up_ref, down_ref, work_ref,
):
    token_ref[...] = jnp.zeros_like(token_ref)
    places = pick_ref.shape[0]
    group, states = coef_ref.shape[0], coef_ref.shape[1] // 2
    if active < group:
        work_ref[...] = jnp.zeros_like(work_ref)
        sum_ref[...] = jnp.zeros_like(sum_ref)
    mask = mask_ref[...]
    pick = pick_ref[...]
    rows = lax.broadcasted_iota(jnp.int32, (BLOCK, BLOCK), 0)
    columns = lax.broadcasted_iota(jnp.int32, (BLOCK, BLOCK), 1)
    turn = (rows + columns == BLOCK - 1).astype(jnp.bfloat16)
    for c in range(active):
        fill_tables(c, states, low_ref, up_ref, down_ref)
        values = nn(pick, values_ref[c]).astype(jnp.bfloat16) * mask
        grads = nn(pick, grads_ref[c]).astype(jnp.bfloat16) * mask
        pairs = tn(nn(values, turn).astype(jnp.bfloat16), grads)
        skewed = pltpu.roll(pairs, 1, 1, stride=1, stride_axis=0)
        lag_sum = jnp.sum(jnp.where(columns <= rows, skewed, 0.0), axis=0, keepdims=True)
        high, rest = split_rows(lag_sum)
        extra = jnp.concatenate([high, rest, jnp.zeros((14, BLOCK), jnp.bfloat16)], axis=0)
        folded = nn(jnp.concatenate([grads, extra], axis=0), up_ref[c, 0])
        put_rows(work_ref, c, places, group, folded[:places])
        sum_ref[c : c + 1, :] = folded[places : places + 1] + folded[places + 1 : places + 2]
    lam_re, lam_im = lam_ref[0, :, :states], lam_ref[0, :, states:]
    far_re, far_im = lam_ref[1, :, :states], lam_ref[1, :, states:]
    coef_re, coef_im = coef_ref[:, :states], coef_ref[:, states:]

    def retreat(step, carry):
        re, im, total_re, total_im = carry
        p = places - 1 - step
        rows = pl.ds(pl.multiple_of(p * group, group), group)
        near = cmul(get_step(work_ref, rows, 0), get_step(work_ref, rows, 1), lam_re, lam_im)
        begin = start_ref[rows, :states], start_ref[rows, states:]
        product = cmul(begin[0], begin[1], near[0], near[1])
        mixed = cmul(re, im, coef_re, coef_im)
        put_step(work_ref, rows, 0, mixed[0])
        put_step(work_ref, rows, 1, -mixed[1])
        keep = follows_ref[p]
        far = cmul(re, im, far_re, far_im)
        return (
            (near[0] + far[0]) * keep,
            (near[1] + far[1]) * keep,
            total_re + product[0],
            total_im + product[1],
        )

    zero = jnp.zeros((group, states), jnp.float32)
    _, _, total_re, total_im = lax.fori_loop(0, places, retreat, (zero, zero, zero, zero), unroll=4)
    sum_ref[:, :states] = sum_ref[:, :states] + total_re
    sum_ref[:, states:] = -(sum_ref[:, states:] + total_im)
    for c in range(active):
        mixed = get_rows(work_ref, c, places, group).astype(jnp.bfloat16)
        grads = nn(pick, grads_ref[c]).astype(jnp.bfloat16) * mask
        result = nt(mixed, down_ref[c, 0]) + nt(grads, taps_ref[c])
        out_ref[c] = tn(pick, result.astype(jnp.bfloat16) * mask).astype(jnp.bfloat16)


def whole(shape):
    return pl.BlockSpec(shape, lambda i: (0,) * len(shape))


def part(shape, place, dim=0):
    index = tuple(place if k == dim else 0 for k in range(len(shape)))
    return pl.BlockSpec(shape, lambda i: index)


class Parts:
    def __init__(self, kernel, name, inputs, results, scratch, parts, flops):
        self.kernel, self.name, self.inputs, self.results = kernel, name, inputs, results
        self.scratch, self.parts, self.flops = scratch, parts, flops
        self.done, self.outs, self.waits = 0, [], []

    def run(self, *waits):
        self.waits += waits
        if self.done < self.parts - 1:
            return self.call()
        return None

    def last(self, *waits):
        self.waits += waits
        return self.call()

    def call(self):
        k = self.done
        operands = [array for array, _ in self.inputs]
        specs = [spec(k) for _, spec in self.inputs]
        count, waits, before = len(operands), self.waits, list(self.outs)

        def body(*refs):
            self.kernel(*refs[:count], *refs[count + len(waits) + len(before) :])

        token = jax.ShapeDtypeStruct((8, 128), jnp.float32)
        *self.outs, token = pl.pallas_call(
            body,
            grid=(1,),
            in_specs=specs + [pl.BlockSpec(memory_space=pl.ANY)] * (len(waits) + len(before)),
            out_specs=[spec(k) for _, spec in self.results] + [whole((8, 128))],
            out_shape=[shape for shape, _ in self.results] + [token],
            input_output_aliases={count + len(waits) + n: n for n in range(len(before))},
            scratch_shapes=self.scratch,
            compiler_params=pltpu.CompilerParams(vmem_limit_bytes=48 * 2**20),
            cost_estimate=pl.CostEstimate(
                flops=self.flops, bytes_accessed=4 * 2**20, transcendentals=0
            ),
            name=self.name,
        )(*operands, *waits, *before)
        self.done, self.waits = k + 1, []
        return token


def scratches(active, group, places, states, tables):
    return [
        pltpu.VMEM((active, tables, BLOCK, 2 * states), jnp.bfloat16),
        pltpu.VMEM((active, tables, BLOCK, 2 * states), jnp.bfloat16),
        pltpu.VMEM((2 * states // 128, places * group, 128), jnp.float32),
    ]


def padded(values, lams, coefs):
    channels = values.shape[0]
    group, active = 8, min(8, channels)
    spare = max(0, group - channels)
    lams = jnp.pad(lams, ((0, 0), (0, spare), (0, 0)))
    coefs = jnp.pad(coefs, ((0, spare), (0, 0)))
    return group, active, spare, lams, coefs


def mix_forward(values, pieces, powers, lams, coefs):
    channels, blocks = values.shape[0], values.shape[1]
    pick, mask, follows = pieces
    places, states = pick.shape[0], coefs.shape[1] // 2
    group, active, spare, lams, coefs = padded(values, lams, coefs)
    full = lambda shape: lambda k: whole(shape)
    inputs = [
        (follows, lambda k: pl.BlockSpec(memory_space=pltpu.SMEM)),
        (pick, full((places, blocks))),
        (mask, full((places, BLOCK))),
        (values, lambda k: part((active, blocks, BLOCK), k)),
        (powers, lambda k: part((active, 16, 2 * states), k)),
        (lams, lambda k: part((2, group, 2 * states), k, 1)),
        (coefs, lambda k: part((group, 2 * states), k)),
    ]
    f32 = jnp.float32
    results = [
        (
            jax.ShapeDtypeStruct((channels, blocks, BLOCK), jnp.bfloat16),
            lambda k: part((active, blocks, BLOCK), k),
        ),
        (
            jax.ShapeDtypeStruct((places * (channels + spare), 2 * states), f32),
            lambda k: part((places * group, 2 * states), k),
        ),
        (
            jax.ShapeDtypeStruct((channels, BLOCK, BLOCK), jnp.bfloat16),
            lambda k: part((active, BLOCK, BLOCK), k),
        ),
    ]
    return Parts(
        functools.partial(forward_kernel, active),
        "mix_forward",
        inputs,
        results,
        scratches(active, group, places, states, 2),
        channels // active,
        8 * 10**9,
    )


def mix_backward(values, grads, pieces, powers, lams, coefs, starts, taps):
    channels, blocks = values.shape[0], values.shape[1]
    pick, mask, follows = pieces
    places, states = pick.shape[0], coefs.shape[1] // 2
    group, active, spare, lams, coefs = padded(values, lams, coefs)
    full = lambda shape: lambda k: whole(shape)
    inputs = [
        (follows, lambda k: pl.BlockSpec(memory_space=pltpu.SMEM)),
        (pick, full((places, blocks))),
        (mask, full((places, BLOCK))),
        (values, lambda k: part((active, blocks, BLOCK), k)),
        (grads, lambda k: part((active, blocks, BLOCK), k)),
        (powers, lambda k: part((active, 16, 2 * states), k)),
        (lams, lambda k: part((2, group, 2 * states), k, 1)),
        (coefs, lambda k: part((group, 2 * states), k)),
        (starts, lambda k: part((places * group, 2 * states), k)),
        (taps, lambda k: part((active, BLOCK, BLOCK), k)),
    ]
    results = [
        (
            jax.ShapeDtypeStruct((channels, blocks, BLOCK), jnp.bfloat16),
            lambda k: part((active, blocks, BLOCK), k),
        ),
        (
            jax.ShapeDtypeStruct((channels + spare, 2 * states), jnp.float32),
            lambda k: part((group, 2 * states), k),
        ),
    ]
    return Parts(
        functools.partial(backward_kernel, active),
        "mix_backward",
        inputs,
        results,
        scratches(active, group, places, states, 1),
        channels // active,
        107 * 10**8,
    )


def mixer_inputs(poles, params):
    table = powers_of(poles)
    lams = jnp.stack([table[:, 1], table[:, 12]])
    coefs = jnp.concatenate([params[0], params[1]], axis=1)
    return table, lams, coefs


def adam_step(weight, gradient, first_moment, second, step_value, step_rate, decay_rate):
    first_new = beta_first * first_moment + (1.0 - beta_first) * gradient
    second_new = beta_second * second + (1.0 - beta_second) * gradient * gradient
    first_hat = first_new / (1.0 - jnp.power(beta_first, step_value))
    second_hat = second_new / (1.0 - jnp.power(beta_second, step_value))
    weight_new = weight - step_rate * (
        first_hat / (jnp.sqrt(second_hat) + epsilon_adam) + decay_rate * weight
    )
    return (weight_new, first_new, second_new)


class Cube:
    def __init__(self, tok_size):
        self.size = 2 * tok_size
        bits = tok_size.bit_length() - 1
        across = bits // 3
        self.xs = [1 + k for k in range(across)]
        self.ys = [1 + across + k for k in range(across)]
        self.zs = [1 + k for k in range(2 * across, bits)]
        self.place = lax.axis_index("tok") * 2 + lax.axis_index("rep")

    def bit(self, b):
        return lax.rem(lax.div(self.place, 1 << b), 2)

    def swap(self, block, b):
        pairs = [(i, i ^ (1 << b)) for i in range(self.size)]
        return lax.ppermute(block, ("tok", "rep"), pairs)

    def halves(self, block, have, b):
        above = 1 << sum(1 for k in have if k > b)
        split = block.reshape((above, 2, -1) + block.shape[1:])
        index = self.bit(b)
        mine = lax.dynamic_index_in_dim(split, index, 1, keepdims=False)
        other = lax.dynamic_index_in_dim(split, 1 - index, 1, keepdims=False)
        shape = (-1,) + block.shape[1:]
        return mine.reshape(shape), other.reshape(shape)

    def split(self, block):
        stack = block.reshape((self.size, -1) + block.shape[1:])
        return self.halves(stack, range(self.size.bit_length() - 1), 0)

    def merge(self, mine, other):
        swapped = self.bit(0) == 1
        first, second = jnp.where(swapped, other, mine), jnp.where(swapped, mine, other)
        pair = jnp.stack([first, second], axis=1)
        return pair.reshape((-1,) + pair.shape[3:])


class Gather:
    def __init__(self, cube, shard, order):
        self.cube, self.order, self.have = cube, list(order), []
        self.block = shard[None]

    def send(self, *waits):
        self.arriving = self.cube.swap(after(self.block, *waits), self.order[0])

    def take(self, *waits):
        b = self.order.pop(0)
        other = after(self.arriving, *waits)
        above = 1 << sum(1 for k in self.have if k > b)
        shape = (above, 1, -1) + self.block.shape[1:]
        mine, other = self.block.reshape(shape), other.reshape(shape)
        joined = jnp.where(
            self.cube.bit(b) == 1,
            jnp.concatenate([other, mine], axis=1),
            jnp.concatenate([mine, other], axis=1),
        )
        self.have.append(b)
        self.block = joined.reshape((1 << len(self.have),) + self.block.shape[1:])

    def rest(self, *waits):
        if self.order:
            self.take(*waits)
        while self.order:
            self.send()
            self.take()

    def both(self):
        return self.block, self.cube.swap(self.block, 0)


class Scatter:
    def __init__(self, cube, keep, send, order, have, wide=()):
        self.cube, self.order, self.have = cube, list(order), list(have)
        self.keep, self.sent, self.wide = keep, send, wide
        self.going = False

    def send(self, *waits):
        self.arriving = self.cube.swap(after(self.sent, *waits), self.order[0])
        self.going = True

    def take(self, *waits):
        b, self.going = self.order.pop(0), False
        self.have.remove(b)
        total = self.keep + after(self.arriving, *waits).astype(jnp.float32)
        if not self.order:
            self.keep, self.sent = total, total
            return
        self.keep, sent = self.cube.halves(total, self.have, self.order[0])
        self.sent = sent if self.order[0] in self.wide else sent.astype(jnp.bfloat16)

    def rest(self):
        while self.order:
            if not self.going:
                self.send()
            self.take()
        return self.keep[0]


def after(block, *waits):
    return lax.optimization_barrier((block, *waits))[0] if waits else block


def products(cube, lefts, rights, first, have):
    sides = [cube.halves(left, have, first) for left in lefts]

    def product(side):
        parts = []
        for pair, right in zip(sides, rights):
            left = pair[side]
            parts.append(dot(left.reshape((-1, left.shape[2])), right, 1, 1))
        shape = (-1, lefts[0].shape[1], rights[0].shape[0])
        return (parts[0] + parts[1]).reshape(shape)

    send = product(1).astype(jnp.bfloat16)
    return product(0), send


def dot(a, b, a_dim, b_dim):
    return lax.dot_general(
        a, b, (((a_dim,), (b_dim,)), ((), ())), preferred_element_type=jnp.float32
    )


def per_device(
    tok_size,
    tokens,
    cotangent,
    lengths,
    up_weight,
    value_weight,
    expand_weight,
    down_weight,
    norm_params,
    state_params,
    state_poles,
    up_mean,
    up_square,
    value_mean,
    value_square,
    expand_mean,
    expand_square,
    down_mean,
    down_square,
    norm_mean,
    norm_square,
    state_mean,
    state_square,
):
    low = jnp.bfloat16
    cube = Cube(tok_size)
    xs, ys, zs = cube.xs, cube.ys, cube.zs
    down_zs, tok_bits = zs[::-1], xs + ys + zs
    nz, nx = len(zs), len(xs)

    def flat(block):
        return block.reshape((-1,) + block.shape[2:])

    def dots(lefts, rights, left_dim, right_dim):
        return dot(flat(lefts[0]), flat(rights[0]), left_dim, right_dim) + dot(
            flat(lefts[1]), flat(rights[1]), left_dim, right_dim
        )

    inner = value_weight.shape[1]
    norm_columns = jnp.pad(norm_params.T, ((0, 0), (0, 126)))
    packed = jnp.concatenate([value_weight, norm_columns], axis=1).astype(low)
    pack = Gather(cube, packed, xs + ys + down_zs)
    up = Gather(cube, up_weight.astype(low), down_zs + xs + ys)
    down = Gather(cube, down_weight.astype(low), down_zs + ys + xs)
    expand = Gather(cube, expand_weight.astype(low), xs + ys + down_zs)

    grad_rows = cotangent[0]
    token_rows = tokens[0].astype(jnp.float32)
    width = token_rows.shape[1]
    average = jnp.mean(token_rows, axis=1)
    centered = token_rows - average[:, None]
    scale = lax.rsqrt(jnp.mean(centered * centered, axis=1) + epsilon_norm)
    hats = [
        (part.astype(jnp.float32) - average) * scale for part in cube.split(tokens[0].T)
    ]

    up.send()
    down.send()
    expand.send()
    for _ in range(2 * nx):
        pack.send()
        pack.take()
    up.take()
    down.take()
    for _ in range(nz):
        pack.send(up.block, down.block)
        pack.take()
    up.send(pack.block)
    down.send(pack.block)
    expand.take(pack.block)
    if expand.order:
        expand.send()
    packs = pack.both()
    values = [pack[:, :, :inner] for pack in packs]
    gains = [pack[:, :, inner : inner + 1].astype(jnp.float32) for pack in packs]
    shifts = [pack[:, :, inner + 1 : inner + 2].astype(jnp.float32) for pack in packs]
    normed = [(h * g + b).astype(low) for h, g, b in zip(hats, gains, shifts)]
    value_preactivation = dots(values, normed, 0, 0)
    value_act, value_back = jax.vjp(gelu_curve, value_preactivation)
    value_low = value_act.astype(low)
    channel_values = lax.all_to_all(value_low, "tok", split_axis=0, concat_axis=1, tiled=True)

    for _ in range(nz - 2):
        up.take(value_low)
        down.take(value_low)
        up.send()
        down.send()
    for _ in range(2 * nx - 2):
        expand.take(value_low)
        expand.send()
    poles, coefs = lax.optimization_barrier((state_poles, state_params, value_low))[:2]
    channels, length = channel_values.shape
    blocked = (channels, length // BLOCK, BLOCK)
    pieces = pieces_of(lengths[0], length)
    powers, lams, coefs = mixer_inputs(poles, coefs)
    channel_values = channel_values.reshape(blocked)
    grad_columns = grad_rows.T
    normed_swapped = cube.swap(normed[1], 0)
    columns_swapped = cube.swap(grad_columns, 0)
    mixer = mix_forward(channel_values, pieces, powers, lams, coefs)

    def run(*waits):
        token = mixer.run(*waits)
        return [] if token is None else [token]

    up.take(channel_values)
    down.take(channel_values)
    expand.take(channel_values)
    up.send()
    down.send()
    expand.send()
    token = run(up.block, down.block, expand.block)
    for _ in range(nx):
        up.take(*token)
        down.take(*token)
        up.send()
        down.send()
    token = run(up.block, down.block)
    expand.take(*token)
    if expand.order:
        expand.send()
    token = run(*token, expand.block, normed_swapped, columns_swapped)
    mixer.last()
    state_out, starts, taps = mixer.outs
    token_states = lax.all_to_all(
        state_out.reshape(channels, length), "tok", split_axis=1, concat_axis=0, tiled=True
    )
    state_sides = cube.split(token_states)
    expand.rest(token_states)
    up.rest(token_states)
    down.rest(token_states)
    ups, downs, expands = up.both(), down.both(), expand.both()

    upper, upper_back = jax.vjp(gelu_curve, dots(ups, normed, 0, 0))
    gated_grad = cube.merge(
        *[dot(flat(down), grad_rows, 1, 1).reshape(down.shape[:2] + (-1,)) for down in downs]
    )
    expanded = dots(expands, state_sides, 0, 0)
    expanded_grad = (gated_grad * upper).astype(low)
    state_grad = cube.merge(
        *[
            dot(flat(expand), expanded_grad, 1, 0).astype(low).reshape(expand.shape[:2] + (-1,))
            for expand in expands
        ]
    )
    channel_grad = lax.all_to_all(state_grad, "tok", split_axis=0, concat_axis=1, tiled=True)
    gated = (upper * expanded).astype(low)
    gated_sides = cube.split(gated)
    up_pre_grad = upper_back(gated_grad * expanded)[0].astype(low)

    def both(block):
        return block, cube.swap(block, 0)

    def scatter(lefts, rights, order):
        keep, send = products(cube, lefts, rights, order[0], tok_bits)
        sums = Scatter(cube, keep, send, order, tok_bits)
        sums.send()
        return sums

    down_sums = scatter(
        (gated_sides[0], cube.swap(gated_sides[1], 0)),
        (grad_columns, columns_swapped),
        xs + ys + zs,
    )
    up_sums = scatter((normed[0], normed_swapped), both(up_pre_grad), ys + xs + zs)
    expand_sums = scatter(
        (state_sides[0], cube.swap(state_sides[1], 0)), both(expanded_grad), zs + ys + xs
    )
    layer_out = (token_rows + dots(gated_sides, downs, 0, 0)).astype(low)[None]

    mixer = mix_backward(
        channel_values, channel_grad.reshape(blocked), pieces, powers, lams, coefs, starts, taps
    )
    token = run(up_sums.sent, down_sums.sent, expand_sums.sent)
    token = run()
    expand_sums.take(*token)
    expand_sums.send()
    token = run(expand_sums.sent)
    for _ in range(nx):
        up_sums.take(*token)
        down_sums.take(*token)
        up_sums.send()
        down_sums.send()
    expand_sums.take(*token)
    expand_sums.send()
    mixer.last(up_sums.sent, down_sums.sent, expand_sums.sent)
    value_grad_channels, param_grad = mixer.outs
    states = param_grad.shape[1] // 2
    param_grad = jnp.stack([param_grad[:channels, :states], param_grad[:channels, states:]])
    param_sum = param_grad + cube.swap(param_grad, 0)
    for sums in (up_sums, down_sums, expand_sums):
        sums.arriving = after(sums.arriving, value_grad_channels)
    value_grad_channels = after(value_grad_channels, up_sums.arriving, down_sums.arriving)
    value_grad = lax.all_to_all(
        value_grad_channels.reshape(channels, length),
        "tok",
        split_axis=1,
        concat_axis=0,
        tiled=True,
    )
    value_pre_grad = value_back(value_grad.astype(jnp.float32))[0].astype(low)
    ups_grads = [dot(flat(up), up_pre_grad, 1, 0) for up in ups]
    normed_grads = [
        (g + dot(flat(value), value_pre_grad, 1, 0)).reshape(h.shape)
        for g, value, h in zip(ups_grads, values, hats)
    ]
    packed_grads = []
    for side, h, g in zip(normed, hats, normed_grads):
        weight_grad = dot(flat(side), value_pre_grad, 1, 1).reshape(side.shape[:2] + (-1,))
        norm_grad = jnp.stack([jnp.sum(g * h, axis=2), jnp.sum(g, axis=2)], axis=2)
        norm_grad = jnp.pad(norm_grad, ((0, 0), (0, 0), (0, 126)))
        packed_grads.append(jnp.concatenate([weight_grad, norm_grad], axis=2))
    packed_sums = Scatter(
        cube, packed_grads[0], packed_grads[1].astype(low), [0] + tok_bits, [0] + tok_bits, ys + zs
    )
    for sums in (up_sums, down_sums):
        sums.take()
        sums.send()
    expand_sums.take(value_pre_grad)
    if expand_sums.order:
        expand_sums.send()
    packed_sums.send()
    packed_sums.take(up_sums.arriving, down_sums.arriving)
    for sums in (up_sums, down_sums, expand_sums):
        if sums.order:
            sums.take(value_pre_grad)
        if sums.order:
            sums.send()
    packed_sums.send()
    packed_sums.take()
    packed_sums.send(up_sums.arriving, down_sums.arriving)
    packed_sum = packed_sums.rest()
    up_sum, down_sum, expand_sum = [
        sums.rest() for sums in (up_sums, down_sums, expand_sums)
    ]
    value_sum = packed_sum[:, :inner]
    norm_sum = packed_sum[:, inner : inner + 2].T
    hat_grads = [g * gain for g, gain in zip(normed_grads, gains)]
    hat_mean = sum(jnp.sum(d, axis=(0, 1)) for d in hat_grads) / width
    hat_product = sum(jnp.sum(d * h, axis=(0, 1)) for d, h in zip(hat_grads, hats)) / width
    row_grads = [(d - hat_mean - h * hat_product) * scale for d, h in zip(hat_grads, hats)]
    token_grad = (cube.merge(*row_grads).T + grad_rows.astype(jnp.float32))[None]
    step_value = jnp.float32(STEP)
    up_next, up_mean_next, up_square_next = adam_step(
        up_weight, up_sum, up_mean, up_square, step_value, 0.08, 0.1
    )
    value_next, value_mean_next, value_square_next = adam_step(
        value_weight, value_sum, value_mean, value_square, step_value, 0.08, 0.1
    )
    expand_next, expand_mean_next, expand_square_next = adam_step(
        expand_weight, expand_sum, expand_mean, expand_square, step_value, 0.08, 0.1
    )
    down_next, down_mean_next, down_square_next = adam_step(
        down_weight, down_sum, down_mean, down_square, step_value, 0.08, 0.1
    )
    norm_next, norm_mean_next, norm_square_next = adam_step(
        norm_params, norm_sum, norm_mean, norm_square, step_value, 1.0, 0.0
    )
    state_next, state_mean_next, state_square_next = adam_step(
        state_params, param_sum, state_mean, state_square, step_value, 0.006, 0.0
    )
    return (
        layer_out,
        token_grad,
        up_next,
        up_mean_next,
        up_square_next,
        value_next,
        value_mean_next,
        value_square_next,
        expand_next,
        expand_mean_next,
        expand_square_next,
        down_next,
        down_mean_next,
        down_square_next,
        norm_next,
        norm_mean_next,
        norm_square_next,
        state_next,
        state_mean_next,
        state_square_next,
    )


def solution(mesh):
    placed = (
        P("rep", "tok", None),
        P("rep", "tok", None),
        P("rep", None),
        P(("tok", "rep"), None),
        P(("tok", "rep"), None),
        P(("tok", "rep"), None),
        P(("tok", "rep"), None),
        P(None, ("tok", "rep")),
        P(None, "tok", None),
        P(None, "tok", None),
        P(("tok", "rep"), None),
        P(("tok", "rep"), None),
        P(("tok", "rep"), None),
        P(("tok", "rep"), None),
        P(("tok", "rep"), None),
        P(("tok", "rep"), None),
        P(("tok", "rep"), None),
        P(("tok", "rep"), None),
        P(None, ("tok", "rep")),
        P(None, ("tok", "rep")),
        P(None, "tok", None),
        P(None, "tok", None),
    )
    return jax.shard_map(
        functools.partial(per_device, mesh.shape["tok"]),
        mesh=mesh,
        in_specs=placed,
        out_specs=(
            P("rep", "tok", None),
            P("rep", "tok", None),
            P(("tok", "rep"), None),
            P(("tok", "rep"), None),
            P(("tok", "rep"), None),
            P(("tok", "rep"), None),
            P(("tok", "rep"), None),
            P(("tok", "rep"), None),
            P(("tok", "rep"), None),
            P(("tok", "rep"), None),
            P(("tok", "rep"), None),
            P(("tok", "rep"), None),
            P(("tok", "rep"), None),
            P(("tok", "rep"), None),
            P(None, ("tok", "rep")),
            P(None, ("tok", "rep")),
            P(None, ("tok", "rep")),
            P(None, "tok", None),
            P(None, "tok", None),
            P(None, "tok", None),
        ),
        check_vma=False,
    )
```

```python
import functools

import jax
import jax.numpy as jnp
from jax import lax
from jax.experimental import pallas as pl
from jax.experimental.pallas import tpu as pltpu
from jax.sharding import PartitionSpec as P

BLOCK = 128
STEP = 5


epsilon_norm = 1e-05
epsilon_adam = 1e-08
beta_first = 0.9
beta_second = 0.999


def gelu_curve(values):
    return jax.nn.gelu(values, approximate=True)


def pieces_of(lengths_row, length):
    blocks = length // BLOCK
    items = lengths_row.shape[0]
    ends = jnp.cumsum(lengths_row, dtype=jnp.int32)
    heads = BLOCK * jnp.arange(blocks, dtype=jnp.int32)
    head_rank = jnp.arange(blocks, dtype=jnp.int32) + jnp.sum(
        (ends[None, :] < heads[:, None]).astype(jnp.int32), axis=1
    )
    end_rank = jnp.arange(items, dtype=jnp.int32) + jnp.sum(
        (heads[None, :] <= ends[:, None]).astype(jnp.int32), axis=1
    )
    places = jnp.arange(blocks + items, dtype=jnp.int32)[:, None]
    starts = jnp.sum(jnp.where(head_rank[None, :] == places, heads[None, :], 0), axis=1) + jnp.sum(
        jnp.where(end_rank[None, :] == places, ends[None, :], 0), axis=1
    )
    stops = jnp.concatenate([starts[1:], jnp.full((1,), length, jnp.int32)])
    owner = starts // BLOCK
    segment = jnp.sum((ends[None, :] <= starts[:, None]).astype(jnp.int32), axis=1)
    positions = owner[:, None] * BLOCK + jnp.arange(BLOCK, dtype=jnp.int32)[None, :]
    mask = (positions >= starts[:, None]) & (positions < stops[:, None])
    pick = owner[:, None] == jnp.arange(blocks, dtype=jnp.int32)[None, :]
    follows = (segment[1:] == segment[:-1]) & (owner[1:] != owner[:-1])
    follows = jnp.concatenate([jnp.zeros((1,), bool), follows])
    return (
        pick.astype(jnp.bfloat16),
        mask.astype(jnp.bfloat16),
        follows.astype(jnp.float32),
    )


def powers_of(poles):
    decay_rate = jnp.exp(poles[0])[:, None, :]
    frequency = poles[1][:, None, :]
    lags = jnp.array([0, 1, 2, 3, 4, 5, 6, 7, 8, 16, 32, 64, 128, 128, 128, 128], jnp.float32)
    lags = lags[None, :, None]
    magnitude = jnp.exp(-decay_rate * lags)
    phase = frequency * lags
    return jnp.concatenate([magnitude * jnp.cos(phase), magnitude * jnp.sin(phase)], axis=2)


def cmul(ar, ai, br, bi):
    return ar * br - ai * bi, ar * bi + ai * br


def fill_tables(c, states, low_ref, up_ref, down_ref):
    for lane in range(0, states, 128):
        re_lanes = pl.ds(lane, 128)
        im_lanes = pl.ds(states + lane, 128)
        base = low_ref[c, 0:8, re_lanes], low_ref[c, 0:8, im_lanes]
        for ref, forward in ((up_ref, True), (down_ref, False)):
            if forward:
                re, im = base
            else:
                re = jnp.concatenate([base[0][7 - k : 8 - k] for k in range(8)], axis=0)
                im = jnp.concatenate([base[1][7 - k : 8 - k] for k in range(8)], axis=0)
            for k in range(4):
                nr, ni = cmul(
                    re,
                    im,
                    low_ref[c, 8 + k : 9 + k, re_lanes],
                    low_ref[c, 8 + k : 9 + k, im_lanes],
                )
                if forward:
                    re = jnp.concatenate([re, nr], axis=0)
                    im = jnp.concatenate([im, ni], axis=0)
                else:
                    re = jnp.concatenate([nr, re], axis=0)
                    im = jnp.concatenate([ni, im], axis=0)
            for lanes, entries in ((re_lanes, re), (im_lanes, im)):
                high, rest = split_rows(entries)
                ref[c, 0, :, lanes] = high
                if ref.shape[1] > 1:
                    ref[c, 1, :, lanes] = rest


def nt(a, b):
    return lax.dot_general(a, b, (((1,), (1,)), ((), ())), preferred_element_type=jnp.float32)


def nn(a, b):
    return lax.dot_general(a, b, (((1,), (0,)), ((), ())), preferred_element_type=jnp.float32)


def tn(a, b):
    return lax.dot_general(a, b, (((0,), (0,)), ((), ())), preferred_element_type=jnp.float32)


def split_rows(row):
    high = row.astype(jnp.bfloat16)
    rest = (row - high.astype(jnp.float32)).astype(jnp.bfloat16)
    return high, rest


def toeplitz(kernel_row):
    spread = jnp.broadcast_to(kernel_row, (BLOCK, BLOCK))
    rolled = pltpu.roll(spread, 0, 1, stride=1, stride_axis=0)
    rows = lax.broadcasted_iota(jnp.int32, (BLOCK, BLOCK), 0)
    columns = lax.broadcasted_iota(jnp.int32, (BLOCK, BLOCK), 1)
    return jnp.where(columns >= rows, rolled, 0.0)


def put_rows(ref, c, places, group, block):
    for k in range(ref.shape[0]):
        ref[k, pl.ds(c, places, stride=group), :] = block[:, 128 * k : 128 * (k + 1)]


def get_rows(ref, c, places, group):
    chunks = [ref[k, pl.ds(c, places, stride=group), :] for k in range(ref.shape[0])]
    return jnp.concatenate(chunks, axis=1)


def get_step(ref, rows, half):
    count = ref.shape[0] // 2
    return jnp.concatenate([ref[half * count + k, rows, :] for k in range(count)], axis=1)


def put_step(ref, rows, half, block):
    count = ref.shape[0] // 2
    for k in range(count):
        ref[half * count + k, rows, :] = block[:, 128 * k : 128 * (k + 1)]


def forward_kernel(
    active, follows_ref, pick_ref, mask_ref, values_ref, low_ref, lam_ref, coef_ref,
    out_ref, start_ref, taps_ref, token_ref, up_ref, down_ref, work_ref,
):
    token_ref[...] = jnp.zeros_like(token_ref)
    places = pick_ref.shape[0]
    group, states = coef_ref.shape[0], coef_ref.shape[1] // 2
    if active < group:
        work_ref[...] = jnp.zeros_like(work_ref)
    mask = mask_ref[...]
    pick = pick_ref[...]
    for c in range(active):
        fill_tables(c, states, low_ref, up_ref, down_ref)
        spread = nn(pick, values_ref[c]).astype(jnp.bfloat16) * mask
        put_rows(work_ref, c, places, group, nn(spread, down_ref[c, 0]) + nn(spread, down_ref[c, 1]))
    lam_re, lam_im = lam_ref[0, :, :states], lam_ref[0, :, states:]
    far_re, far_im = lam_ref[1, :, :states], lam_ref[1, :, states:]
    coef_re, coef_im = coef_ref[:, :states], coef_ref[:, states:]
    mix_re, mix_im = cmul(coef_re, coef_im, lam_re, lam_im)

    def advance(p, carry):
        re, im = carry
        rows = pl.ds(pl.multiple_of(p * group, group), group)
        keep = follows_ref[p]
        re, im = re * keep, im * keep
        start_ref[rows, :states] = re
        start_ref[rows, states:] = im
        far = cmul(re, im, far_re, far_im)
        new_re = far[0] + get_step(work_ref, rows, 0)
        new_im = far[1] + get_step(work_ref, rows, 1)
        mixed = cmul(re, im, mix_re, mix_im)
        put_step(work_ref, rows, 0, mixed[0])
        put_step(work_ref, rows, 1, -mixed[1])
        return new_re, new_im

    zero = jnp.zeros((group, states), jnp.float32)
    lax.fori_loop(0, places, advance, (zero, zero), unroll=4)
    for c in range(active):
        row = jnp.concatenate([coef_ref[c : c + 1, :states], -coef_ref[c : c + 1, states:]], axis=1)
        high, rest = split_rows(row)
        rows = jnp.concatenate([high, rest, jnp.zeros((14, 2 * states), jnp.bfloat16)], axis=0)
        mixed = split_rows(get_rows(work_ref, c, places, group))
        stack = jnp.concatenate([mixed[0], rows, mixed[1]], axis=0)
        carried = nt(stack, up_ref[c, 0])
        finer = nt(stack[: places + 16], up_ref[c, 1])
        carried = jnp.concatenate(
            [carried[:places] + carried[places + 16 :], carried[places : places + 16]], axis=0
        ) + finer
        kernel_row = carried[places : places + 1] + carried[places + 1 : places + 2]
        taps = split_rows(toeplitz(kernel_row))
        taps_ref[c] = taps[0]
        spread = nn(pick, values_ref[c]).astype(jnp.bfloat16) * mask
        result = (carried[:places] + nn(spread, taps[0]) + nn(spread, taps[1])).astype(jnp.bfloat16) * mask
        out_ref[c] = tn(pick, result).astype(jnp.bfloat16)


def backward_kernel(
    active, follows_ref, pick_ref, mask_ref, values_ref, grads_ref, low_ref, lam_ref, coef_ref,
    start_ref, taps_ref, out_ref, sum_ref, token_ref, up_ref, down_ref, work_ref,
):
    token_ref[...] = jnp.zeros_like(token_ref)
    places = pick_ref.shape[0]
    group, states = coef_ref.shape[0], coef_ref.shape[1] // 2
    if active < group:
        work_ref[...] = jnp.zeros_like(work_ref)
        sum_ref[...] = jnp.zeros_like(sum_ref)
    mask = mask_ref[...]
    pick = pick_ref[...]
    rows = lax.broadcasted_iota(jnp.int32, (BLOCK, BLOCK), 0)
    columns = lax.broadcasted_iota(jnp.int32, (BLOCK, BLOCK), 1)
    turn = (rows + columns == BLOCK - 1).astype(jnp.bfloat16)
    for c in range(active):
        fill_tables(c, states, low_ref, up_ref, down_ref)
        values = nn(pick, values_ref[c]).astype(jnp.bfloat16) * mask
        grads = nn(pick, grads_ref[c]).astype(jnp.bfloat16) * mask
        pairs = tn(nn(values, turn).astype(jnp.bfloat16), grads)
        skewed = pltpu.roll(pairs, 1, 1, stride=1, stride_axis=0)
        lag_sum = jnp.sum(jnp.where(columns <= rows, skewed, 0.0), axis=0, keepdims=True)
        high, rest = split_rows(lag_sum)
        extra = jnp.concatenate([high, rest, jnp.zeros((14, BLOCK), jnp.bfloat16)], axis=0)
        folded = nn(jnp.concatenate([grads, extra], axis=0), up_ref[c, 0])
        put_rows(work_ref, c, places, group, folded[:places])
        sum_ref[c : c + 1, :] = folded[places : places + 1] + folded[places + 1 : places + 2]
    lam_re, lam_im = lam_ref[0, :, :states], lam_ref[0, :, states:]
    far_re, far_im = lam_ref[1, :, :states], lam_ref[1, :, states:]
    coef_re, coef_im = coef_ref[:, :states], coef_ref[:, states:]

    def retreat(step, carry):
        re, im, total_re, total_im = carry
        p = places - 1 - step
        rows = pl.ds(pl.multiple_of(p * group, group), group)
        near = cmul(get_step(work_ref, rows, 0), get_step(work_ref, rows, 1), lam_re, lam_im)
        begin = start_ref[rows, :states], start_ref[rows, states:]
        product = cmul(begin[0], begin[1], near[0], near[1])
        mixed = cmul(re, im, coef_re, coef_im)
        put_step(work_ref, rows, 0, mixed[0])
        put_step(work_ref, rows, 1, -mixed[1])
        keep = follows_ref[p]
        far = cmul(re, im, far_re, far_im)
        return (
            (near[0] + far[0]) * keep,
            (near[1] + far[1]) * keep,
            total_re + product[0],
            total_im + product[1],
        )

    zero = jnp.zeros((group, states), jnp.float32)
    _, _, total_re, total_im = lax.fori_loop(0, places, retreat, (zero, zero, zero, zero), unroll=4)
    sum_ref[:, :states] = sum_ref[:, :states] + total_re
    sum_ref[:, states:] = -(sum_ref[:, states:] + total_im)
    for c in range(active):
        mixed = get_rows(work_ref, c, places, group).astype(jnp.bfloat16)
        grads = nn(pick, grads_ref[c]).astype(jnp.bfloat16) * mask
        result = nt(mixed, down_ref[c, 0]) + nt(grads, taps_ref[c])
        out_ref[c] = tn(pick, result.astype(jnp.bfloat16) * mask).astype(jnp.bfloat16)


def whole(shape):
    return pl.BlockSpec(shape, lambda i: (0,) * len(shape))


def part(shape, place, dim=0):
    index = tuple(place if k == dim else 0 for k in range(len(shape)))
    return pl.BlockSpec(shape, lambda i: index)


class Parts:
    def __init__(self, kernel, name, inputs, results, scratch, parts, flops):
        self.kernel, self.name, self.inputs, self.results = kernel, name, inputs, results
        self.scratch, self.parts, self.flops = scratch, parts, flops
        self.done, self.outs, self.waits = 0, [], []

    def run(self, *waits):
        self.waits += waits
        if self.done < self.parts - 1:
            return self.call()
        return None

    def last(self, *waits):
        self.waits += waits
        return self.call()

    def call(self):
        k = self.done
        operands = [array for array, _ in self.inputs]
        specs = [spec(k) for _, spec in self.inputs]
        count, waits, before = len(operands), self.waits, list(self.outs)

        def body(*refs):
            self.kernel(*refs[:count], *refs[count + len(waits) + len(before) :])

        token = jax.ShapeDtypeStruct((8, 128), jnp.float32)
        *self.outs, token = pl.pallas_call(
            body,
            grid=(1,),
            in_specs=specs + [pl.BlockSpec(memory_space=pl.ANY)] * (len(waits) + len(before)),
            out_specs=[spec(k) for _, spec in self.results] + [whole((8, 128))],
            out_shape=[shape for shape, _ in self.results] + [token],
            input_output_aliases={count + len(waits) + n: n for n in range(len(before))},
            scratch_shapes=self.scratch,
            compiler_params=pltpu.CompilerParams(vmem_limit_bytes=48 * 2**20),
            cost_estimate=pl.CostEstimate(
                flops=self.flops, bytes_accessed=4 * 2**20, transcendentals=0
            ),
            name=self.name,
        )(*operands, *waits, *before)
        self.done, self.waits = k + 1, []
        return token


def scratches(active, group, places, states, tables):
    return [
        pltpu.VMEM((active, tables, BLOCK, 2 * states), jnp.bfloat16),
        pltpu.VMEM((active, tables, BLOCK, 2 * states), jnp.bfloat16),
        pltpu.VMEM((2 * states // 128, places * group, 128), jnp.float32),
    ]


def padded(values, lams, coefs):
    channels = values.shape[0]
    group, active = 8, min(8, channels)
    spare = max(0, group - channels)
    lams = jnp.pad(lams, ((0, 0), (0, spare), (0, 0)))
    coefs = jnp.pad(coefs, ((0, spare), (0, 0)))
    return group, active, spare, lams, coefs


def mix_forward(values, pieces, powers, lams, coefs):
    channels, blocks = values.shape[0], values.shape[1]
    pick, mask, follows = pieces
    places, states = pick.shape[0], coefs.shape[1] // 2
    group, active, spare, lams, coefs = padded(values, lams, coefs)
    full = lambda shape: lambda k: whole(shape)
    inputs = [
        (follows, lambda k: pl.BlockSpec(memory_space=pltpu.SMEM)),
        (pick, full((places, blocks))),
        (mask, full((places, BLOCK))),
        (values, lambda k: part((active, blocks, BLOCK), k)),
        (powers, lambda k: part((active, 16, 2 * states), k)),
        (lams, lambda k: part((2, group, 2 * states), k, 1)),
        (coefs, lambda k: part((group, 2 * states), k)),
    ]
    f32 = jnp.float32
    results = [
        (
            jax.ShapeDtypeStruct((channels, blocks, BLOCK), jnp.bfloat16),
            lambda k: part((active, blocks, BLOCK), k),
        ),
        (
            jax.ShapeDtypeStruct((places * (channels + spare), 2 * states), f32),
            lambda k: part((places * group, 2 * states), k),
        ),
        (
            jax.ShapeDtypeStruct((channels, BLOCK, BLOCK), jnp.bfloat16),
            lambda k: part((active, BLOCK, BLOCK), k),
        ),
    ]
    return Parts(
        functools.partial(forward_kernel, active),
        "mix_forward",
        inputs,
        results,
        scratches(active, group, places, states, 2),
        channels // active,
        8 * 10**9,
    )


def mix_backward(values, grads, pieces, powers, lams, coefs, starts, taps):
    channels, blocks = values.shape[0], values.shape[1]
    pick, mask, follows = pieces
    places, states = pick.shape[0], coefs.shape[1] // 2
    group, active, spare, lams, coefs = padded(values, lams, coefs)
    full = lambda shape: lambda k: whole(shape)
    inputs = [
        (follows, lambda k: pl.BlockSpec(memory_space=pltpu.SMEM)),
        (pick, full((places, blocks))),
        (mask, full((places, BLOCK))),
        (values, lambda k: part((active, blocks, BLOCK), k)),
        (grads, lambda k: part((active, blocks, BLOCK), k)),
        (powers, lambda k: part((active, 16, 2 * states), k)),
        (lams, lambda k: part((2, group, 2 * states), k, 1)),
        (coefs, lambda k: part((group, 2 * states), k)),
        (starts, lambda k: part((places * group, 2 * states), k)),
        (taps, lambda k: part((active, BLOCK, BLOCK), k)),
    ]
    results = [
        (
            jax.ShapeDtypeStruct((channels, blocks, BLOCK), jnp.bfloat16),
            lambda k: part((active, blocks, BLOCK), k),
        ),
        (
            jax.ShapeDtypeStruct((channels + spare, 2 * states), jnp.float32),
            lambda k: part((group, 2 * states), k),
        ),
    ]
    return Parts(
        functools.partial(backward_kernel, active),
        "mix_backward",
        inputs,
        results,
        scratches(active, group, places, states, 1),
        channels // active,
        107 * 10**8,
    )


def mixer_inputs(poles, params):
    table = powers_of(poles)
    lams = jnp.stack([table[:, 1], table[:, 12]])
    coefs = jnp.concatenate([params[0], params[1]], axis=1)
    return table, lams, coefs


def adam_step(weight, gradient, first_moment, second, step_value, step_rate, decay_rate):
    first_new = beta_first * first_moment + (1.0 - beta_first) * gradient
    second_new = beta_second * second + (1.0 - beta_second) * gradient * gradient
    first_hat = first_new / (1.0 - jnp.power(beta_first, step_value))
    second_hat = second_new / (1.0 - jnp.power(beta_second, step_value))
    weight_new = weight - step_rate * (
        first_hat / (jnp.sqrt(second_hat) + epsilon_adam) + decay_rate * weight
    )
    return (weight_new, first_new, second_new)


class Cube:
    def __init__(self, tok_size):
        self.size = 2 * tok_size
        bits = tok_size.bit_length() - 1
        across = bits // 3
        self.xs = [1 + k for k in range(across)]
        self.ys = [1 + across + k for k in range(across)]
        self.zs = [1 + k for k in range(2 * across, bits)]
        self.place = lax.axis_index("tok") * 2 + lax.axis_index("rep")

    def bit(self, b):
        return lax.rem(lax.div(self.place, 1 << b), 2)

    def swap(self, block, b):
        return self.trade(block, 1 << b)

    def trade(self, block, mask):
        pairs = [(i, i ^ mask) for i in range(self.size)]
        return lax.ppermute(block, ("tok", "rep"), pairs)

    def halves(self, block, have, b):
        above = 1 << sum(1 for k in have if k > b)
        split = block.reshape((above, 2, -1) + block.shape[1:])
        index = self.bit(b)
        mine = lax.dynamic_index_in_dim(split, index, 1, keepdims=False)
        other = lax.dynamic_index_in_dim(split, 1 - index, 1, keepdims=False)
        shape = (-1,) + block.shape[1:]
        return mine.reshape(shape), other.reshape(shape)

    def split(self, block):
        stack = block.reshape((self.size, -1) + block.shape[1:])
        return self.halves(stack, range(self.size.bit_length() - 1), 0)

    def merge(self, mine, other):
        swapped = self.bit(0) == 1
        first, second = jnp.where(swapped, other, mine), jnp.where(swapped, mine, other)
        pair = jnp.stack([first, second], axis=1)
        return pair.reshape((-1,) + pair.shape[3:])


class Gather:
    def __init__(self, cube, shard, order):
        self.cube, self.order, self.have = cube, list(order), []
        self.block, self.going = shard[None], False

    def send(self, *waits):
        if self.order and not self.going:
            self.arriving = self.cube.swap(after(self.block, *waits), self.order[0])
            self.going = True

    def join(self, mine, other, b):
        above = 1 << sum(1 for k in self.have if k > b)
        shape = (above, 1, -1) + mine.shape[1:]
        first, second = mine.reshape(shape), other.reshape(shape)
        joined = jnp.where(
            self.cube.bit(b) == 1,
            jnp.concatenate([second, first], axis=1),
            jnp.concatenate([first, second], axis=1),
        )
        return joined.reshape((2 * mine.shape[0],) + mine.shape[1:])

    def take(self, *waits):
        self.send()
        if self.order:
            b, self.going = self.order.pop(0), False
            self.block = self.join(self.block, after(self.arriving, *waits), b)
            self.have.append(b)

    def direct(self, bits):
        masks = [sum(1 << b for k, b in enumerate(bits) if n >> k & 1) for n in range(1 << len(bits))]
        blocks = {m: self.cube.trade(self.block, m) if m else self.block for m in masks}
        for b in bits:
            blocks = {
                m: self.join(blocks[m], blocks[m | 1 << b], b) for m in blocks if not m >> b & 1
            }
            self.have.append(b)
        self.block = blocks[0]

    def rest(self):
        while self.order:
            self.take()

    def both(self):
        return self.block, self.cube.swap(self.block, 0)


class Scatter:
    def __init__(self, cube, keep, send, order, have, wide=()):
        self.cube, self.order, self.have = cube, list(order), list(have)
        self.keep, self.sent, self.wide = keep, send, wide
        self.going = False

    def send(self, *waits):
        if self.order and not self.going:
            self.arriving = self.cube.swap(after(self.sent, *waits), self.order[0])
            self.going = True

    def take(self, *waits):
        self.send()
        if not self.order:
            return
        b, self.going = self.order.pop(0), False
        self.have.remove(b)
        total = self.keep + after(self.arriving, *waits).astype(jnp.float32)
        if not self.order:
            self.keep, self.sent = total, total
            return
        self.keep, sent = self.cube.halves(total, self.have, self.order[0])
        self.sent = sent if self.order[0] in self.wide else sent.astype(jnp.bfloat16)

    def rest(self):
        while self.order:
            self.take()
        return self.keep[0]


def direct_sum(cube, total, have, bits, kind):
    have, parts = list(have), {0: total}
    for b in bits:
        halves = {m: cube.halves(part, have, b) for m, part in parts.items()}
        have.remove(b)
        parts = {m | k << b: halves[m][k] for m in halves for k in range(2)}
    keep = parts.pop(0)
    return keep + sum(cube.trade(p.astype(kind), m).astype(jnp.float32) for m, p in parts.items())


def after(block, *waits):
    return lax.optimization_barrier((block, *waits))[0] if waits else block


def gelu_parts(a):
    root = 0.7978845608028654
    square = a * a
    t = jnp.tanh(root * a * (1.0 + 0.044715 * square))
    half = 0.5 * (1.0 + t)
    slope = half + 0.5 * a * (1.0 - t * t) * root * (1.0 + 3.0 * 0.044715 * square)
    return a * half, slope


def gate_kernel(
    split, core_ref, normed_ref, state_refs, grad_ref, up_refs, expand_refs, down_refs,
    grad_out, up_out, gated_refs, state_outs, state_scratch, sum_scratch,
):
    step, last = pl.program_id(0), pl.num_programs(0) - 1
    channels = state_refs[0].shape[0]
    swapped = core_ref[0] == 1

    @pl.when(step == 0)
    def _():
        for k in range(2):
            turned = state_refs[k][...].astype(jnp.float32).T
            state_scratch[:, channels * k : channels * (k + 1)] = turned.astype(jnp.bfloat16)
        sum_scratch[...] = jnp.zeros_like(sum_scratch)

    def pair(mine, other):
        return jnp.where(swapped, other, mine), jnp.where(swapped, mine, other)

    rows = normed_ref.shape[1] // 2
    up_pre = nn(normed_ref[:, :rows], up_refs[0][...]) + nn(normed_ref[:, rows:], up_refs[1][...])
    if split:
        down = []
        for s in range(down_refs[0].shape[0]):
            down += pair(down_refs[0][s], down_refs[1][s])
        down = jnp.concatenate(down, axis=0)
    else:
        down = down_refs[0][...]
    gated_grad = nt(grad_ref[...], down)
    expanded = nn(state_scratch[:, :channels], expand_refs[0][...]) + nn(
        state_scratch[:, channels:], expand_refs[1][...]
    )
    upper, slope = gelu_parts(up_pre)
    expanded_grad = (gated_grad * upper).astype(jnp.bfloat16)
    grad_out[...] = expanded_grad
    up_out[...] = (gated_grad * expanded * slope).astype(jnp.bfloat16)
    gated = (upper * expanded).T.astype(jnp.bfloat16)
    if split:
        size = gated_refs[0].shape[1]
        for s in range(gated_refs[0].shape[0]):
            first = gated[2 * s * size : (2 * s + 1) * size]
            second = gated[(2 * s + 1) * size : (2 * s + 2) * size]
            mine, other = pair(first, second)
            gated_refs[0][s] = mine
            gated_refs[1][s] = other
    else:
        gated_refs[0][...] = gated
    for k in range(2):
        sum_scratch[:, channels * k : channels * (k + 1)] += nt(expanded_grad, expand_refs[k][...])

    @pl.when(step == last)
    def _():
        for k in range(2):
            total = sum_scratch[:, channels * k : channels * (k + 1)].T
            state_outs[k][...] = total.astype(jnp.bfloat16)


def gate(cube, normed, states, grad_rows, ups, expands, downs):
    tokens, width = grad_rows.shape
    hidden = ups[0].shape[1]
    split = downs[0].shape[1] % 16 == 0
    block = 2 * downs[0].shape[1] * max(1, 192 // downs[0].shape[1]) if split else 384
    low, f32 = jnp.bfloat16, jnp.float32
    full = lambda array: pl.BlockSpec(array.shape, lambda i: (0,) * array.ndim)
    if split:
        shards = block // (2 * downs[0].shape[1])
        down_spec = pl.BlockSpec((shards,) + downs[0].shape[1:], lambda i: (i, 0, 0))
        gated_shape = jax.ShapeDtypeStruct(downs[0].shape[:2] + (tokens,), low)
        gated_spec = pl.BlockSpec((shards, downs[0].shape[1], tokens), lambda i: (i, 0, 0))
        count = 2
    else:
        downs = [cube.merge(*downs)]
        down_spec = pl.BlockSpec((block, width), lambda i: (i, 0))
        gated_shape = jax.ShapeDtypeStruct((hidden, tokens), low)
        gated_spec = pl.BlockSpec((block, tokens), lambda i: (i, 0))
        count = 1
    columns = lambda array: pl.BlockSpec((array.shape[0], block), lambda i: (0, i))
    channels = states[0].shape[0]
    row_spec = pl.BlockSpec((tokens, block), lambda i: (0, i))
    state_shape = jax.ShapeDtypeStruct((channels, tokens), low)

    def body(core, normed, s0, s1, grad, u0, u1, e0, e1, *refs):
        down_refs, refs = refs[:count], refs[count:]
        grad_out, up_out, gated_refs, refs = refs[0], refs[1], refs[2 : 2 + count], refs[2 + count :]
        gate_kernel(
            split, core, normed, (s0, s1), grad, (u0, u1), (e0, e1), down_refs,
            grad_out, up_out, gated_refs, refs[:2], refs[2], refs[3],
        )

    outs = pl.pallas_call(
        body,
        grid=(hidden // block,),
        in_specs=[pl.BlockSpec(memory_space=pltpu.SMEM), full(normed)]
        + [full(s) for s in states]
        + [full(grad_rows)]
        + [columns(u) for u in ups]
        + [columns(e) for e in expands]
        + [down_spec] * count,
        out_specs=[row_spec, row_spec] + [gated_spec] * count + [full(state_shape)] * 2,
        out_shape=[jax.ShapeDtypeStruct((tokens, hidden), low)] * 2
        + [gated_shape] * count
        + [state_shape] * 2,
        scratch_shapes=[
            pltpu.VMEM((tokens, 2 * channels), low),
            pltpu.VMEM((tokens, 2 * channels), f32),
        ],
        compiler_params=pltpu.CompilerParams(vmem_limit_bytes=48 * 2**20),
        cost_estimate=pl.CostEstimate(
            flops=10**6, bytes_accessed=2**10, transcendentals=0
        ),
        name="gate",
    )(cube.bit(0).reshape(1), normed, *states, grad_rows, *ups, *expands, *downs)
    grad_out, up_out = outs[:2]
    gated = outs[2 : 2 + count]
    gated = gated if split else cube.split(gated[0])
    return grad_out, up_out, gated, outs[2 + count :]


def value_kernel(
    width, grad_ref, pre_ref, value_refs, normed_refs, hat_refs, part_refs, keep_ref, send_ref, out_refs
):
    slope = gelu_parts(pre_ref[...])[1]
    grad = (grad_ref[...].astype(jnp.float32) * slope).astype(jnp.bfloat16)
    for k, ref in ((1, send_ref), (0, keep_ref)):
        total = part_refs[k][...] + nn(value_refs[k][:, :width], grad)
        out_refs[k][...] = total
        ref[:, :width] = nt(normed_refs[k][...], grad).astype(ref.dtype)
        lane = lax.broadcasted_iota(jnp.int32, (total.shape[0], 128), 1)
        gain = jnp.sum(total * hat_refs[k][...], axis=1, keepdims=True)
        shift = jnp.sum(total, axis=1, keepdims=True)
        columns = jnp.where(lane == 0, gain, jnp.where(lane == 1, shift, 0.0))
        ref[:, width:] = columns.astype(ref.dtype)


def value_grads(width, value_grad, value_pre, packs, normed, hats, parts):
    rows, tokens = normed[0].shape
    columns = packs[0].shape[1]

    def body(grad, pre, p0, p1, n0, n1, h0, h1, a0, a1, keep, send, g0, g1):
        value_kernel(
            width, grad, pre, (p0, p1), (n0, n1), (h0, h1), (a0, a1), keep, send, (g0, g1)
        )

    operands = (value_grad, value_pre, *packs, *normed, *hats, *parts)
    results = [((rows, columns), jnp.float32), ((rows, columns), jnp.bfloat16)]
    results += [((rows, tokens), jnp.float32)] * 2
    keep, send, first, second = pl.pallas_call(
        body,
        grid=(1,),
        in_specs=[whole(a.shape) for a in operands],
        out_specs=[whole(shape) for shape, _ in results],
        out_shape=[jax.ShapeDtypeStruct(shape, kind) for shape, kind in results],
        compiler_params=pltpu.CompilerParams(vmem_limit_bytes=48 * 2**20),
        cost_estimate=pl.CostEstimate(flops=10**6, bytes_accessed=2**10, transcendentals=0),
        name="value_grads",
    )(*operands)
    return keep, send, (first, second)


def products_kernel(bit_ref, own_send, own_keep, got_send, got_keep, own, got, send_ref, keep_ref):
    def product(a, b):
        flat = lambda ref: ref[...].reshape((-1, ref.shape[3]))
        return nn(flat(a), own[...]) + nn(flat(b), got[...])

    send_ref[...] = product(own_send, got_send).astype(jnp.bfloat16)
    keep_ref[...] = product(own_keep, got_keep)


def products(cube, lefts, rights, first, have):
    shards, rows, tokens = lefts[0].shape
    columns = rights[0].shape[1]
    above = 1 << sum(1 for k in have if k > first)
    shape = (shards // 2, rows, columns)
    if rows % 16:
        sides = [cube.halves(left, have, first) for left in lefts]
        keep, send = [
            sum(
                dot(pair[k].reshape((-1, tokens)), right, 1, 0)
                for pair, right in zip(sides, rights)
            ).reshape(shape)
            for k in range(2)
        ]
        return keep, send.astype(jnp.bfloat16)
    lefts = [left.reshape((above, 2, -1, tokens)) for left in lefts]
    side = (above, 1) + lefts[0].shape[2:]
    send_spec = pl.BlockSpec(side, lambda j, bit: (0, 1 - bit[0], 0, 0))
    keep_spec = pl.BlockSpec(side, lambda j, bit: (0, bit[0], 0, 0))
    block = min(columns, 1024)
    count = shards * rows // 2
    right_spec = pl.BlockSpec((tokens, block), lambda j, bit: (0, j))
    out_spec = pl.BlockSpec((count, block), lambda j, bit: (0, j))
    send, keep = pl.pallas_call(
        products_kernel,
        grid_spec=pltpu.PrefetchScalarGridSpec(
            num_scalar_prefetch=1,
            grid=(columns // block,),
            in_specs=[send_spec, keep_spec] * 2 + [right_spec] * 2,
            out_specs=[out_spec] * 2,
        ),
        out_shape=[
            jax.ShapeDtypeStruct((count, columns), jnp.bfloat16),
            jax.ShapeDtypeStruct((count, columns), jnp.float32),
        ],
        compiler_params=pltpu.CompilerParams(vmem_limit_bytes=48 * 2**20),
        cost_estimate=pl.CostEstimate(
            flops=10**6, bytes_accessed=2**10, transcendentals=0
        ),
        name="weight_grad",
    )(cube.bit(first).reshape(1), lefts[0], lefts[0], lefts[1], lefts[1], *rights)
    return keep.reshape(shape), send.reshape(shape)


def dot(a, b, a_dim, b_dim):
    return lax.dot_general(
        a, b, (((a_dim,), (b_dim,)), ((), ())), preferred_element_type=jnp.float32
    )


def per_device(
    tok_size,
    tokens,
    cotangent,
    lengths,
    up_weight,
    value_weight,
    expand_weight,
    down_weight,
    norm_params,
    state_params,
    state_poles,
    up_mean,
    up_square,
    value_mean,
    value_square,
    expand_mean,
    expand_square,
    down_mean,
    down_square,
    norm_mean,
    norm_square,
    state_mean,
    state_square,
):
    low = jnp.bfloat16
    cube = Cube(tok_size)
    xs, ys, zs = cube.xs, cube.ys, cube.zs
    down_zs, tok_bits = zs[::-1], xs + ys + zs
    nz, nx = len(zs), len(xs)

    def flat(block):
        return block.reshape((-1,) + block.shape[2:])

    def dots(lefts, rights, left_dim, right_dim):
        return dot(flat(lefts[0]), flat(rights[0]), left_dim, right_dim) + dot(
            flat(lefts[1]), flat(rights[1]), left_dim, right_dim
        )

    inner = value_weight.shape[1]
    norm_columns = jnp.pad(norm_params.T, ((0, 0), (0, 126)))
    packed = jnp.concatenate([value_weight, norm_columns], axis=1).astype(low)
    pack = Gather(cube, packed, xs + ys + down_zs)
    up = Gather(cube, up_weight.astype(low), down_zs + xs + ys)
    down = Gather(cube, down_weight.astype(low), down_zs + ys + xs)
    expand = Gather(cube, expand_weight.astype(low), xs + ys + down_zs)

    grad_rows = cotangent[0]
    token_rows = tokens[0].astype(jnp.float32)
    width = token_rows.shape[1]
    average = jnp.mean(token_rows, axis=1)
    centered = token_rows - average[:, None]
    scale = lax.rsqrt(jnp.mean(centered * centered, axis=1) + epsilon_norm)
    hats = [
        (part.astype(jnp.float32) - average) * scale for part in cube.split(tokens[0].T)
    ]

    expand.send()
    pack.direct(zs)
    up.send(pack.block)
    down.send(pack.block)
    if expand.order[1:]:
        expand.take(pack.block)
        expand.send()
    pack.direct(xs + ys)
    packs = pack.both()
    up.take()
    down.take()
    up.send()
    down.send()
    values = [pack[:, :, :inner] for pack in packs]
    gains = [pack[:, :, inner : inner + 1].astype(jnp.float32) for pack in packs]
    shifts = [pack[:, :, inner + 1 : inner + 2].astype(jnp.float32) for pack in packs]
    normed = [(h * g + b).astype(low) for h, g, b in zip(hats, gains, shifts)]
    value_preactivation = dots(values, normed, 0, 0)
    value_act = gelu_curve(value_preactivation)
    value_low = after(value_act.astype(low), up.block, down.block)
    channel_values = lax.all_to_all(value_low, "tok", split_axis=0, concat_axis=1, tiled=True)

    for _ in range(nz - 2):
        up.take(value_low)
        down.take(value_low)
        up.send()
        down.send()
    for _ in range(2 * nx - 2):
        expand.take(value_low)
        expand.send()
    poles, coefs = lax.optimization_barrier((state_poles, state_params, value_low))[:2]
    channels, length = channel_values.shape
    blocked = (channels, length // BLOCK, BLOCK)
    pieces = pieces_of(lengths[0], length)
    powers, lams, coefs = mixer_inputs(poles, coefs)
    channel_values = channel_values.reshape(blocked)
    normed_rows = jnp.concatenate([flat(side).T for side in normed], axis=1)
    normed_swapped = cube.swap(normed[1], 0)
    columns_swapped = cube.swap(grad_rows, 0)
    mixer = mix_forward(channel_values, pieces, powers, lams, coefs)

    def run(*waits):
        token = mixer.run(*waits)
        return [] if token is None else [token]

    up.take(channel_values)
    down.take(channel_values)
    expand.take(channel_values)
    up.send()
    down.send()
    expand.send()
    token = run(up.block, down.block, expand.block)
    for _ in range(nx):
        up.take(*token)
        down.take(*token)
        up.send()
        down.send()
    expand.take(*token)
    if expand.order:
        expand.send()
    token = run(up.block, down.block, expand.block)
    token = run(*token)
    if expand.order:
        expand.take(*token)
    mixer.last(*token, expand.block, normed_swapped, columns_swapped, normed_rows)
    state_out, starts, taps = mixer.outs
    for part in (up, down):
        part.arriving = after(part.arriving, state_out)
    token_states = lax.all_to_all(
        state_out.reshape(channels, length), "tok", split_axis=1, concat_axis=0, tiled=True
    )
    state_sides = cube.split(token_states)
    expand.rest()
    up.rest()
    down.rest()
    ups, downs, expands = up.both(), down.both(), expand.both()

    expanded_grad, up_pre_grad, gated_sides, state_grads = gate(
        cube,
        normed_rows,
        [flat(side) for side in state_sides],
        grad_rows,
        [flat(side) for side in ups],
        [flat(side) for side in expands],
        downs,
    )
    state_grad = cube.merge(*[g.reshape(state_sides[0].shape) for g in state_grads])
    channel_grad = lax.all_to_all(state_grad, "tok", split_axis=0, concat_axis=1, tiled=True)
    channel_grad = channel_grad.reshape(blocked)
    gated_swapped = cube.swap(gated_sides[1], 0)
    expanded_swapped = cube.swap(expanded_grad, 0)
    up_pre_swapped = cube.swap(after(up_pre_grad, gated_swapped), 0)
    state_swapped = cube.swap(state_sides[1], 0)

    def scatter(lefts, rights, order):
        keep, send = products(cube, lefts, rights, order[0], tok_bits)
        return Scatter(cube, keep, send, order, tok_bits)

    down_sums = scatter(
        (gated_sides[0], gated_swapped),
        (grad_rows, columns_swapped),
        xs + ys + zs,
    )
    up_sums = scatter((normed[0], normed_swapped), (up_pre_grad, up_pre_swapped), ys + xs + zs)
    expand_sums = scatter(
        (state_sides[0], state_swapped), (expanded_grad, expanded_swapped), zs + ys + xs
    )
    down_sums.send()
    up_sums.send()
    expand_sums.send(channel_grad)
    mixer = mix_backward(
        channel_values, channel_grad, pieces, powers, lams, coefs, starts, taps
    )
    token = run(up_sums.sent, down_sums.sent, expand_sums.sent)
    token = run(*token)
    expand_sums.take(*token)
    expand_sums.send()
    token = run(*token, expand_sums.sent)
    for _ in range(nx):
        up_sums.take(*token)
        down_sums.take(*token)
        up_sums.send()
        down_sums.send()
    expand_sums.take(*token)
    expand_sums.send()
    mixer.last(*token, up_sums.sent, down_sums.sent, expand_sums.sent)
    value_grad_channels, param_grad = mixer.outs
    states = param_grad.shape[1] // 2
    param_grad = jnp.stack([param_grad[:channels, :states], param_grad[:channels, states:]])
    param_sum = param_grad + cube.swap(param_grad, 0)
    for sums in (up_sums, down_sums, expand_sums):
        sums.arriving = after(sums.arriving, value_grad_channels)
    value_grad_channels = after(value_grad_channels, up_sums.arriving, down_sums.arriving)
    value_grad = lax.all_to_all(
        value_grad_channels.reshape(channels, length),
        "tok",
        split_axis=1,
        concat_axis=0,
        tiled=True,
    )
    for sums in (up_sums, down_sums):
        sums.take()
        sums.send()
    expand_sums.take(value_grad)
    if expand_sums.order:
        expand_sums.send()
    up_pre_late = after(up_pre_grad, value_grad_channels)
    ups_grads = [dot(flat(part), up_pre_late, 1, 1) for part in ups]
    keep, send, normed_grads = value_grads(
        inner,
        value_grad,
        value_preactivation,
        [flat(part) for part in packs],
        [flat(part) for part in normed],
        [flat(part) for part in hats],
        ups_grads,
    )
    normed_grads = [g.reshape(h.shape) for g, h in zip(normed_grads, hats)]
    keep, send = [part.reshape(hats[0].shape[:2] + (-1,)) for part in (keep, send)]
    packed_sum = keep + cube.swap(send, 0).astype(jnp.float32)
    core_sum = packed_sum
    normed_grads = [after(g, core_sum) for g in normed_grads]
    gated_late = after(gated_sides[0], packed_sum), gated_sides[1]
    layer_out = (token_rows + dots(gated_late, downs, 0, 0)).astype(low)[None]
    packed_sum = direct_sum(cube, packed_sum, tok_bits, xs + ys, low)
    for sums in (up_sums, down_sums, expand_sums):
        if sums.order:
            sums.take(core_sum)
        if sums.order:
            sums.send()
            sums.arriving = after(sums.arriving, packed_sum)
    packed_sum = direct_sum(cube, packed_sum, zs, zs, jnp.float32)[0]
    up_sum, down_sum, expand_sum = [
        sums.rest() for sums in (up_sums, down_sums, expand_sums)
    ]
    value_sum = packed_sum[:, :inner]
    norm_sum = packed_sum[:, inner : inner + 2].T
    hat_grads = [g * gain for g, gain in zip(normed_grads, gains)]
    hat_mean = sum(jnp.sum(d, axis=(0, 1)) for d in hat_grads) / width
    hat_product = sum(jnp.sum(d * h, axis=(0, 1)) for d, h in zip(hat_grads, hats)) / width
    row_grads = [(d - hat_mean - h * hat_product) * scale for d, h in zip(hat_grads, hats)]
    token_grad = (cube.merge(*row_grads).T + grad_rows.astype(jnp.float32))[None]
    step_value = jnp.float32(STEP)
    up_next, up_mean_next, up_square_next = adam_step(
        up_weight, up_sum, up_mean, up_square, step_value, 0.08, 0.1
    )
    value_next, value_mean_next, value_square_next = adam_step(
        value_weight, value_sum, value_mean, value_square, step_value, 0.08, 0.1
    )
    expand_next, expand_mean_next, expand_square_next = adam_step(
        expand_weight, expand_sum, expand_mean, expand_square, step_value, 0.08, 0.1
    )
    down_next, down_mean_next, down_square_next = adam_step(
        down_weight, down_sum, down_mean, down_square, step_value, 0.08, 0.1
    )
    norm_next, norm_mean_next, norm_square_next = adam_step(
        norm_params, norm_sum, norm_mean, norm_square, step_value, 1.0, 0.0
    )
    state_next, state_mean_next, state_square_next = adam_step(
        state_params, param_sum, state_mean, state_square, step_value, 0.006, 0.0
    )
    return (
        layer_out,
        token_grad,
        up_next,
        up_mean_next,
        up_square_next,
        value_next,
        value_mean_next,
        value_square_next,
        expand_next,
        expand_mean_next,
        expand_square_next,
        down_next,
        down_mean_next,
        down_square_next,
        norm_next,
        norm_mean_next,
        norm_square_next,
        state_next,
        state_mean_next,
        state_square_next,
    )


def solution(mesh):
    placed = (
        P("rep", "tok", None),
        P("rep", "tok", None),
        P("rep", None),
        P(("tok", "rep"), None),
        P(("tok", "rep"), None),
        P(("tok", "rep"), None),
        P(("tok", "rep"), None),
        P(None, ("tok", "rep")),
        P(None, "tok", None),
        P(None, "tok", None),
        P(("tok", "rep"), None),
        P(("tok", "rep"), None),
        P(("tok", "rep"), None),
        P(("tok", "rep"), None),
        P(("tok", "rep"), None),
        P(("tok", "rep"), None),
        P(("tok", "rep"), None),
        P(("tok", "rep"), None),
        P(None, ("tok", "rep")),
        P(None, ("tok", "rep")),
        P(None, "tok", None),
        P(None, "tok", None),
    )
    return jax.shard_map(
        functools.partial(per_device, mesh.shape["tok"]),
        mesh=mesh,
        in_specs=placed,
        out_specs=(
            P("rep", "tok", None),
            P("rep", "tok", None),
            P(("tok", "rep"), None),
            P(("tok", "rep"), None),
            P(("tok", "rep"), None),
            P(("tok", "rep"), None),
            P(("tok", "rep"), None),
            P(("tok", "rep"), None),
            P(("tok", "rep"), None),
            P(("tok", "rep"), None),
            P(("tok", "rep"), None),
            P(("tok", "rep"), None),
            P(("tok", "rep"), None),
            P(("tok", "rep"), None),
            P(None, ("tok", "rep")),
            P(None, ("tok", "rep")),
            P(None, ("tok", "rep")),
            P(None, "tok", None),
            P(None, "tok", None),
            P(None, "tok", None),
        ),
        check_vma=False,
    )
```

```python
import functools

import jax
import jax.numpy as jnp
from jax import lax
from jax.experimental import pallas as pl
from jax.experimental.pallas import tpu as pltpu
from jax.sharding import PartitionSpec as P

BLOCK = 128
STEP = 5


epsilon_norm = 1e-05
epsilon_adam = 1e-08
beta_first = 0.9
beta_second = 0.999


def gelu_curve(values):
    return jax.nn.gelu(values, approximate=True)


def pieces_of(lengths_row, length, shares):
    blocks = length // BLOCK
    each = blocks // shares
    items = lengths_row.shape[0]
    ends = jnp.cumsum(lengths_row, dtype=jnp.int32)
    heads = BLOCK * jnp.arange(blocks, dtype=jnp.int32)
    head_rank = jnp.arange(blocks, dtype=jnp.int32) + jnp.sum(
        (ends[None, :] < heads[:, None]).astype(jnp.int32), axis=1
    )
    end_rank = jnp.arange(items, dtype=jnp.int32) + jnp.sum(
        (heads[None, :] <= ends[:, None]).astype(jnp.int32), axis=1
    )
    places = jnp.arange(blocks + items, dtype=jnp.int32)[:, None]
    starts = jnp.sum(jnp.where(head_rank[None, :] == places, heads[None, :], 0), axis=1) + jnp.sum(
        jnp.where(end_rank[None, :] == places, ends[None, :], 0), axis=1
    )
    stops = jnp.concatenate([starts[1:], jnp.full((1,), length, jnp.int32)])
    owner = starts // BLOCK
    segment = jnp.sum((ends[None, :] <= starts[:, None]).astype(jnp.int32), axis=1)
    positions = owner[:, None] * BLOCK + jnp.arange(BLOCK, dtype=jnp.int32)[None, :]
    mask = (positions >= starts[:, None]) & (positions < stops[:, None])
    heads = each * jnp.arange(shares, dtype=jnp.int32)[None, None, :]
    heads = heads + jnp.arange(each, dtype=jnp.int32)[:, None, None]
    pick = owner[None, :, None] == heads
    follows = (segment[1:] == segment[:-1]) & (owner[1:] != owner[:-1])
    follows = jnp.concatenate([jnp.zeros((1,), bool), follows])
    return (
        pick.astype(jnp.bfloat16),
        mask.astype(jnp.bfloat16),
        follows.astype(jnp.float32),
    )


def powers_of(poles):
    decay_rate = jnp.exp(poles[0])[:, None, :]
    frequency = poles[1][:, None, :]
    lags = jnp.array([0, 1, 2, 3, 4, 5, 6, 7, 8, 16, 32, 64, 128, 128, 128, 128], jnp.float32)
    lags = lags[None, :, None]
    magnitude = jnp.exp(-decay_rate * lags)
    phase = frequency * lags
    return jnp.concatenate([magnitude * jnp.cos(phase), magnitude * jnp.sin(phase)], axis=2)


def cmul(ar, ai, br, bi):
    return ar * br - ai * bi, ar * bi + ai * br


def fill_tables(c, states, low_ref, up_ref, down_ref):
    for lane in range(0, states, 128):
        re_lanes = pl.ds(lane, 128)
        im_lanes = pl.ds(states + lane, 128)
        base = low_ref[c, 0:8, re_lanes], low_ref[c, 0:8, im_lanes]
        for ref, forward in ((up_ref, True), (down_ref, False)):
            if forward:
                re, im = base
            else:
                re = jnp.concatenate([base[0][7 - k : 8 - k] for k in range(8)], axis=0)
                im = jnp.concatenate([base[1][7 - k : 8 - k] for k in range(8)], axis=0)
            for k in range(4):
                nr, ni = cmul(
                    re,
                    im,
                    low_ref[c, 8 + k : 9 + k, re_lanes],
                    low_ref[c, 8 + k : 9 + k, im_lanes],
                )
                if forward:
                    re = jnp.concatenate([re, nr], axis=0)
                    im = jnp.concatenate([im, ni], axis=0)
                else:
                    re = jnp.concatenate([nr, re], axis=0)
                    im = jnp.concatenate([ni, im], axis=0)
            for lanes, entries in ((re_lanes, re), (im_lanes, im)):
                high, rest = split_rows(entries)
                ref[c, 0, :, lanes] = high
                if ref.shape[1] > 1:
                    ref[c, 1, :, lanes] = rest


def nt(a, b):
    return lax.dot_general(a, b, (((1,), (1,)), ((), ())), preferred_element_type=jnp.float32)


def nn(a, b):
    return lax.dot_general(a, b, (((1,), (0,)), ((), ())), preferred_element_type=jnp.float32)


def tn(a, b):
    return lax.dot_general(a, b, (((0,), (0,)), ((), ())), preferred_element_type=jnp.float32)


def split_rows(row):
    high = row.astype(jnp.bfloat16)
    rest = (row - high.astype(jnp.float32)).astype(jnp.bfloat16)
    return high, rest


def toeplitz(kernel_row):
    spread = jnp.broadcast_to(kernel_row, (BLOCK, BLOCK))
    rolled = pltpu.roll(spread, 0, 1, stride=1, stride_axis=0)
    rows = lax.broadcasted_iota(jnp.int32, (BLOCK, BLOCK), 0)
    columns = lax.broadcasted_iota(jnp.int32, (BLOCK, BLOCK), 1)
    return jnp.where(columns >= rows, rolled, 0.0)


def put_rows(ref, c, places, group, block):
    for k in range(ref.shape[0]):
        ref[k, pl.ds(c, places, stride=group), :] = block[:, 128 * k : 128 * (k + 1)]


def get_rows(ref, c, places, group):
    chunks = [ref[k, pl.ds(c, places, stride=group), :] for k in range(ref.shape[0])]
    return jnp.concatenate(chunks, axis=1)


def get_step(ref, rows, half):
    count = ref.shape[0] // 2
    return jnp.concatenate([ref[half * count + k, rows, :] for k in range(count)], axis=1)


def put_step(ref, rows, half, block):
    count = ref.shape[0] // 2
    for k in range(count):
        ref[half * count + k, rows, :] = block[:, 128 * k : 128 * (k + 1)]


def gather_rows(pick, ref, c, mask):
    rows = [nn(p, ref[c, :, BLOCK * h : BLOCK * (h + 1)]) for h, p in enumerate(pick)]
    return sum(rows).astype(jnp.bfloat16) * mask


def scatter_rows(pick, ref, c, result, mask):
    low = result.astype(jnp.bfloat16) * mask
    for h, p in enumerate(pick):
        ref[c, :, BLOCK * h : BLOCK * (h + 1)] = tn(p, low).astype(jnp.bfloat16)


def forward_kernel(
    active, follows_ref, pick_ref, mask_ref, values_ref, low_ref, lam_ref, coef_ref,
    out_ref, start_ref, taps_ref, token_ref, up_ref, down_ref, work_ref,
):
    token_ref[...] = jnp.zeros_like(token_ref)
    places = pick_ref.shape[1]
    group, states = coef_ref.shape[0], coef_ref.shape[1] // 2
    if active < group:
        work_ref[...] = jnp.zeros_like(work_ref)
    mask = mask_ref[...]
    pick = [pick_ref[h] for h in range(pick_ref.shape[0])]
    each = range(active)
    spread = [gather_rows(pick, values_ref, c, mask) for c in each]
    for c in each:
        fill_tables(c, states, low_ref, up_ref, down_ref)
    for c in each:
        ends = nn(spread[c], down_ref[c, 0]) + nn(spread[c], down_ref[c, 1])
        put_rows(work_ref, c, places, group, ends)
    lam_re, lam_im = lam_ref[0, :, :states], lam_ref[0, :, states:]
    far_re, far_im = lam_ref[1, :, :states], lam_ref[1, :, states:]
    coef_re, coef_im = coef_ref[:, :states], coef_ref[:, states:]
    mix_re, mix_im = cmul(coef_re, coef_im, lam_re, lam_im)

    def advance(p, carry):
        re, im = carry
        rows = pl.ds(pl.multiple_of(p * group, group), group)
        keep = follows_ref[p]
        re, im = re * keep, im * keep
        start_ref[rows, :states] = re
        start_ref[rows, states:] = im
        far = cmul(re, im, far_re, far_im)
        new_re = far[0] + get_step(work_ref, rows, 0)
        new_im = far[1] + get_step(work_ref, rows, 1)
        mixed = cmul(re, im, mix_re, mix_im)
        put_step(work_ref, rows, 0, mixed[0])
        put_step(work_ref, rows, 1, -mixed[1])
        return new_re, new_im

    zero = jnp.zeros((group, states), jnp.float32)
    lax.fori_loop(0, places, advance, (zero, zero), unroll=4)
    carried, taps = [], []
    for c in each:
        row = jnp.concatenate([coef_ref[c : c + 1, :states], -coef_ref[c : c + 1, states:]], axis=1)
        high, rest = split_rows(row)
        rows = jnp.concatenate([high, rest, jnp.zeros((14, 2 * states), jnp.bfloat16)], axis=0)
        mixed = split_rows(get_rows(work_ref, c, places, group))
        stack = jnp.concatenate([mixed[0], rows, mixed[1]], axis=0)
        coarse = nt(stack, up_ref[c, 0])
        finer = nt(stack[: places + 16], up_ref[c, 1])
        carried.append(coarse[:places] + coarse[places + 16 :] + finer[:places])
        kernel_row = coarse[places : places + 16] + finer[places:]
        taps.append(split_rows(toeplitz(kernel_row[0:1] + kernel_row[1:2])))
        taps_ref[c] = taps[c][0]
    results = [
        carried[c] + nn(spread[c], taps[c][0]) + nn(spread[c], taps[c][1]) for c in each
    ]
    for c in each:
        scatter_rows(pick, out_ref, c, results[c], mask)


def backward_kernel(
    active, follows_ref, pick_ref, mask_ref, values_ref, grads_ref, low_ref, lam_ref, coef_ref,
    start_ref, taps_ref, out_ref, sum_ref, token_ref, up_ref, down_ref, work_ref,
):
    token_ref[...] = jnp.zeros_like(token_ref)
    places = pick_ref.shape[1]
    group, states = coef_ref.shape[0], coef_ref.shape[1] // 2
    if active < group:
        work_ref[...] = jnp.zeros_like(work_ref)
        sum_ref[...] = jnp.zeros_like(sum_ref)
    mask = mask_ref[...]
    pick = [pick_ref[h] for h in range(pick_ref.shape[0])]
    rows = lax.broadcasted_iota(jnp.int32, (BLOCK, BLOCK), 0)
    columns = lax.broadcasted_iota(jnp.int32, (BLOCK, BLOCK), 1)
    turn = (rows + columns == BLOCK - 1).astype(jnp.bfloat16)
    each = range(active)
    values = [gather_rows(pick, values_ref, c, mask) for c in each]
    grads = [gather_rows(pick, grads_ref, c, mask) for c in each]
    turned = [nn(values[c], turn).astype(jnp.bfloat16) for c in each]
    pairs = [tn(turned[c], grads[c]) for c in each]
    for c in each:
        fill_tables(c, states, low_ref, up_ref, down_ref)
    stacks = []
    for c in each:
        skewed = pltpu.roll(pairs[c], 1, 1, stride=1, stride_axis=0)
        lag_sum = jnp.sum(jnp.where(columns <= rows, skewed, 0.0), axis=0, keepdims=True)
        high, rest = split_rows(lag_sum)
        extra = jnp.concatenate([high, rest, jnp.zeros((14, BLOCK), jnp.bfloat16)], axis=0)
        stacks.append(jnp.concatenate([grads[c], extra], axis=0))
    for c in each:
        folded = nn(stacks[c], up_ref[c, 0])
        put_rows(work_ref, c, places, group, folded[:places])
        sum_ref[c : c + 1, :] = folded[places : places + 1] + folded[places + 1 : places + 2]
    lam_re, lam_im = lam_ref[0, :, :states], lam_ref[0, :, states:]
    far_re, far_im = lam_ref[1, :, :states], lam_ref[1, :, states:]
    coef_re, coef_im = coef_ref[:, :states], coef_ref[:, states:]

    def retreat(step, carry):
        re, im, total_re, total_im = carry
        p = places - 1 - step
        rows = pl.ds(pl.multiple_of(p * group, group), group)
        near = cmul(get_step(work_ref, rows, 0), get_step(work_ref, rows, 1), lam_re, lam_im)
        begin = start_ref[rows, :states], start_ref[rows, states:]
        product = cmul(begin[0], begin[1], near[0], near[1])
        mixed = cmul(re, im, coef_re, coef_im)
        put_step(work_ref, rows, 0, mixed[0])
        put_step(work_ref, rows, 1, -mixed[1])
        keep = follows_ref[p]
        far = cmul(re, im, far_re, far_im)
        return (
            (near[0] + far[0]) * keep,
            (near[1] + far[1]) * keep,
            total_re + product[0],
            total_im + product[1],
        )

    zero = jnp.zeros((group, states), jnp.float32)
    _, _, total_re, total_im = lax.fori_loop(0, places, retreat, (zero, zero, zero, zero), unroll=4)
    sum_ref[:, :states] = sum_ref[:, :states] + total_re
    sum_ref[:, states:] = -(sum_ref[:, states:] + total_im)
    near = [nt(grads[c], taps_ref[c]) for c in each]
    results = []
    for c in each:
        mixed = get_rows(work_ref, c, places, group).astype(jnp.bfloat16)
        results.append(nt(mixed, down_ref[c, 0]) + near[c])
    for c in each:
        scatter_rows(pick, out_ref, c, results[c], mask)


def whole(shape):
    return pl.BlockSpec(shape, lambda i: (0,) * len(shape))


def part(shape, place, dim=0):
    index = tuple(place if k == dim else 0 for k in range(len(shape)))
    return pl.BlockSpec(shape, lambda i: index)


class Parts:
    def __init__(self, kernel, name, inputs, results, scratch, parts, flops):
        self.kernel, self.name, self.inputs, self.results = kernel, name, inputs, results
        self.scratch, self.parts, self.flops = scratch, parts, flops
        self.done, self.outs, self.waits = 0, [], []

    def run(self, *waits):
        self.waits += waits
        if self.done < self.parts - 1:
            return self.call()
        return None

    def last(self, *waits):
        self.waits += waits
        return self.call()

    def call(self):
        k = self.done
        operands = [array for array, _ in self.inputs]
        specs = [spec(k) for _, spec in self.inputs]
        count, waits, before = len(operands), self.waits, list(self.outs)

        def body(*refs):
            self.kernel(*refs[:count], *refs[count + len(waits) + len(before) :])

        token = jax.ShapeDtypeStruct((8, 128), jnp.float32)
        *self.outs, token = pl.pallas_call(
            body,
            grid=(1,),
            in_specs=specs + [pl.BlockSpec(memory_space=pl.ANY)] * (len(waits) + len(before)),
            out_specs=[spec(k) for _, spec in self.results] + [whole((8, 128))],
            out_shape=[shape for shape, _ in self.results] + [token],
            input_output_aliases={count + len(waits) + n: n for n in range(len(before))},
            scratch_shapes=self.scratch,
            compiler_params=pltpu.CompilerParams(vmem_limit_bytes=48 * 2**20),
            cost_estimate=pl.CostEstimate(
                flops=self.flops, bytes_accessed=4 * 2**20, transcendentals=0
            ),
            name=self.name,
        )(*operands, *waits, *before)
        self.done, self.waits = k + 1, []
        return token


def scratches(active, group, places, states, tables):
    return [
        pltpu.VMEM((active, tables, BLOCK, 2 * states), jnp.bfloat16),
        pltpu.VMEM((active, tables, BLOCK, 2 * states), jnp.bfloat16),
        pltpu.VMEM((2 * states // 128, places * group, 128), jnp.float32),
    ]


def padded(values, lams, coefs):
    channels = values.shape[0]
    group, active = 8, min(8, channels)
    spare = max(0, group - channels)
    lams = jnp.pad(lams, ((0, 0), (0, spare), (0, 0)))
    coefs = jnp.pad(coefs, ((0, spare), (0, 0)))
    return group, active, spare, lams, coefs


def mix_forward(values, pieces, powers, lams, coefs):
    channels, shares, width = values.shape
    pick, mask, follows = pieces
    places, states = pick.shape[1], coefs.shape[1] // 2
    group, active, spare, lams, coefs = padded(values, lams, coefs)
    full = lambda shape: lambda k: whole(shape)
    inputs = [
        (follows, lambda k: pl.BlockSpec(memory_space=pltpu.SMEM)),
        (pick, full(pick.shape)),
        (mask, full((places, BLOCK))),
        (values, lambda k: part((active, shares, width), k)),
        (powers, lambda k: part((active, 16, 2 * states), k)),
        (lams, lambda k: part((2, group, 2 * states), k, 1)),
        (coefs, lambda k: part((group, 2 * states), k)),
    ]
    f32 = jnp.float32
    results = [
        (
            jax.ShapeDtypeStruct(values.shape, jnp.bfloat16),
            lambda k: part((active, shares, width), k),
        ),
        (
            jax.ShapeDtypeStruct((places * (channels + spare), 2 * states), f32),
            lambda k: part((places * group, 2 * states), k),
        ),
        (
            jax.ShapeDtypeStruct((channels, BLOCK, BLOCK), jnp.bfloat16),
            lambda k: part((active, BLOCK, BLOCK), k),
        ),
    ]
    return Parts(
        functools.partial(forward_kernel, active),
        "mix_forward",
        inputs,
        results,
        scratches(active, group, places, states, 2),
        channels // active,
        8 * 10**9,
    )


def mix_backward(values, grads, pieces, powers, lams, coefs, starts, taps):
    channels, shares, width = values.shape
    pick, mask, follows = pieces
    places, states = pick.shape[1], coefs.shape[1] // 2
    group, active, spare, lams, coefs = padded(values, lams, coefs)
    full = lambda shape: lambda k: whole(shape)
    inputs = [
        (follows, lambda k: pl.BlockSpec(memory_space=pltpu.SMEM)),
        (pick, full(pick.shape)),
        (mask, full((places, BLOCK))),
        (values, lambda k: part((active, shares, width), k)),
        (grads, lambda k: part((active, shares, width), k)),
        (powers, lambda k: part((active, 16, 2 * states), k)),
        (lams, lambda k: part((2, group, 2 * states), k, 1)),
        (coefs, lambda k: part((group, 2 * states), k)),
        (starts, lambda k: part((places * group, 2 * states), k)),
        (taps, lambda k: part((active, BLOCK, BLOCK), k)),
    ]
    results = [
        (
            jax.ShapeDtypeStruct(values.shape, jnp.bfloat16),
            lambda k: part((active, shares, width), k),
        ),
        (
            jax.ShapeDtypeStruct((channels + spare, 2 * states), jnp.float32),
            lambda k: part((group, 2 * states), k),
        ),
    ]
    return Parts(
        functools.partial(backward_kernel, active),
        "mix_backward",
        inputs,
        results,
        scratches(active, group, places, states, 1),
        channels // active,
        107 * 10**8,
    )


def mixer_inputs(poles, params):
    table = powers_of(poles)
    lams = jnp.stack([table[:, 1], table[:, 12]])
    coefs = jnp.concatenate([params[0], params[1]], axis=1)
    return table, lams, coefs


def adam_step(weight, gradient, first_moment, second, step_value, step_rate, decay_rate):
    first_new = beta_first * first_moment + (1.0 - beta_first) * gradient
    second_new = beta_second * second + (1.0 - beta_second) * gradient * gradient
    first_hat = first_new / (1.0 - jnp.power(beta_first, step_value))
    second_hat = second_new / (1.0 - jnp.power(beta_second, step_value))
    weight_new = weight - step_rate * (
        first_hat / (jnp.sqrt(second_hat) + epsilon_adam) + decay_rate * weight
    )
    return (weight_new, first_new, second_new)


class Cube:
    def __init__(self, tok_size):
        self.size = 2 * tok_size
        bits = tok_size.bit_length() - 1
        across = bits // 3
        self.xs = [1 + k for k in range(across)]
        self.ys = [1 + across + k for k in range(across)]
        self.zs = [1 + k for k in range(2 * across, bits)]
        self.place = lax.axis_index("tok") * 2 + lax.axis_index("rep")

    def bit(self, b):
        return lax.rem(lax.div(self.place, 1 << b), 2)

    def swap(self, block, b):
        return self.trade(block, 1 << b)

    def trade(self, block, mask):
        pairs = [(i, i ^ mask) for i in range(self.size)]
        return lax.ppermute(block, ("tok", "rep"), pairs)

    def halves(self, block, have, b):
        above = 1 << sum(1 for k in have if k > b)
        split = block.reshape((above, 2, -1) + block.shape[1:])
        index = self.bit(b)
        mine = lax.dynamic_index_in_dim(split, index, 1, keepdims=False)
        other = lax.dynamic_index_in_dim(split, 1 - index, 1, keepdims=False)
        shape = (-1,) + block.shape[1:]
        return mine.reshape(shape), other.reshape(shape)

    def split(self, block):
        stack = block.reshape((self.size, -1) + block.shape[1:])
        return self.halves(stack, range(self.size.bit_length() - 1), 0)

    def merge(self, mine, other):
        swapped = self.bit(0) == 1
        first, second = jnp.where(swapped, other, mine), jnp.where(swapped, mine, other)
        pair = jnp.stack([first, second], axis=1)
        return pair.reshape((-1,) + pair.shape[3:])


class Gather:
    def __init__(self, cube, shard, order):
        self.cube, self.order, self.have = cube, list(order), []
        self.block, self.going = shard[None], False

    def send(self, *waits):
        if self.order and not self.going:
            self.arriving = self.cube.swap(after(self.block, *waits), self.order[0])
            self.going = True

    def join(self, mine, other, b):
        above = 1 << sum(1 for k in self.have if k > b)
        shape = (above, 1, -1) + mine.shape[1:]
        first, second = mine.reshape(shape), other.reshape(shape)
        joined = jnp.where(
            self.cube.bit(b) == 1,
            jnp.concatenate([second, first], axis=1),
            jnp.concatenate([first, second], axis=1),
        )
        return joined.reshape((2 * mine.shape[0],) + mine.shape[1:])

    def take(self, *waits):
        self.send()
        if self.order:
            b, self.going = self.order.pop(0), False
            self.block = self.join(self.block, after(self.arriving, *waits), b)
            self.have.append(b)

    def direct(self, bits):
        masks = [sum(1 << b for k, b in enumerate(bits) if n >> k & 1) for n in range(1 << len(bits))]
        blocks = {m: self.cube.trade(self.block, m) if m else self.block for m in masks}
        for b in bits:
            blocks = {
                m: self.join(blocks[m], blocks[m | 1 << b], b) for m in blocks if not m >> b & 1
            }
            self.have.append(b)
        self.block = blocks[0]

    def rest(self):
        while self.order:
            self.take()

    def both(self):
        return self.block, self.cube.swap(self.block, 0)


class Scatter:
    def __init__(self, cube, keep, send, order, have, wide=()):
        self.cube, self.order, self.have = cube, list(order), list(have)
        self.keep, self.sent, self.wide = keep, send, wide
        self.going = False

    def send(self, *waits):
        if self.order and not self.going:
            self.arriving = self.cube.swap(after(self.sent, *waits), self.order[0])
            self.going = True

    def take(self, *waits):
        self.send()
        if not self.order:
            return
        b, self.going = self.order.pop(0), False
        self.have.remove(b)
        total = self.keep + after(self.arriving, *waits).astype(jnp.float32)
        if not self.order:
            self.keep, self.sent = total, total
            return
        self.keep, sent = self.cube.halves(total, self.have, self.order[0])
        self.sent = sent if self.order[0] in self.wide else sent.astype(jnp.bfloat16)

    def rest(self):
        while self.order:
            self.take()
        return self.keep[0]


def direct_sum(cube, total, have, bits, kind):
    have, parts = list(have), {0: total}
    for b in bits:
        halves = {m: cube.halves(part, have, b) for m, part in parts.items()}
        have.remove(b)
        parts = {m | k << b: halves[m][k] for m in halves for k in range(2)}
    keep = parts.pop(0)
    return keep + sum(cube.trade(p.astype(kind), m).astype(jnp.float32) for m, p in parts.items())


def after(block, *waits):
    return lax.optimization_barrier((block, *waits))[0] if waits else block


def gelu_parts(a):
    root = 0.7978845608028654
    square = a * a
    t = jnp.tanh(root * a * (1.0 + 0.044715 * square))
    half = 0.5 * (1.0 + t)
    slope = half + 0.5 * a * (1.0 - t * t) * root * (1.0 + 3.0 * 0.044715 * square)
    return a * half, slope


def gate_kernel(
    split, core_ref, normed_ref, state_refs, grad_ref, up_refs, expand_refs, down_refs,
    grad_out, up_out, gated_refs, state_outs, norm_outs, state_scratch, sum_scratch, norm_scratch,
):
    step, last = pl.program_id(0), pl.num_programs(0) - 1
    channels = state_refs[0].shape[0]
    swapped = core_ref[0] == 1

    @pl.when(step == 0)
    def _():
        for k in range(2):
            turned = state_refs[k][...].astype(jnp.float32).T
            state_scratch[:, channels * k : channels * (k + 1)] = turned.astype(jnp.bfloat16)
        sum_scratch[...] = jnp.zeros_like(sum_scratch)
        norm_scratch[...] = jnp.zeros_like(norm_scratch)

    def pair(mine, other):
        return jnp.where(swapped, other, mine), jnp.where(swapped, mine, other)

    rows = normed_ref.shape[1] // 2
    up_pre = nn(normed_ref[:, :rows], up_refs[0][...]) + nn(normed_ref[:, rows:], up_refs[1][...])
    if split:
        down = []
        for s in range(down_refs[0].shape[0]):
            down += pair(down_refs[0][s], down_refs[1][s])
        down = jnp.concatenate(down, axis=0)
    else:
        down = down_refs[0][...]
    gated_grad = nt(grad_ref[...], down)
    expanded = nn(state_scratch[:, :channels], expand_refs[0][...]) + nn(
        state_scratch[:, channels:], expand_refs[1][...]
    )
    upper, slope = gelu_parts(up_pre)
    expanded_grad = (gated_grad * upper).astype(jnp.bfloat16)
    grad_out[...] = expanded_grad
    up_pre_grad = (gated_grad * expanded * slope).astype(jnp.bfloat16)
    up_out[...] = up_pre_grad
    gated = (upper * expanded).T.astype(jnp.bfloat16)
    if split:
        size = gated_refs[0].shape[1]
        for s in range(gated_refs[0].shape[0]):
            first = gated[2 * s * size : (2 * s + 1) * size]
            second = gated[(2 * s + 1) * size : (2 * s + 2) * size]
            mine, other = pair(first, second)
            gated_refs[0][s] = mine
            gated_refs[1][s] = other
    else:
        gated_refs[0][...] = gated
    for k in range(2):
        sum_scratch[:, channels * k : channels * (k + 1)] += nt(expanded_grad, expand_refs[k][...])
        norm_scratch[:, rows * k : rows * (k + 1)] += nt(up_pre_grad, up_refs[k][...])

    @pl.when(step == last)
    def _():
        for k in range(2):
            total = sum_scratch[:, channels * k : channels * (k + 1)].T
            state_outs[k][...] = total.astype(jnp.bfloat16)
            norm_outs[k][...] = norm_scratch[:, rows * k : rows * (k + 1)].T


def gate(cube, normed, states, grad_rows, ups, expands, downs):
    tokens, width = grad_rows.shape
    hidden = ups[0].shape[1]
    split = downs[0].shape[1] % 16 == 0
    block = 2 * downs[0].shape[1] * max(1, 192 // downs[0].shape[1]) if split else 384
    low, f32 = jnp.bfloat16, jnp.float32
    full = lambda array: pl.BlockSpec(array.shape, lambda i: (0,) * array.ndim)
    if split:
        shards = block // (2 * downs[0].shape[1])
        down_spec = pl.BlockSpec((shards,) + downs[0].shape[1:], lambda i: (i, 0, 0))
        gated_shape = jax.ShapeDtypeStruct(downs[0].shape[:2] + (tokens,), low)
        gated_spec = pl.BlockSpec((shards, downs[0].shape[1], tokens), lambda i: (i, 0, 0))
        count = 2
    else:
        downs = [cube.merge(*downs)]
        down_spec = pl.BlockSpec((block, width), lambda i: (i, 0))
        gated_shape = jax.ShapeDtypeStruct((hidden, tokens), low)
        gated_spec = pl.BlockSpec((block, tokens), lambda i: (i, 0))
        count = 1
    columns = lambda array: pl.BlockSpec((array.shape[0], block), lambda i: (0, i))
    channels = states[0].shape[0]
    row_spec = pl.BlockSpec((tokens, block), lambda i: (0, i))
    state_shape = jax.ShapeDtypeStruct((channels, tokens), low)
    norm_shape = jax.ShapeDtypeStruct((width // 2, tokens), f32)

    def body(core, normed, s0, s1, grad, u0, u1, e0, e1, *refs):
        down_refs, refs = refs[:count], refs[count:]
        grad_out, up_out, gated_refs, refs = refs[0], refs[1], refs[2 : 2 + count], refs[2 + count :]
        gate_kernel(
            split, core, normed, (s0, s1), grad, (u0, u1), (e0, e1), down_refs,
            grad_out, up_out, gated_refs, refs[:2], refs[2:4], *refs[4:],
        )

    outs = pl.pallas_call(
        body,
        grid=(hidden // block,),
        in_specs=[pl.BlockSpec(memory_space=pltpu.SMEM), full(normed)]
        + [full(s) for s in states]
        + [full(grad_rows)]
        + [columns(u) for u in ups]
        + [columns(e) for e in expands]
        + [down_spec] * count,
        out_specs=[row_spec, row_spec]
        + [gated_spec] * count
        + [full(state_shape)] * 2
        + [full(norm_shape)] * 2,
        out_shape=[jax.ShapeDtypeStruct((tokens, hidden), low)] * 2
        + [gated_shape] * count
        + [state_shape] * 2
        + [norm_shape] * 2,
        scratch_shapes=[
            pltpu.VMEM((tokens, 2 * channels), low),
            pltpu.VMEM((tokens, 2 * channels), f32),
            pltpu.VMEM((tokens, width), f32),
        ],
        compiler_params=pltpu.CompilerParams(vmem_limit_bytes=48 * 2**20),
        cost_estimate=pl.CostEstimate(
            flops=10**6, bytes_accessed=2**10, transcendentals=0
        ),
        name="gate",
    )(cube.bit(0).reshape(1), normed, *states, grad_rows, *ups, *expands, *downs)
    grad_out, up_out = outs[:2]
    gated = outs[2 : 2 + count]
    gated = gated if split else cube.split(gated[0])
    return grad_out, up_out, gated, outs[2 + count : 4 + count], outs[4 + count :]


def value_kernel(
    width, grad_ref, pre_ref, value_refs, normed_refs, hat_refs, part_refs, keep_ref, send_ref, out_refs
):
    slope = gelu_parts(pre_ref[...])[1]
    grad = (grad_ref[...].astype(jnp.float32) * slope).astype(jnp.bfloat16)
    for k, ref in ((1, send_ref), (0, keep_ref)):
        total = part_refs[k][...] + nn(value_refs[k][:, :width], grad)
        out_refs[k][...] = total
        ref[:, :width] = nt(normed_refs[k][...], grad).astype(ref.dtype)
        lane = lax.broadcasted_iota(jnp.int32, (total.shape[0], 128), 1)
        gain = jnp.sum(total * hat_refs[k][...], axis=1, keepdims=True)
        shift = jnp.sum(total, axis=1, keepdims=True)
        columns = jnp.where(lane == 0, gain, jnp.where(lane == 1, shift, 0.0))
        ref[:, width:] = columns.astype(ref.dtype)


def value_grads(width, value_grad, value_pre, packs, normed, hats, parts):
    rows, tokens = normed[0].shape
    columns = packs[0].shape[1]

    def body(grad, pre, p0, p1, n0, n1, h0, h1, a0, a1, keep, send, g0, g1):
        value_kernel(
            width, grad, pre, (p0, p1), (n0, n1), (h0, h1), (a0, a1), keep, send, (g0, g1)
        )

    operands = (value_grad, value_pre, *packs, *normed, *hats, *parts)
    results = [((rows, columns), jnp.float32), ((rows, columns), jnp.bfloat16)]
    results += [((rows, tokens), jnp.float32)] * 2
    keep, send, first, second = pl.pallas_call(
        body,
        grid=(1,),
        in_specs=[whole(a.shape) for a in operands],
        out_specs=[whole(shape) for shape, _ in results],
        out_shape=[jax.ShapeDtypeStruct(shape, kind) for shape, kind in results],
        compiler_params=pltpu.CompilerParams(vmem_limit_bytes=48 * 2**20),
        cost_estimate=pl.CostEstimate(flops=10**6, bytes_accessed=2**10, transcendentals=0),
        name="value_grads",
    )(*operands)
    return keep, send, (first, second)


def products_kernel(bit_ref, own_send, own_keep, got_send, got_keep, own, got, send_ref, keep_ref):
    def product(a, b):
        flat = lambda ref: ref[...].reshape((-1, ref.shape[3]))
        return nn(flat(a), own[...]) + nn(flat(b), got[...])

    send_ref[...] = product(own_send, got_send).astype(jnp.bfloat16)
    keep_ref[...] = product(own_keep, got_keep)


def products(cube, lefts, rights, first, have):
    shards, rows, tokens = lefts[0].shape
    columns = rights[0].shape[1]
    above = 1 << sum(1 for k in have if k > first)
    shape = (shards // 2, rows, columns)
    if rows % 16:
        sides = [cube.halves(left, have, first) for left in lefts]
        keep, send = [
            sum(
                dot(pair[k].reshape((-1, tokens)), right, 1, 0)
                for pair, right in zip(sides, rights)
            ).reshape(shape)
            for k in range(2)
        ]
        return keep, send.astype(jnp.bfloat16)
    lefts = [left.reshape((above, 2, -1, tokens)) for left in lefts]
    side = (above, 1) + lefts[0].shape[2:]
    send_spec = pl.BlockSpec(side, lambda j, bit: (0, 1 - bit[0], 0, 0))
    keep_spec = pl.BlockSpec(side, lambda j, bit: (0, bit[0], 0, 0))
    block = min(columns, 1024)
    count = shards * rows // 2
    right_spec = pl.BlockSpec((tokens, block), lambda j, bit: (0, j))
    out_spec = pl.BlockSpec((count, block), lambda j, bit: (0, j))
    send, keep = pl.pallas_call(
        products_kernel,
        grid_spec=pltpu.PrefetchScalarGridSpec(
            num_scalar_prefetch=1,
            grid=(columns // block,),
            in_specs=[send_spec, keep_spec] * 2 + [right_spec] * 2,
            out_specs=[out_spec] * 2,
        ),
        out_shape=[
            jax.ShapeDtypeStruct((count, columns), jnp.bfloat16),
            jax.ShapeDtypeStruct((count, columns), jnp.float32),
        ],
        compiler_params=pltpu.CompilerParams(vmem_limit_bytes=48 * 2**20),
        cost_estimate=pl.CostEstimate(
            flops=10**6, bytes_accessed=2**10, transcendentals=0
        ),
        name="weight_grad",
    )(cube.bit(first).reshape(1), lefts[0], lefts[0], lefts[1], lefts[1], *rights)
    return keep.reshape(shape), send.reshape(shape)


def dot(a, b, a_dim, b_dim):
    return lax.dot_general(
        a, b, (((a_dim,), (b_dim,)), ((), ())), preferred_element_type=jnp.float32
    )


def per_device(
    tok_size,
    tokens,
    cotangent,
    lengths,
    up_weight,
    value_weight,
    expand_weight,
    down_weight,
    norm_params,
    state_params,
    state_poles,
    up_mean,
    up_square,
    value_mean,
    value_square,
    expand_mean,
    expand_square,
    down_mean,
    down_square,
    norm_mean,
    norm_square,
    state_mean,
    state_square,
):
    low = jnp.bfloat16
    cube = Cube(tok_size)
    xs, ys, zs = cube.xs, cube.ys, cube.zs
    down_zs, tok_bits = zs[::-1], xs + ys + zs
    nz, nx = len(zs), len(xs)

    def flat(block):
        return block.reshape((-1,) + block.shape[2:])

    def dots(lefts, rights, left_dim, right_dim):
        return dot(flat(lefts[0]), flat(rights[0]), left_dim, right_dim) + dot(
            flat(lefts[1]), flat(rights[1]), left_dim, right_dim
        )

    inner = value_weight.shape[1]
    norm_columns = jnp.pad(norm_params.T, ((0, 0), (0, 126)))
    packed = jnp.concatenate([value_weight, norm_columns], axis=1).astype(low)
    pack = Gather(cube, packed, xs + ys + down_zs)
    up = Gather(cube, up_weight.astype(low), down_zs + xs + ys)
    down = Gather(cube, down_weight.astype(low), down_zs + ys + xs)
    expand = Gather(cube, expand_weight.astype(low), xs + ys + down_zs)

    grad_rows = cotangent[0]
    token_rows = tokens[0].astype(jnp.float32)
    width = token_rows.shape[1]
    average = jnp.mean(token_rows, axis=1)
    centered = token_rows - average[:, None]
    scale = lax.rsqrt(jnp.mean(centered * centered, axis=1) + epsilon_norm)
    hats = [
        (part.astype(jnp.float32) - average) * scale for part in cube.split(tokens[0].T)
    ]

    expand.send()
    pack.direct(zs)
    up.send(pack.block)
    down.send(pack.block)
    if expand.order[1:]:
        expand.take(pack.block)
        expand.send()
    pack.direct(xs + ys)
    packs = pack.both()
    up.take()
    down.take()
    up.send()
    down.send()
    values = [pack[:, :, :inner] for pack in packs]
    gains = [pack[:, :, inner : inner + 1].astype(jnp.float32) for pack in packs]
    shifts = [pack[:, :, inner + 1 : inner + 2].astype(jnp.float32) for pack in packs]
    normed = [(h * g + b).astype(low) for h, g, b in zip(hats, gains, shifts)]
    value_preactivation = dots(values, normed, 0, 0)
    value_act = gelu_curve(value_preactivation)
    value_low = after(value_act.astype(low), up.block, down.block)
    channel_values = lax.all_to_all(value_low, "tok", split_axis=0, concat_axis=1, tiled=True)

    for _ in range(nz - 2):
        up.take(value_low)
        down.take(value_low)
        up.send()
        down.send()
    for _ in range(2 * nx - 2):
        expand.take(value_low)
        expand.send()
    poles, coefs = lax.optimization_barrier((state_poles, state_params, value_low))[:2]
    channels, length = channel_values.shape
    blocked = (channels, tok_size, length // tok_size)
    pieces = pieces_of(lengths[0], length, tok_size)
    powers, lams, coefs = mixer_inputs(poles, coefs)
    channel_values = channel_values.reshape(blocked)
    normed_rows = jnp.concatenate([flat(side).T for side in normed], axis=1)
    normed_swapped = cube.swap(normed[1], 0)
    columns_swapped = cube.swap(grad_rows, 0)
    mixer = mix_forward(channel_values, pieces, powers, lams, coefs)

    def run(*waits):
        token = mixer.run(*waits)
        return [] if token is None else [token]

    up.take(channel_values)
    down.take(channel_values)
    expand.take(channel_values)
    up.send()
    down.send()
    expand.send()
    token = run(up.block, down.block, expand.block)
    for _ in range(nx):
        up.take(*token)
        down.take(*token)
        up.send()
        down.send()
    expand.take(*token)
    if expand.order:
        expand.send()
    token = run(up.block, down.block, expand.block)
    token = run(*token)
    if expand.order:
        expand.take(*token)
    mixer.last(*token, expand.block, normed_swapped, columns_swapped, normed_rows)
    state_out, starts, taps = mixer.outs
    for part in (up, down):
        part.arriving = after(part.arriving, state_out)
    token_states = lax.all_to_all(
        state_out.reshape(channels, length), "tok", split_axis=1, concat_axis=0, tiled=True
    )
    state_sides = cube.split(token_states)
    expand.rest()
    up.rest()
    down.rest()
    ups, downs, expands = up.both(), down.both(), expand.both()

    expanded_grad, up_pre_grad, gated_sides, state_grads, ups_grads = gate(
        cube,
        normed_rows,
        [flat(side) for side in state_sides],
        grad_rows,
        [flat(side) for side in ups],
        [flat(side) for side in expands],
        downs,
    )
    state_grad = cube.merge(*[g.reshape(state_sides[0].shape) for g in state_grads])
    gated_swapped = cube.swap(gated_sides[1], 0)
    expanded_swapped = cube.swap(expanded_grad, 0)
    up_pre_swapped = cube.swap(after(up_pre_grad, gated_swapped), 0)
    state_swapped = cube.swap(state_sides[1], 0)

    def scatter(lefts, rights, order):
        keep, send = products(cube, lefts, rights, order[0], tok_bits)
        return Scatter(cube, keep, send, order, tok_bits)

    down_sums = scatter(
        (gated_sides[0], gated_swapped),
        (grad_rows, columns_swapped),
        xs + ys + zs,
    )
    up_sums = scatter((normed[0], normed_swapped), (up_pre_grad, up_pre_swapped), ys + xs + zs)
    expand_sums = scatter(
        (state_sides[0], state_swapped), (expanded_grad, expanded_swapped), zs + ys + xs
    )
    channel_grad = lax.all_to_all(state_grad, "tok", split_axis=0, concat_axis=1, tiled=True)
    channel_grad = channel_grad.reshape(blocked)
    down_sums.send()
    up_sums.send()
    expand_sums.send(channel_grad)
    mixer = mix_backward(
        channel_values, channel_grad, pieces, powers, lams, coefs, starts, taps
    )
    token = run(up_sums.sent, down_sums.sent, expand_sums.sent)
    token = run(*token)
    token = run(*token)
    expand_sums.take(*token)
    expand_sums.send()
    mixer.last(*token, expand_sums.sent)
    value_grad_channels, param_grad = mixer.outs
    states = param_grad.shape[1] // 2
    param_grad = jnp.stack([param_grad[:channels, :states], param_grad[:channels, states:]])
    param_sum = param_grad + cube.swap(param_grad, 0)
    for _ in range(nx):
        for sums in (down_sums, up_sums):
            sums.take(value_grad_channels)
            sums.send()
    value_grad = lax.all_to_all(
        value_grad_channels.reshape(channels, length),
        "tok",
        split_axis=1,
        concat_axis=0,
        tiled=True,
    )
    value_grad = after(value_grad, up_sums.sent, down_sums.sent)
    keep, send, normed_grads = value_grads(
        inner,
        value_grad,
        value_preactivation,
        [flat(part) for part in packs],
        [flat(part) for part in normed],
        [flat(part) for part in hats],
        ups_grads,
    )
    normed_grads = [g.reshape(h.shape) for g, h in zip(normed_grads, hats)]
    keep, send = [part.reshape(hats[0].shape[:2] + (-1,)) for part in (keep, send)]
    packed_sum = keep + cube.swap(send, 0).astype(jnp.float32)
    core_sum = packed_sum
    for _ in range(nx):
        for sums in (down_sums, up_sums, expand_sums):
            sums.take(send)
            sums.send()
    packed_sum = after(packed_sum, up_sums.sent, down_sums.sent)
    normed_grads = [after(g, core_sum) for g in normed_grads]
    gated_late = after(gated_sides[0], packed_sum), gated_sides[1]
    layer_out = (token_rows + dots(gated_late, downs, 0, 0)).astype(low)[None]
    packed_sum = direct_sum(cube, packed_sum, tok_bits, xs + ys, low)
    for sums in (down_sums, up_sums, expand_sums):
        sums.take(packed_sum)
        sums.send()
    packed_sum = direct_sum(cube, packed_sum, zs, zs, jnp.float32)[0]
    up_sum, down_sum, expand_sum = [
        sums.rest() for sums in (up_sums, down_sums, expand_sums)
    ]
    value_sum = packed_sum[:, :inner]
    norm_sum = packed_sum[:, inner : inner + 2].T
    hat_grads = [g * gain for g, gain in zip(normed_grads, gains)]
    hat_mean = sum(jnp.sum(d, axis=(0, 1)) for d in hat_grads) / width
    hat_product = sum(jnp.sum(d * h, axis=(0, 1)) for d, h in zip(hat_grads, hats)) / width
    row_grads = [(d - hat_mean - h * hat_product) * scale for d, h in zip(hat_grads, hats)]
    token_grad = (cube.merge(*row_grads).T + grad_rows.astype(jnp.float32))[None]
    step_value = jnp.float32(STEP)
    up_next, up_mean_next, up_square_next = adam_step(
        up_weight, up_sum, up_mean, up_square, step_value, 0.08, 0.1
    )
    value_next, value_mean_next, value_square_next = adam_step(
        value_weight, value_sum, value_mean, value_square, step_value, 0.08, 0.1
    )
    expand_next, expand_mean_next, expand_square_next = adam_step(
        expand_weight, expand_sum, expand_mean, expand_square, step_value, 0.08, 0.1
    )
    down_next, down_mean_next, down_square_next = adam_step(
        down_weight, down_sum, down_mean, down_square, step_value, 0.08, 0.1
    )
    norm_next, norm_mean_next, norm_square_next = adam_step(
        norm_params, norm_sum, norm_mean, norm_square, step_value, 1.0, 0.0
    )
    state_next, state_mean_next, state_square_next = adam_step(
        state_params, param_sum, state_mean, state_square, step_value, 0.006, 0.0
    )
    return (
        layer_out,
        token_grad,
        up_next,
        up_mean_next,
        up_square_next,
        value_next,
        value_mean_next,
        value_square_next,
        expand_next,
        expand_mean_next,
        expand_square_next,
        down_next,
        down_mean_next,
        down_square_next,
        norm_next,
        norm_mean_next,
        norm_square_next,
        state_next,
        state_mean_next,
        state_square_next,
    )


def solution(mesh):
    placed = (
        P("rep", "tok", None),
        P("rep", "tok", None),
        P("rep", None),
        P(("tok", "rep"), None),
        P(("tok", "rep"), None),
        P(("tok", "rep"), None),
        P(("tok", "rep"), None),
        P(None, ("tok", "rep")),
        P(None, "tok", None),
        P(None, "tok", None),
        P(("tok", "rep"), None),
        P(("tok", "rep"), None),
        P(("tok", "rep"), None),
        P(("tok", "rep"), None),
        P(("tok", "rep"), None),
        P(("tok", "rep"), None),
        P(("tok", "rep"), None),
        P(("tok", "rep"), None),
        P(None, ("tok", "rep")),
        P(None, ("tok", "rep")),
        P(None, "tok", None),
        P(None, "tok", None),
    )
    return jax.shard_map(
        functools.partial(per_device, mesh.shape["tok"]),
        mesh=mesh,
        in_specs=placed,
        out_specs=(
            P("rep", "tok", None),
            P("rep", "tok", None),
            P(("tok", "rep"), None),
            P(("tok", "rep"), None),
            P(("tok", "rep"), None),
            P(("tok", "rep"), None),
            P(("tok", "rep"), None),
            P(("tok", "rep"), None),
            P(("tok", "rep"), None),
            P(("tok", "rep"), None),
            P(("tok", "rep"), None),
            P(("tok", "rep"), None),
            P(("tok", "rep"), None),
            P(("tok", "rep"), None),
            P(None, ("tok", "rep")),
            P(None, ("tok", "rep")),
            P(None, ("tok", "rep")),
            P(None, "tok", None),
            P(None, "tok", None),
            P(None, "tok", None),
        ),
        check_vma=False,
    )
```

```python
import functools

import jax
import jax.numpy as jnp
from jax import lax
from jax.experimental import pallas as pl
from jax.experimental.pallas import tpu as pltpu
from jax.sharding import PartitionSpec as P

BLOCK = 128
STEP = 5


epsilon_norm = 1e-05
epsilon_adam = 1e-08
beta_first = 0.9
beta_second = 0.999


def gelu_curve(values):
    return jax.nn.gelu(values, approximate=True)


def pieces_of(lengths_row, length, shares):
    blocks = length // BLOCK
    each = blocks // shares
    items = lengths_row.shape[0]
    ends = jnp.cumsum(lengths_row, dtype=jnp.int32)
    heads = BLOCK * jnp.arange(blocks, dtype=jnp.int32)
    head_rank = jnp.arange(blocks, dtype=jnp.int32) + jnp.sum(
        (ends[None, :] < heads[:, None]).astype(jnp.int32), axis=1
    )
    end_rank = jnp.arange(items, dtype=jnp.int32) + jnp.sum(
        (heads[None, :] <= ends[:, None]).astype(jnp.int32), axis=1
    )
    places = jnp.arange(blocks + items, dtype=jnp.int32)[:, None]
    starts = jnp.sum(jnp.where(head_rank[None, :] == places, heads[None, :], 0), axis=1) + jnp.sum(
        jnp.where(end_rank[None, :] == places, ends[None, :], 0), axis=1
    )
    stops = jnp.concatenate([starts[1:], jnp.full((1,), length, jnp.int32)])
    owner = starts // BLOCK
    segment = jnp.sum((ends[None, :] <= starts[:, None]).astype(jnp.int32), axis=1)
    positions = owner[:, None] * BLOCK + jnp.arange(BLOCK, dtype=jnp.int32)[None, :]
    mask = (positions >= starts[:, None]) & (positions < stops[:, None])
    heads = each * jnp.arange(shares, dtype=jnp.int32)[None, None, :]
    heads = heads + jnp.arange(each, dtype=jnp.int32)[:, None, None]
    pick = owner[None, :, None] == heads
    follows = (segment[1:] == segment[:-1]) & (owner[1:] != owner[:-1])
    follows = jnp.concatenate([jnp.zeros((1,), bool), follows])
    return (
        pick.astype(jnp.bfloat16),
        mask.astype(jnp.bfloat16),
        follows.astype(jnp.float32),
    )


def powers_of(poles):
    decay_rate = jnp.exp(poles[0])[:, None, :]
    frequency = poles[1][:, None, :]
    lags = jnp.array([0, 1, 2, 3, 4, 5, 6, 7, 8, 16, 32, 64, 128, 128, 128, 128], jnp.float32)
    lags = lags[None, :, None]
    magnitude = jnp.exp(-decay_rate * lags)
    phase = frequency * lags
    return jnp.concatenate([magnitude * jnp.cos(phase), magnitude * jnp.sin(phase)], axis=2)


def cmul(ar, ai, br, bi):
    return ar * br - ai * bi, ar * bi + ai * br


def fill_tables(c, states, low_ref, up_ref, down_ref):
    for lane in range(0, states, 128):
        re_lanes = pl.ds(lane, 128)
        im_lanes = pl.ds(states + lane, 128)
        base = low_ref[c, 0:8, re_lanes], low_ref[c, 0:8, im_lanes]
        for ref, forward in ((up_ref, True), (down_ref, False)):
            if forward:
                re, im = base
            else:
                re = jnp.concatenate([base[0][7 - k : 8 - k] for k in range(8)], axis=0)
                im = jnp.concatenate([base[1][7 - k : 8 - k] for k in range(8)], axis=0)
            for k in range(4):
                nr, ni = cmul(
                    re,
                    im,
                    low_ref[c, 8 + k : 9 + k, re_lanes],
                    low_ref[c, 8 + k : 9 + k, im_lanes],
                )
                if forward:
                    re = jnp.concatenate([re, nr], axis=0)
                    im = jnp.concatenate([im, ni], axis=0)
                else:
                    re = jnp.concatenate([nr, re], axis=0)
                    im = jnp.concatenate([ni, im], axis=0)
            for lanes, entries in ((re_lanes, re), (im_lanes, im)):
                high, rest = split_rows(entries)
                ref[c, 0, :, lanes] = high
                if ref.shape[1] > 1:
                    ref[c, 1, :, lanes] = rest


def nt(a, b):
    return lax.dot_general(a, b, (((1,), (1,)), ((), ())), preferred_element_type=jnp.float32)


def nn(a, b):
    return lax.dot_general(a, b, (((1,), (0,)), ((), ())), preferred_element_type=jnp.float32)


def tn(a, b):
    return lax.dot_general(a, b, (((0,), (0,)), ((), ())), preferred_element_type=jnp.float32)


def split_rows(row):
    high = row.astype(jnp.bfloat16)
    rest = (row - high.astype(jnp.float32)).astype(jnp.bfloat16)
    return high, rest


def toeplitz(kernel_row):
    spread = jnp.broadcast_to(kernel_row, (BLOCK, BLOCK))
    rolled = pltpu.roll(spread, 0, 1, stride=1, stride_axis=0)
    rows = lax.broadcasted_iota(jnp.int32, (BLOCK, BLOCK), 0)
    columns = lax.broadcasted_iota(jnp.int32, (BLOCK, BLOCK), 1)
    return jnp.where(columns >= rows, rolled, 0.0)


def put_rows(ref, c, places, group, block):
    for k in range(ref.shape[0]):
        ref[k, pl.ds(c, places, stride=group), :] = block[:, 128 * k : 128 * (k + 1)]


def get_rows(ref, c, places, group):
    chunks = [ref[k, pl.ds(c, places, stride=group), :] for k in range(ref.shape[0])]
    return jnp.concatenate(chunks, axis=1)


def get_step(ref, rows, half):
    count = ref.shape[0] // 2
    return jnp.concatenate([ref[half * count + k, rows, :] for k in range(count)], axis=1)


def put_step(ref, rows, half, block):
    count = ref.shape[0] // 2
    for k in range(count):
        ref[half * count + k, rows, :] = block[:, 128 * k : 128 * (k + 1)]


def gather_rows(pick, ref, c, mask):
    rows = [nn(p, ref[c, :, BLOCK * h : BLOCK * (h + 1)]) for h, p in enumerate(pick)]
    return sum(rows).astype(jnp.bfloat16) * mask


def scatter_rows(pick, ref, c, result, mask):
    low = result.astype(jnp.bfloat16) * mask
    for h, p in enumerate(pick):
        ref[c, :, BLOCK * h : BLOCK * (h + 1)] = tn(p, low).astype(jnp.bfloat16)


def forward_kernel(
    active, follows_ref, pick_ref, mask_ref, values_ref, low_ref, lam_ref, coef_ref,
    out_ref, start_ref, taps_ref, token_ref, up_ref, down_ref, work_ref,
):
    token_ref[...] = jnp.zeros_like(token_ref)
    places = pick_ref.shape[1]
    group, states = coef_ref.shape[0], coef_ref.shape[1] // 2
    if active < group:
        work_ref[...] = jnp.zeros_like(work_ref)
    mask = mask_ref[...]
    pick = [pick_ref[h] for h in range(pick_ref.shape[0])]
    each = range(active)
    spread = [gather_rows(pick, values_ref, c, mask) for c in each]
    for c in each:
        fill_tables(c, states, low_ref, up_ref, down_ref)
    for c in each:
        ends = nn(spread[c], down_ref[c, 0]) + nn(spread[c], down_ref[c, 1])
        put_rows(work_ref, c, places, group, ends)
    lam_re, lam_im = lam_ref[0, :, :states], lam_ref[0, :, states:]
    far_re, far_im = lam_ref[1, :, :states], lam_ref[1, :, states:]
    coef_re, coef_im = coef_ref[:, :states], coef_ref[:, states:]
    mix_re, mix_im = cmul(coef_re, coef_im, lam_re, lam_im)

    def advance(p, carry):
        re, im = carry
        rows = pl.ds(pl.multiple_of(p * group, group), group)
        keep = follows_ref[p]
        re, im = re * keep, im * keep
        start_ref[rows, :states] = re
        start_ref[rows, states:] = im
        far = cmul(re, im, far_re, far_im)
        new_re = far[0] + get_step(work_ref, rows, 0)
        new_im = far[1] + get_step(work_ref, rows, 1)
        mixed = cmul(re, im, mix_re, mix_im)
        put_step(work_ref, rows, 0, mixed[0])
        put_step(work_ref, rows, 1, -mixed[1])
        return new_re, new_im

    zero = jnp.zeros((group, states), jnp.float32)
    lax.fori_loop(0, places, advance, (zero, zero), unroll=4)
    carried, taps = [], []
    for c in each:
        row = jnp.concatenate([coef_ref[c : c + 1, :states], -coef_ref[c : c + 1, states:]], axis=1)
        high, rest = split_rows(row)
        rows = jnp.concatenate([high, rest, jnp.zeros((14, 2 * states), jnp.bfloat16)], axis=0)
        mixed = split_rows(get_rows(work_ref, c, places, group))
        stack = jnp.concatenate([mixed[0], rows, mixed[1]], axis=0)
        coarse = nt(stack, up_ref[c, 0])
        finer = nt(stack[: places + 16], up_ref[c, 1])
        carried.append(coarse[:places] + coarse[places + 16 :] + finer[:places])
        kernel_row = coarse[places : places + 16] + finer[places:]
        taps.append(split_rows(toeplitz(kernel_row[0:1] + kernel_row[1:2])))
        taps_ref[c] = taps[c][0]
    results = [
        carried[c] + nn(spread[c], taps[c][0]) + nn(spread[c], taps[c][1]) for c in each
    ]
    for c in each:
        scatter_rows(pick, out_ref, c, results[c], mask)


def backward_kernel(
    active, follows_ref, pick_ref, mask_ref, values_ref, grads_ref, low_ref, lam_ref, coef_ref,
    start_ref, taps_ref, out_ref, sum_ref, token_ref, up_ref, down_ref, work_ref,
):
    token_ref[...] = jnp.zeros_like(token_ref)
    places = pick_ref.shape[1]
    group, states = coef_ref.shape[0], coef_ref.shape[1] // 2
    if active < group:
        work_ref[...] = jnp.zeros_like(work_ref)
        sum_ref[...] = jnp.zeros_like(sum_ref)
    mask = mask_ref[...]
    pick = [pick_ref[h] for h in range(pick_ref.shape[0])]
    rows = lax.broadcasted_iota(jnp.int32, (BLOCK, BLOCK), 0)
    columns = lax.broadcasted_iota(jnp.int32, (BLOCK, BLOCK), 1)
    turn = (rows + columns == BLOCK - 1).astype(jnp.bfloat16)
    each = range(active)
    values = [gather_rows(pick, values_ref, c, mask) for c in each]
    grads = [gather_rows(pick, grads_ref, c, mask) for c in each]
    turned = [nn(values[c], turn).astype(jnp.bfloat16) for c in each]
    pairs = [tn(turned[c], grads[c]) for c in each]
    for c in each:
        fill_tables(c, states, low_ref, up_ref, down_ref)
    stacks = []
    for c in each:
        skewed = pltpu.roll(pairs[c], 1, 1, stride=1, stride_axis=0)
        lag_sum = jnp.sum(jnp.where(columns <= rows, skewed, 0.0), axis=0, keepdims=True)
        high, rest = split_rows(lag_sum)
        extra = jnp.concatenate([high, rest, jnp.zeros((14, BLOCK), jnp.bfloat16)], axis=0)
        stacks.append(jnp.concatenate([grads[c], extra], axis=0))
    for c in each:
        folded = nn(stacks[c], up_ref[c, 0])
        put_rows(work_ref, c, places, group, folded[:places])
        sum_ref[c : c + 1, :] = folded[places : places + 1] + folded[places + 1 : places + 2]
    lam_re, lam_im = lam_ref[0, :, :states], lam_ref[0, :, states:]
    far_re, far_im = lam_ref[1, :, :states], lam_ref[1, :, states:]
    coef_re, coef_im = coef_ref[:, :states], coef_ref[:, states:]

    def retreat(step, carry):
        re, im, total_re, total_im = carry
        p = places - 1 - step
        rows = pl.ds(pl.multiple_of(p * group, group), group)
        near = cmul(get_step(work_ref, rows, 0), get_step(work_ref, rows, 1), lam_re, lam_im)
        begin = start_ref[rows, :states], start_ref[rows, states:]
        product = cmul(begin[0], begin[1], near[0], near[1])
        mixed = cmul(re, im, coef_re, coef_im)
        put_step(work_ref, rows, 0, mixed[0])
        put_step(work_ref, rows, 1, -mixed[1])
        keep = follows_ref[p]
        far = cmul(re, im, far_re, far_im)
        return (
            (near[0] + far[0]) * keep,
            (near[1] + far[1]) * keep,
            total_re + product[0],
            total_im + product[1],
        )

    zero = jnp.zeros((group, states), jnp.float32)
    _, _, total_re, total_im = lax.fori_loop(0, places, retreat, (zero, zero, zero, zero), unroll=4)
    sum_ref[:, :states] = sum_ref[:, :states] + total_re
    sum_ref[:, states:] = -(sum_ref[:, states:] + total_im)
    near = [nt(grads[c], taps_ref[c]) for c in each]
    results = []
    for c in each:
        mixed = get_rows(work_ref, c, places, group).astype(jnp.bfloat16)
        results.append(nt(mixed, down_ref[c, 0]) + near[c])
    for c in each:
        scatter_rows(pick, out_ref, c, results[c], mask)


def whole(shape):
    return pl.BlockSpec(shape, lambda i: (0,) * len(shape))


def part(shape, place, dim=0):
    index = tuple(place if k == dim else 0 for k in range(len(shape)))
    return pl.BlockSpec(shape, lambda i: index)


class Parts:
    def __init__(self, kernel, name, inputs, results, scratch, parts, flops):
        self.kernel, self.name, self.inputs, self.results = kernel, name, inputs, results
        self.scratch, self.parts, self.flops = scratch, parts, flops
        self.done, self.outs, self.waits = 0, [], []

    def run(self, *waits):
        self.waits += waits
        if self.done < self.parts - 1:
            return self.call()
        return None

    def last(self, *waits):
        self.waits += waits
        return self.call()

    def call(self):
        k = self.done
        operands = [array for array, _ in self.inputs]
        specs = [spec(k) for _, spec in self.inputs]
        count, waits, before = len(operands), self.waits, list(self.outs)

        def body(*refs):
            self.kernel(*refs[:count], *refs[count + len(waits) + len(before) :])

        token = jax.ShapeDtypeStruct((8, 128), jnp.float32)
        *self.outs, token = pl.pallas_call(
            body,
            grid=(1,),
            in_specs=specs + [pl.BlockSpec(memory_space=pl.ANY)] * (len(waits) + len(before)),
            out_specs=[spec(k) for _, spec in self.results] + [whole((8, 128))],
            out_shape=[shape for shape, _ in self.results] + [token],
            input_output_aliases={count + len(waits) + n: n for n in range(len(before))},
            scratch_shapes=self.scratch,
            compiler_params=pltpu.CompilerParams(vmem_limit_bytes=48 * 2**20),
            cost_estimate=pl.CostEstimate(
                flops=self.flops, bytes_accessed=4 * 2**20, transcendentals=0
            ),
            name=self.name,
        )(*operands, *waits, *before)
        self.done, self.waits = k + 1, []
        return token


def scratches(active, group, places, states, tables):
    return [
        pltpu.VMEM((active, tables, BLOCK, 2 * states), jnp.bfloat16),
        pltpu.VMEM((active, tables, BLOCK, 2 * states), jnp.bfloat16),
        pltpu.VMEM((2 * states // 128, places * group, 128), jnp.float32),
    ]


def padded(values, lams, coefs):
    channels = values.shape[0]
    group, active = 8, min(8, channels)
    spare = max(0, group - channels)
    lams = jnp.pad(lams, ((0, 0), (0, spare), (0, 0)))
    coefs = jnp.pad(coefs, ((0, spare), (0, 0)))
    return group, active, spare, lams, coefs


def mix_forward(values, pieces, powers, lams, coefs):
    channels, shares, width = values.shape
    pick, mask, follows = pieces
    places, states = pick.shape[1], coefs.shape[1] // 2
    group, active, spare, lams, coefs = padded(values, lams, coefs)
    full = lambda shape: lambda k: whole(shape)
    inputs = [
        (follows, lambda k: pl.BlockSpec(memory_space=pltpu.SMEM)),
        (pick, full(pick.shape)),
        (mask, full((places, BLOCK))),
        (values, lambda k: part((active, shares, width), k)),
        (powers, lambda k: part((active, 16, 2 * states), k)),
        (lams, lambda k: part((2, group, 2 * states), k, 1)),
        (coefs, lambda k: part((group, 2 * states), k)),
    ]
    f32 = jnp.float32
    results = [
        (
            jax.ShapeDtypeStruct(values.shape, jnp.bfloat16),
            lambda k: part((active, shares, width), k),
        ),
        (
            jax.ShapeDtypeStruct((places * (channels + spare), 2 * states), f32),
            lambda k: part((places * group, 2 * states), k),
        ),
        (
            jax.ShapeDtypeStruct((channels, BLOCK, BLOCK), jnp.bfloat16),
            lambda k: part((active, BLOCK, BLOCK), k),
        ),
    ]
    return Parts(
        functools.partial(forward_kernel, active),
        "mix_forward",
        inputs,
        results,
        scratches(active, group, places, states, 2),
        channels // active,
        8 * 10**9,
    )


def mix_backward(values, grads, pieces, powers, lams, coefs, starts, taps):
    channels, shares, width = values.shape
    pick, mask, follows = pieces
    places, states = pick.shape[1], coefs.shape[1] // 2
    group, active, spare, lams, coefs = padded(values, lams, coefs)
    full = lambda shape: lambda k: whole(shape)
    inputs = [
        (follows, lambda k: pl.BlockSpec(memory_space=pltpu.SMEM)),
        (pick, full(pick.shape)),
        (mask, full((places, BLOCK))),
        (values, lambda k: part((active, shares, width), k)),
        (grads, lambda k: part((active, shares, width), k)),
        (powers, lambda k: part((active, 16, 2 * states), k)),
        (lams, lambda k: part((2, group, 2 * states), k, 1)),
        (coefs, lambda k: part((group, 2 * states), k)),
        (starts, lambda k: part((places * group, 2 * states), k)),
        (taps, lambda k: part((active, BLOCK, BLOCK), k)),
    ]
    results = [
        (
            jax.ShapeDtypeStruct(values.shape, jnp.bfloat16),
            lambda k: part((active, shares, width), k),
        ),
        (
            jax.ShapeDtypeStruct((channels + spare, 2 * states), jnp.float32),
            lambda k: part((group, 2 * states), k),
        ),
    ]
    return Parts(
        functools.partial(backward_kernel, active),
        "mix_backward",
        inputs,
        results,
        scratches(active, group, places, states, 1),
        channels // active,
        107 * 10**8,
    )


def mixer_inputs(poles, params):
    table = powers_of(poles)
    lams = jnp.stack([table[:, 1], table[:, 12]])
    coefs = jnp.concatenate([params[0], params[1]], axis=1)
    return table, lams, coefs


def adam_step(weight, gradient, first_moment, second, step_value, step_rate, decay_rate):
    first_new = beta_first * first_moment + (1.0 - beta_first) * gradient
    second_new = beta_second * second + (1.0 - beta_second) * gradient * gradient
    first_hat = first_new / (1.0 - jnp.power(beta_first, step_value))
    second_hat = second_new / (1.0 - jnp.power(beta_second, step_value))
    weight_new = weight - step_rate * (
        first_hat / (jnp.sqrt(second_hat) + epsilon_adam) + decay_rate * weight
    )
    return (weight_new, first_new, second_new)


class Cube:
    def __init__(self, tok_size):
        self.size = 2 * tok_size
        bits = tok_size.bit_length() - 1
        across = bits // 3
        self.xs = [1 + k for k in range(across)]
        self.ys = [1 + across + k for k in range(across)]
        self.zs = [1 + k for k in range(2 * across, bits)]
        self.place = lax.axis_index("tok") * 2 + lax.axis_index("rep")

    def bit(self, b):
        return lax.rem(lax.div(self.place, 1 << b), 2)

    def swap(self, block, b):
        return self.trade(block, 1 << b)

    def trade(self, block, mask):
        pairs = [(i, i ^ mask) for i in range(self.size)]
        return lax.ppermute(block, ("tok", "rep"), pairs)

    def halves(self, block, have, b):
        above = 1 << sum(1 for k in have if k > b)
        split = block.reshape((above, 2, -1) + block.shape[1:])
        index = self.bit(b)
        mine = lax.dynamic_index_in_dim(split, index, 1, keepdims=False)
        other = lax.dynamic_index_in_dim(split, 1 - index, 1, keepdims=False)
        shape = (-1,) + block.shape[1:]
        return mine.reshape(shape), other.reshape(shape)

    def split(self, block):
        stack = block.reshape((self.size, -1) + block.shape[1:])
        return self.halves(stack, range(self.size.bit_length() - 1), 0)

    def merge(self, mine, other):
        swapped = self.bit(0) == 1
        first, second = jnp.where(swapped, other, mine), jnp.where(swapped, mine, other)
        pair = jnp.stack([first, second], axis=1)
        return pair.reshape((-1,) + pair.shape[3:])


class Gather:
    def __init__(self, cube, shard, order):
        self.cube, self.order, self.have = cube, list(order), []
        self.block, self.going = shard[None], False

    def send(self, *waits):
        if self.order and not self.going:
            self.arriving = self.cube.swap(after(self.block, *waits), self.order[0])
            self.going = True

    def join(self, mine, other, b):
        above = 1 << sum(1 for k in self.have if k > b)
        shape = (above, 1, -1) + mine.shape[1:]
        first, second = mine.reshape(shape), other.reshape(shape)
        joined = jnp.where(
            self.cube.bit(b) == 1,
            jnp.concatenate([second, first], axis=1),
            jnp.concatenate([first, second], axis=1),
        )
        return joined.reshape((2 * mine.shape[0],) + mine.shape[1:])

    def take(self, *waits):
        self.send()
        if self.order:
            b, self.going = self.order.pop(0), False
            self.block = self.join(self.block, after(self.arriving, *waits), b)
            self.have.append(b)

    def direct(self, bits):
        masks = [sum(1 << b for k, b in enumerate(bits) if n >> k & 1) for n in range(1 << len(bits))]
        blocks = {m: self.cube.trade(self.block, m) if m else self.block for m in masks}
        for b in bits:
            blocks = {
                m: self.join(blocks[m], blocks[m | 1 << b], b) for m in blocks if not m >> b & 1
            }
            self.have.append(b)
        self.block = blocks[0]

    def rest(self):
        while self.order:
            self.take()

    def both(self):
        return self.block, self.cube.swap(self.block, 0)


class Scatter:
    def __init__(self, cube, keep, send, order, have, wide=()):
        self.cube, self.order, self.have = cube, list(order), list(have)
        self.keep, self.sent, self.wide = keep, send, wide
        self.going = False

    def send(self, *waits):
        if self.order and not self.going:
            self.arriving = self.cube.swap(after(self.sent, *waits), self.order[0])
            self.going = True

    def take(self, *waits):
        self.send()
        if not self.order:
            return
        b, self.going = self.order.pop(0), False
        self.have.remove(b)
        total = self.keep + after(self.arriving, *waits).astype(jnp.float32)
        if not self.order:
            self.keep, self.sent = total, total
            return
        self.keep, sent = self.cube.halves(total, self.have, self.order[0])
        self.sent = sent if self.order[0] in self.wide else sent.astype(jnp.bfloat16)

    def rest(self):
        while self.order:
            self.take()
        return self.keep[0]


def direct_sum(cube, total, have, bits, kind):
    have, parts = list(have), {0: total}
    for b in bits:
        halves = {m: cube.halves(part, have, b) for m, part in parts.items()}
        have.remove(b)
        parts = {m | k << b: halves[m][k] for m in halves for k in range(2)}
    keep = parts.pop(0)
    return keep + sum(cube.trade(p.astype(kind), m).astype(jnp.float32) for m, p in parts.items())


def after(block, *waits):
    return lax.optimization_barrier((block, *waits))[0] if waits else block


def gelu_parts(a):
    root = 0.7978845608028654
    square = a * a
    t = jnp.tanh(root * a * (1.0 + 0.044715 * square))
    half = 0.5 * (1.0 + t)
    slope = half + 0.5 * a * (1.0 - t * t) * root * (1.0 + 3.0 * 0.044715 * square)
    return a * half, slope


def gate_kernel(
    split, core_ref, normed_ref, state_refs, grad_ref, up_refs, expand_refs, down_refs,
    grad_out, up_out, gated_refs, state_outs, norm_outs, state_scratch, sum_scratch, norm_scratch,
):
    step, last = pl.program_id(0), pl.num_programs(0) - 1
    channels = state_refs[0].shape[0]
    swapped = core_ref[0] == 1

    @pl.when(step == 0)
    def _():
        for k in range(2):
            turned = state_refs[k][...].astype(jnp.float32).T
            state_scratch[:, channels * k : channels * (k + 1)] = turned.astype(jnp.bfloat16)
        sum_scratch[...] = jnp.zeros_like(sum_scratch)
        norm_scratch[...] = jnp.zeros_like(norm_scratch)

    def pair(mine, other):
        return jnp.where(swapped, other, mine), jnp.where(swapped, mine, other)

    rows = normed_ref.shape[1] // 2
    up_pre = nn(normed_ref[:, :rows], up_refs[0][...]) + nn(normed_ref[:, rows:], up_refs[1][...])
    if split:
        down = []
        for s in range(down_refs[0].shape[0]):
            down += pair(down_refs[0][s], down_refs[1][s])
        down = jnp.concatenate(down, axis=0)
    else:
        down = down_refs[0][...]
    gated_grad = nt(grad_ref[...], down)
    expanded = nn(state_scratch[:, :channels], expand_refs[0][...]) + nn(
        state_scratch[:, channels:], expand_refs[1][...]
    )
    upper, slope = gelu_parts(up_pre)
    expanded_grad = (gated_grad * upper).astype(jnp.bfloat16)
    grad_out[...] = expanded_grad
    up_pre_grad = (gated_grad * expanded * slope).astype(jnp.bfloat16)
    up_out[...] = up_pre_grad
    gated = (upper * expanded).T.astype(jnp.bfloat16)
    if split:
        size = gated_refs[0].shape[1]
        for s in range(gated_refs[0].shape[0]):
            first = gated[2 * s * size : (2 * s + 1) * size]
            second = gated[(2 * s + 1) * size : (2 * s + 2) * size]
            mine, other = pair(first, second)
            gated_refs[0][s] = mine
            gated_refs[1][s] = other
    else:
        gated_refs[0][...] = gated
    for k in range(2):
        sum_scratch[:, channels * k : channels * (k + 1)] += nt(expanded_grad, expand_refs[k][...])
        norm_scratch[:, rows * k : rows * (k + 1)] += nt(up_pre_grad, up_refs[k][...])

    @pl.when(step == last)
    def _():
        for k in range(2):
            total = sum_scratch[:, channels * k : channels * (k + 1)].T
            state_outs[k][...] = total.astype(jnp.bfloat16)
            norm_outs[k][...] = norm_scratch[:, rows * k : rows * (k + 1)].T


def gate(cube, normed, states, grad_rows, ups, expands, downs):
    tokens, width = grad_rows.shape
    hidden = ups[0].shape[1]
    split = downs[0].shape[1] % 16 == 0
    block = 2 * downs[0].shape[1] * max(1, 192 // downs[0].shape[1]) if split else 384
    low, f32 = jnp.bfloat16, jnp.float32
    full = lambda array: pl.BlockSpec(array.shape, lambda i: (0,) * array.ndim)
    if split:
        shards = block // (2 * downs[0].shape[1])
        down_spec = pl.BlockSpec((shards,) + downs[0].shape[1:], lambda i: (i, 0, 0))
        gated_shape = jax.ShapeDtypeStruct(downs[0].shape[:2] + (tokens,), low)
        gated_spec = pl.BlockSpec((shards, downs[0].shape[1], tokens), lambda i: (i, 0, 0))
        count = 2
    else:
        downs = [cube.merge(*downs)]
        down_spec = pl.BlockSpec((block, width), lambda i: (i, 0))
        gated_shape = jax.ShapeDtypeStruct((hidden, tokens), low)
        gated_spec = pl.BlockSpec((block, tokens), lambda i: (i, 0))
        count = 1
    columns = lambda array: pl.BlockSpec((array.shape[0], block), lambda i: (0, i))
    channels = states[0].shape[0]
    row_spec = pl.BlockSpec((tokens, block), lambda i: (0, i))
    state_shape = jax.ShapeDtypeStruct((channels, tokens), low)
    norm_shape = jax.ShapeDtypeStruct((width // 2, tokens), f32)

    def body(core, normed, s0, s1, grad, u0, u1, e0, e1, *refs):
        down_refs, refs = refs[:count], refs[count:]
        grad_out, up_out, gated_refs, refs = refs[0], refs[1], refs[2 : 2 + count], refs[2 + count :]
        gate_kernel(
            split, core, normed, (s0, s1), grad, (u0, u1), (e0, e1), down_refs,
            grad_out, up_out, gated_refs, refs[:2], refs[2:4], *refs[4:],
        )

    outs = pl.pallas_call(
        body,
        grid=(hidden // block,),
        in_specs=[pl.BlockSpec(memory_space=pltpu.SMEM), full(normed)]
        + [full(s) for s in states]
        + [full(grad_rows)]
        + [columns(u) for u in ups]
        + [columns(e) for e in expands]
        + [down_spec] * count,
        out_specs=[row_spec, row_spec]
        + [gated_spec] * count
        + [full(state_shape)] * 2
        + [full(norm_shape)] * 2,
        out_shape=[jax.ShapeDtypeStruct((tokens, hidden), low)] * 2
        + [gated_shape] * count
        + [state_shape] * 2
        + [norm_shape] * 2,
        scratch_shapes=[
            pltpu.VMEM((tokens, 2 * channels), low),
            pltpu.VMEM((tokens, 2 * channels), f32),
            pltpu.VMEM((tokens, width), f32),
        ],
        compiler_params=pltpu.CompilerParams(vmem_limit_bytes=48 * 2**20),
        cost_estimate=pl.CostEstimate(
            flops=10**6, bytes_accessed=2**10, transcendentals=0
        ),
        name="gate",
    )(cube.bit(0).reshape(1), normed, *states, grad_rows, *ups, *expands, *downs)
    grad_out, up_out = outs[:2]
    gated = outs[2 : 2 + count]
    gated = gated if split else cube.split(gated[0])
    return grad_out, up_out, gated, outs[2 + count : 4 + count], outs[4 + count :]


def value_kernel(
    width, grad_ref, pre_ref, value_refs, normed_refs, hat_refs, part_refs, keep_ref, send_ref, out_refs
):
    slope = gelu_parts(pre_ref[...])[1]
    grad = (grad_ref[...].astype(jnp.float32) * slope).astype(jnp.bfloat16)
    for k, ref in ((1, send_ref), (0, keep_ref)):
        total = part_refs[k][...] + nn(value_refs[k][:, :width], grad)
        out_refs[k][...] = total
        ref[:, :width] = nt(normed_refs[k][...], grad).astype(ref.dtype)
        lane = lax.broadcasted_iota(jnp.int32, (total.shape[0], 128), 1)
        gain = jnp.sum(total * hat_refs[k][...], axis=1, keepdims=True)
        shift = jnp.sum(total, axis=1, keepdims=True)
        columns = jnp.where(lane == 0, gain, jnp.where(lane == 1, shift, 0.0))
        ref[:, width:] = columns.astype(ref.dtype)


def value_grads(width, value_grad, value_pre, packs, normed, hats, parts):
    rows, tokens = normed[0].shape
    columns = packs[0].shape[1]

    def body(grad, pre, p0, p1, n0, n1, h0, h1, a0, a1, keep, send, g0, g1):
        value_kernel(
            width, grad, pre, (p0, p1), (n0, n1), (h0, h1), (a0, a1), keep, send, (g0, g1)
        )

    operands = (value_grad, value_pre, *packs, *normed, *hats, *parts)
    results = [((rows, columns), jnp.float32), ((rows, columns), jnp.bfloat16)]
    results += [((rows, tokens), jnp.float32)] * 2
    keep, send, first, second = pl.pallas_call(
        body,
        grid=(1,),
        in_specs=[whole(a.shape) for a in operands],
        out_specs=[whole(shape) for shape, _ in results],
        out_shape=[jax.ShapeDtypeStruct(shape, kind) for shape, kind in results],
        compiler_params=pltpu.CompilerParams(vmem_limit_bytes=48 * 2**20),
        cost_estimate=pl.CostEstimate(flops=10**6, bytes_accessed=2**10, transcendentals=0),
        name="value_grads",
    )(*operands)
    return keep, send, (first, second)


def products_kernel(bit_ref, own_send, own_keep, got_send, got_keep, own, got, send_ref, keep_ref):
    def product(a, b):
        flat = lambda ref: ref[...].reshape((-1, ref.shape[3]))
        return nn(flat(a), own[...]) + nn(flat(b), got[...])

    send_ref[...] = product(own_send, got_send).astype(jnp.bfloat16)
    keep_ref[...] = product(own_keep, got_keep)


def products(cube, lefts, rights, first, have):
    shards, rows, tokens = lefts[0].shape
    columns = rights[0].shape[1]
    above = 1 << sum(1 for k in have if k > first)
    shape = (shards // 2, rows, columns)
    if rows % 16:
        sides = [cube.halves(left, have, first) for left in lefts]
        keep, send = [
            sum(
                dot(pair[k].reshape((-1, tokens)), right, 1, 0)
                for pair, right in zip(sides, rights)
            ).reshape(shape)
            for k in range(2)
        ]
        return keep, send.astype(jnp.bfloat16)
    lefts = [left.reshape((above, 2, -1, tokens)) for left in lefts]
    side = (above, 1) + lefts[0].shape[2:]
    send_spec = pl.BlockSpec(side, lambda j, bit: (0, 1 - bit[0], 0, 0))
    keep_spec = pl.BlockSpec(side, lambda j, bit: (0, bit[0], 0, 0))
    block = min(columns, 1024)
    count = shards * rows // 2
    right_spec = pl.BlockSpec((tokens, block), lambda j, bit: (0, j))
    out_spec = pl.BlockSpec((count, block), lambda j, bit: (0, j))
    send, keep = pl.pallas_call(
        products_kernel,
        grid_spec=pltpu.PrefetchScalarGridSpec(
            num_scalar_prefetch=1,
            grid=(columns // block,),
            in_specs=[send_spec, keep_spec] * 2 + [right_spec] * 2,
            out_specs=[out_spec] * 2,
        ),
        out_shape=[
            jax.ShapeDtypeStruct((count, columns), jnp.bfloat16),
            jax.ShapeDtypeStruct((count, columns), jnp.float32),
        ],
        compiler_params=pltpu.CompilerParams(vmem_limit_bytes=48 * 2**20),
        cost_estimate=pl.CostEstimate(
            flops=10**6, bytes_accessed=2**10, transcendentals=0
        ),
        name="weight_grad",
    )(cube.bit(first).reshape(1), lefts[0], lefts[0], lefts[1], lefts[1], *rights)
    return keep.reshape(shape), send.reshape(shape)


def dot(a, b, a_dim, b_dim):
    return lax.dot_general(
        a, b, (((a_dim,), (b_dim,)), ((), ())), preferred_element_type=jnp.float32
    )


def per_device(
    tok_size,
    tokens,
    cotangent,
    lengths,
    up_weight,
    value_weight,
    expand_weight,
    down_weight,
    norm_params,
    state_params,
    state_poles,
    up_mean,
    up_square,
    value_mean,
    value_square,
    expand_mean,
    expand_square,
    down_mean,
    down_square,
    norm_mean,
    norm_square,
    state_mean,
    state_square,
):
    low = jnp.bfloat16
    cube = Cube(tok_size)
    xs, ys, zs = cube.xs, cube.ys, cube.zs
    down_zs, tok_bits = zs[::-1], xs + ys + zs
    nz, nx = len(zs), len(xs)

    def flat(block):
        return block.reshape((-1,) + block.shape[2:])

    def dots(lefts, rights, left_dim, right_dim):
        return dot(flat(lefts[0]), flat(rights[0]), left_dim, right_dim) + dot(
            flat(lefts[1]), flat(rights[1]), left_dim, right_dim
        )

    inner = value_weight.shape[1]
    norm_columns = jnp.pad(norm_params.T, ((0, 0), (0, 126)))
    packed = jnp.concatenate([value_weight, norm_columns], axis=1).astype(low)
    pack = Gather(cube, packed, xs + ys + down_zs)
    up = Gather(cube, up_weight.astype(low), down_zs + xs + ys)
    down = Gather(cube, down_weight.astype(low), down_zs + ys + xs)
    expand = Gather(cube, expand_weight.astype(low), xs + ys + down_zs)

    grad_rows = cotangent[0]
    token_rows = tokens[0].astype(jnp.float32)
    width = token_rows.shape[1]
    average = jnp.mean(token_rows, axis=1)
    centered = token_rows - average[:, None]
    scale = lax.rsqrt(jnp.mean(centered * centered, axis=1) + epsilon_norm)
    hats = [
        (part.astype(jnp.float32) - average) * scale for part in cube.split(tokens[0].T)
    ]

    expand.send()
    pack.direct(zs)
    up.send(pack.block)
    down.send(pack.block)
    if expand.order[1:]:
        expand.take(pack.block)
        expand.send()
    pack.direct(xs + ys)
    packs = pack.both()
    up.take()
    down.take()
    up.send()
    down.send()
    values = [pack[:, :, :inner] for pack in packs]
    gains = [pack[:, :, inner : inner + 1].astype(jnp.float32) for pack in packs]
    shifts = [pack[:, :, inner + 1 : inner + 2].astype(jnp.float32) for pack in packs]
    normed = [(h * g + b).astype(low) for h, g, b in zip(hats, gains, shifts)]
    value_preactivation = dots(values, normed, 0, 0)
    value_act = gelu_curve(value_preactivation)
    value_low = after(value_act.astype(low), up.block, down.block)
    channel_values = lax.all_to_all(value_low, "tok", split_axis=0, concat_axis=1, tiled=True)

    for _ in range(nz - 2):
        up.take(value_low)
        down.take(value_low)
        up.send()
        down.send()
    for _ in range(2 * nx - 2):
        expand.take(value_low)
        expand.send()
    poles, coefs = lax.optimization_barrier((state_poles, state_params, value_low))[:2]
    channels, length = channel_values.shape
    blocked = (channels, tok_size, length // tok_size)
    pieces = pieces_of(lengths[0], length, tok_size)
    powers, lams, coefs = mixer_inputs(poles, coefs)
    channel_values = channel_values.reshape(blocked)
    normed_rows = jnp.concatenate([flat(side).T for side in normed], axis=1)
    normed_swapped = cube.swap(normed[1], 0)
    columns_swapped = cube.swap(grad_rows, 0)
    mixer = mix_forward(channel_values, pieces, powers, lams, coefs)

    def run(*waits):
        token = mixer.run(*waits)
        return [] if token is None else [token]

    up.take(powers)
    down.take(powers)
    expand.take(powers)
    up.send()
    down.send()
    expand.send()
    token = run(up.block, down.block, expand.block)
    for _ in range(nx):
        up.take(*token)
        down.take(*token)
        up.send()
        down.send()
    expand.take(*token)
    if expand.order:
        expand.send()
    token = run(up.block, down.block, expand.block)
    token = run(*token)
    if expand.order:
        expand.take(*token)
    mixer.last(*token, expand.block, normed_swapped, columns_swapped, normed_rows)
    state_out, starts, taps = mixer.outs
    for part in (up, down):
        part.arriving = after(part.arriving, state_out)
    token_states = lax.all_to_all(
        state_out.reshape(channels, length), "tok", split_axis=1, concat_axis=0, tiled=True
    )
    state_sides = cube.split(token_states)
    expand.rest()
    up.rest()
    down.rest()
    ups, downs, expands = up.both(), down.both(), expand.both()

    expanded_grad, up_pre_grad, gated_sides, state_grads, ups_grads = gate(
        cube,
        normed_rows,
        [flat(side) for side in state_sides],
        grad_rows,
        [flat(side) for side in ups],
        [flat(side) for side in expands],
        downs,
    )
    state_grad = cube.merge(*[g.reshape(state_sides[0].shape) for g in state_grads])
    gated_swapped = cube.swap(gated_sides[1], 0)
    expanded_swapped = cube.swap(expanded_grad, 0)
    up_pre_swapped = cube.swap(after(up_pre_grad, gated_swapped), 0)
    state_swapped = cube.swap(state_sides[1], 0)

    def scatter(lefts, rights, order):
        keep, send = products(cube, lefts, rights, order[0], tok_bits)
        return Scatter(cube, keep, send, order, tok_bits)

    down_sums = scatter(
        (gated_sides[0], gated_swapped),
        (grad_rows, columns_swapped),
        xs + ys + zs,
    )
    up_sums = scatter((normed[0], normed_swapped), (up_pre_grad, up_pre_swapped), ys + xs + zs)
    expand_sums = scatter(
        (state_sides[0], state_swapped), (expanded_grad, expanded_swapped), zs + ys + xs
    )
    channel_grad = lax.all_to_all(state_grad, "tok", split_axis=0, concat_axis=1, tiled=True)
    channel_grad = channel_grad.reshape(blocked)
    down_sums.send()
    up_sums.send()
    expand_sums.send(channel_grad)
    mixer = mix_backward(
        channel_values, channel_grad, pieces, powers, lams, coefs, starts, taps
    )
    token = run(up_sums.sent, down_sums.sent, expand_sums.sent)
    token = run(*token)
    token = run(*token)
    expand_sums.take(*token)
    expand_sums.send()
    mixer.last(*token, expand_sums.sent)
    value_grad_channels, param_grad = mixer.outs
    states = param_grad.shape[1] // 2
    param_grad = jnp.stack([param_grad[:channels, :states], param_grad[:channels, states:]])
    param_sum = param_grad + cube.swap(param_grad, 0)
    mixed = value_grad_channels
    for _ in range(nx):
        for sums in (down_sums, up_sums):
            sums.take(mixed)
            sums.send()
    value_grad_channels = after(value_grad_channels, down_sums.sent, up_sums.sent)
    value_grad = lax.all_to_all(
        value_grad_channels.reshape(channels, length),
        "tok",
        split_axis=1,
        concat_axis=0,
        tiled=True,
    )
    for _ in range(nx):
        down_sums.take(value_grad_channels)
        down_sums.send()
    value_grad = after(value_grad, down_sums.sent)
    keep, send, normed_grads = value_grads(
        inner,
        value_grad,
        value_preactivation,
        [flat(part) for part in packs],
        [flat(part) for part in normed],
        [flat(part) for part in hats],
        ups_grads,
    )
    normed_grads = [g.reshape(h.shape) for g, h in zip(normed_grads, hats)]
    keep, send = [part.reshape(hats[0].shape[:2] + (-1,)) for part in (keep, send)]
    packed_sum = keep + cube.swap(send, 0).astype(jnp.float32)
    core_sum = packed_sum
    for _ in range(nx):
        for sums in (up_sums, expand_sums):
            sums.take(send)
            sums.send()
    packed_sum = after(packed_sum, up_sums.sent, down_sums.sent)
    packed_sum = direct_sum(cube, packed_sum, tok_bits, xs + ys, low)
    gated_late = after(gated_sides[0], packed_sum), gated_sides[1]
    layer_out = (token_rows + dots(gated_late, downs, 0, 0)).astype(low)[None]
    normed_grads = [after(g, packed_sum) for g in normed_grads]
    down_sums.take(core_sum)
    down_sums.send()
    for sums in (up_sums, expand_sums):
        sums.take(packed_sum)
        sums.send()
    packed_sum = direct_sum(cube, packed_sum, zs, zs, jnp.float32)[0]
    up_sum, down_sum, expand_sum = [
        sums.rest() for sums in (up_sums, down_sums, expand_sums)
    ]
    value_sum = packed_sum[:, :inner]
    norm_sum = packed_sum[:, inner : inner + 2].T
    hat_grads = [g * gain for g, gain in zip(normed_grads, gains)]
    hat_mean = sum(jnp.sum(d, axis=(0, 1)) for d in hat_grads) / width
    hat_product = sum(jnp.sum(d * h, axis=(0, 1)) for d, h in zip(hat_grads, hats)) / width
    row_grads = [(d - hat_mean - h * hat_product) * scale for d, h in zip(hat_grads, hats)]
    token_grad = (cube.merge(*row_grads).T + grad_rows.astype(jnp.float32))[None]
    step_value = jnp.float32(STEP)
    up_next, up_mean_next, up_square_next = adam_step(
        up_weight, up_sum, up_mean, up_square, step_value, 0.08, 0.1
    )
    value_next, value_mean_next, value_square_next = adam_step(
        value_weight, value_sum, value_mean, value_square, step_value, 0.08, 0.1
    )
    expand_next, expand_mean_next, expand_square_next = adam_step(
        expand_weight, expand_sum, expand_mean, expand_square, step_value, 0.08, 0.1
    )
    down_next, down_mean_next, down_square_next = adam_step(
        down_weight, down_sum, down_mean, down_square, step_value, 0.08, 0.1
    )
    norm_params, norm_mean, norm_square = lax.optimization_barrier(
        (norm_params, norm_mean, norm_square, core_sum)
    )[:3]
    norm_next, norm_mean_next, norm_square_next = adam_step(
        norm_params, norm_sum, norm_mean, norm_square, step_value, 1.0, 0.0
    )
    state_next, state_mean_next, state_square_next = adam_step(
        state_params, param_sum, state_mean, state_square, step_value, 0.006, 0.0
    )
    return (
        layer_out,
        token_grad,
        up_next,
        up_mean_next,
        up_square_next,
        value_next,
        value_mean_next,
        value_square_next,
        expand_next,
        expand_mean_next,
        expand_square_next,
        down_next,
        down_mean_next,
        down_square_next,
        norm_next,
        norm_mean_next,
        norm_square_next,
        state_next,
        state_mean_next,
        state_square_next,
    )


def solution(mesh):
    placed = (
        P("rep", "tok", None),
        P("rep", "tok", None),
        P("rep", None),
        P(("tok", "rep"), None),
        P(("tok", "rep"), None),
        P(("tok", "rep"), None),
        P(("tok", "rep"), None),
        P(None, ("tok", "rep")),
        P(None, "tok", None),
        P(None, "tok", None),
        P(("tok", "rep"), None),
        P(("tok", "rep"), None),
        P(("tok", "rep"), None),
        P(("tok", "rep"), None),
        P(("tok", "rep"), None),
        P(("tok", "rep"), None),
        P(("tok", "rep"), None),
        P(("tok", "rep"), None),
        P(None, ("tok", "rep")),
        P(None, ("tok", "rep")),
        P(None, "tok", None),
        P(None, "tok", None),
    )
    return jax.shard_map(
        functools.partial(per_device, mesh.shape["tok"]),
        mesh=mesh,
        in_specs=placed,
        out_specs=(
            P("rep", "tok", None),
            P("rep", "tok", None),
            P(("tok", "rep"), None),
            P(("tok", "rep"), None),
            P(("tok", "rep"), None),
            P(("tok", "rep"), None),
            P(("tok", "rep"), None),
            P(("tok", "rep"), None),
            P(("tok", "rep"), None),
            P(("tok", "rep"), None),
            P(("tok", "rep"), None),
            P(("tok", "rep"), None),
            P(("tok", "rep"), None),
            P(("tok", "rep"), None),
            P(None, ("tok", "rep")),
            P(None, ("tok", "rep")),
            P(None, ("tok", "rep")),
            P(None, "tok", None),
            P(None, "tok", None),
            P(None, "tok", None),
        ),
        check_vma=False,
    )
```

```python
import functools

import jax
import jax.numpy as jnp
from jax import lax
from jax.experimental import pallas as pl
from jax.experimental.pallas import tpu as pltpu
from jax.sharding import PartitionSpec as P

BLOCK = 128
STEP = 5


epsilon_norm = 1e-05
epsilon_adam = 1e-08
beta_first = 0.9
beta_second = 0.999


def gelu_curve(values):
    return jax.nn.gelu(values, approximate=True)


def pieces_of(lengths_row, length, shares):
    blocks = length // BLOCK
    each = blocks // shares
    items = lengths_row.shape[0]
    ends = jnp.cumsum(lengths_row, dtype=jnp.int32)
    heads = BLOCK * jnp.arange(blocks, dtype=jnp.int32)
    head_rank = jnp.arange(blocks, dtype=jnp.int32) + jnp.sum(
        (ends[None, :] < heads[:, None]).astype(jnp.int32), axis=1
    )
    end_rank = jnp.arange(items, dtype=jnp.int32) + jnp.sum(
        (heads[None, :] <= ends[:, None]).astype(jnp.int32), axis=1
    )
    places = jnp.arange(blocks + items, dtype=jnp.int32)[:, None]
    starts = jnp.sum(jnp.where(head_rank[None, :] == places, heads[None, :], 0), axis=1) + jnp.sum(
        jnp.where(end_rank[None, :] == places, ends[None, :], 0), axis=1
    )
    stops = jnp.concatenate([starts[1:], jnp.full((1,), length, jnp.int32)])
    owner = starts // BLOCK
    segment = jnp.sum((ends[None, :] <= starts[:, None]).astype(jnp.int32), axis=1)
    positions = owner[:, None] * BLOCK + jnp.arange(BLOCK, dtype=jnp.int32)[None, :]
    mask = (positions >= starts[:, None]) & (positions < stops[:, None])
    heads = each * jnp.arange(shares, dtype=jnp.int32)[None, None, :]
    heads = heads + jnp.arange(each, dtype=jnp.int32)[:, None, None]
    pick = owner[None, :, None] == heads
    follows = (segment[1:] == segment[:-1]) & (owner[1:] != owner[:-1])
    follows = jnp.concatenate([jnp.zeros((1,), bool), follows])
    return (
        pick.astype(jnp.bfloat16),
        mask.astype(jnp.bfloat16),
        follows.astype(jnp.float32),
    )


def powers_of(poles):
    decay_rate = jnp.exp(poles[0])[:, None, :]
    frequency = poles[1][:, None, :]
    lags = jnp.array([0, 1, 2, 3, 4, 5, 6, 7, 8, 16, 32, 64, 128, 128, 128, 128], jnp.float32)
    lags = lags[None, :, None]
    magnitude = jnp.exp(-decay_rate * lags)
    phase = frequency * lags
    return jnp.concatenate([magnitude * jnp.cos(phase), magnitude * jnp.sin(phase)], axis=2)


def cmul(ar, ai, br, bi):
    return ar * br - ai * bi, ar * bi + ai * br


def fill_tables(c, states, low_ref, up_ref, down_ref):
    for lane in range(0, states, 128):
        re_lanes = pl.ds(lane, 128)
        im_lanes = pl.ds(states + lane, 128)
        base = low_ref[c, 0:8, re_lanes], low_ref[c, 0:8, im_lanes]
        for ref, forward in ((up_ref, True), (down_ref, False)):
            if forward:
                re, im = base
            else:
                re = jnp.concatenate([base[0][7 - k : 8 - k] for k in range(8)], axis=0)
                im = jnp.concatenate([base[1][7 - k : 8 - k] for k in range(8)], axis=0)
            for k in range(4):
                nr, ni = cmul(
                    re,
                    im,
                    low_ref[c, 8 + k : 9 + k, re_lanes],
                    low_ref[c, 8 + k : 9 + k, im_lanes],
                )
                if forward:
                    re = jnp.concatenate([re, nr], axis=0)
                    im = jnp.concatenate([im, ni], axis=0)
                else:
                    re = jnp.concatenate([nr, re], axis=0)
                    im = jnp.concatenate([ni, im], axis=0)
            for lanes, entries in ((re_lanes, re), (im_lanes, im)):
                high, rest = split_rows(entries)
                ref[c, 0, :, lanes] = high
                if ref.shape[1] > 1:
                    ref[c, 1, :, lanes] = rest


def nt(a, b):
    return lax.dot_general(a, b, (((1,), (1,)), ((), ())), preferred_element_type=jnp.float32)


def nn(a, b):
    return lax.dot_general(a, b, (((1,), (0,)), ((), ())), preferred_element_type=jnp.float32)


def tn(a, b):
    return lax.dot_general(a, b, (((0,), (0,)), ((), ())), preferred_element_type=jnp.float32)


def split_rows(row):
    high = row.astype(jnp.bfloat16)
    rest = (row - high.astype(jnp.float32)).astype(jnp.bfloat16)
    return high, rest


def toeplitz(kernel_row):
    spread = jnp.broadcast_to(kernel_row, (BLOCK, BLOCK))
    rolled = pltpu.roll(spread, 0, 1, stride=1, stride_axis=0)
    rows = lax.broadcasted_iota(jnp.int32, (BLOCK, BLOCK), 0)
    columns = lax.broadcasted_iota(jnp.int32, (BLOCK, BLOCK), 1)
    return jnp.where(columns >= rows, rolled, 0.0)


def put_rows(ref, c, places, group, block):
    for k in range(ref.shape[0]):
        ref[k, pl.ds(c, places, stride=group), :] = block[:, 128 * k : 128 * (k + 1)]


def get_rows(ref, c, places, group):
    chunks = [ref[k, pl.ds(c, places, stride=group), :] for k in range(ref.shape[0])]
    return jnp.concatenate(chunks, axis=1)


def get_step(ref, rows, half):
    count = ref.shape[0] // 2
    return jnp.concatenate([ref[half * count + k, rows, :] for k in range(count)], axis=1)


def put_step(ref, rows, half, block):
    count = ref.shape[0] // 2
    for k in range(count):
        ref[half * count + k, rows, :] = block[:, 128 * k : 128 * (k + 1)]


def gather_rows(pick, ref, c, mask):
    rows = [nn(p, ref[c, :, BLOCK * h : BLOCK * (h + 1)]) for h, p in enumerate(pick)]
    return sum(rows).astype(jnp.bfloat16) * mask


def scatter_rows(pick, ref, c, result, mask):
    low = result.astype(jnp.bfloat16) * mask
    for h, p in enumerate(pick):
        ref[c, :, BLOCK * h : BLOCK * (h + 1)] = tn(p, low).astype(jnp.bfloat16)


def forward_kernel(
    active, follows_ref, pick_ref, mask_ref, values_ref, low_ref, lam_ref, coef_ref,
    out_ref, start_ref, taps_ref, token_ref, up_ref, down_ref, work_ref,
):
    token_ref[...] = jnp.zeros_like(token_ref)
    places = pick_ref.shape[1]
    group, states = coef_ref.shape[0], coef_ref.shape[1] // 2
    if active < group:
        work_ref[...] = jnp.zeros_like(work_ref)
    mask = mask_ref[...]
    pick = [pick_ref[h] for h in range(pick_ref.shape[0])]
    each = range(active)
    spread = [gather_rows(pick, values_ref, c, mask) for c in each]
    for c in each:
        fill_tables(c, states, low_ref, up_ref, down_ref)
    for c in each:
        ends = nn(spread[c], down_ref[c, 0]) + nn(spread[c], down_ref[c, 1])
        put_rows(work_ref, c, places, group, ends)
    lam_re, lam_im = lam_ref[0, :, :states], lam_ref[0, :, states:]
    far_re, far_im = lam_ref[1, :, :states], lam_ref[1, :, states:]
    coef_re, coef_im = coef_ref[:, :states], coef_ref[:, states:]
    mix_re, mix_im = cmul(coef_re, coef_im, lam_re, lam_im)

    def advance(p, carry):
        re, im = carry
        rows = pl.ds(pl.multiple_of(p * group, group), group)
        keep = follows_ref[p]
        re, im = re * keep, im * keep
        start_ref[rows, :states] = re
        start_ref[rows, states:] = im
        far = cmul(re, im, far_re, far_im)
        new_re = far[0] + get_step(work_ref, rows, 0)
        new_im = far[1] + get_step(work_ref, rows, 1)
        mixed = cmul(re, im, mix_re, mix_im)
        put_step(work_ref, rows, 0, mixed[0])
        put_step(work_ref, rows, 1, -mixed[1])
        return new_re, new_im

    zero = jnp.zeros((group, states), jnp.float32)
    lax.fori_loop(0, places, advance, (zero, zero), unroll=4)
    carried, taps = [], []
    for c in each:
        row = jnp.concatenate([coef_ref[c : c + 1, :states], -coef_ref[c : c + 1, states:]], axis=1)
        high, rest = split_rows(row)
        rows = jnp.concatenate([high, rest, jnp.zeros((14, 2 * states), jnp.bfloat16)], axis=0)
        mixed = split_rows(get_rows(work_ref, c, places, group))
        stack = jnp.concatenate([mixed[0], rows, mixed[1]], axis=0)
        coarse = nt(stack, up_ref[c, 0])
        finer = nt(stack[: places + 16], up_ref[c, 1])
        carried.append(coarse[:places] + coarse[places + 16 :] + finer[:places])
        kernel_row = coarse[places : places + 16] + finer[places:]
        taps.append(split_rows(toeplitz(kernel_row[0:1] + kernel_row[1:2])))
        taps_ref[c] = taps[c][0]
    results = [
        carried[c] + nn(spread[c], taps[c][0]) + nn(spread[c], taps[c][1]) for c in each
    ]
    for c in each:
        scatter_rows(pick, out_ref, c, results[c], mask)


def backward_kernel(
    active, follows_ref, pick_ref, mask_ref, values_ref, grads_ref, low_ref, lam_ref, coef_ref,
    start_ref, taps_ref, out_ref, sum_ref, token_ref, up_ref, down_ref, work_ref,
):
    token_ref[...] = jnp.zeros_like(token_ref)
    places = pick_ref.shape[1]
    group, states = coef_ref.shape[0], coef_ref.shape[1] // 2
    if active < group:
        work_ref[...] = jnp.zeros_like(work_ref)
        sum_ref[...] = jnp.zeros_like(sum_ref)
    mask = mask_ref[...]
    pick = [pick_ref[h] for h in range(pick_ref.shape[0])]
    rows = lax.broadcasted_iota(jnp.int32, (BLOCK, BLOCK), 0)
    columns = lax.broadcasted_iota(jnp.int32, (BLOCK, BLOCK), 1)
    turn = (rows + columns == BLOCK - 1).astype(jnp.bfloat16)
    each = range(active)
    values = [gather_rows(pick, values_ref, c, mask) for c in each]
    grads = [gather_rows(pick, grads_ref, c, mask) for c in each]
    turned = [nn(values[c], turn).astype(jnp.bfloat16) for c in each]
    pairs = [tn(turned[c], grads[c]) for c in each]
    for c in each:
        fill_tables(c, states, low_ref, up_ref, down_ref)
    stacks = []
    for c in each:
        skewed = pltpu.roll(pairs[c], 1, 1, stride=1, stride_axis=0)
        lag_sum = jnp.sum(jnp.where(columns <= rows, skewed, 0.0), axis=0, keepdims=True)
        high, rest = split_rows(lag_sum)
        extra = jnp.concatenate([high, rest, jnp.zeros((14, BLOCK), jnp.bfloat16)], axis=0)
        stacks.append(jnp.concatenate([grads[c], extra], axis=0))
    for c in each:
        folded = nn(stacks[c], up_ref[c, 0])
        put_rows(work_ref, c, places, group, folded[:places])
        sum_ref[c : c + 1, :] = folded[places : places + 1] + folded[places + 1 : places + 2]
    lam_re, lam_im = lam_ref[0, :, :states], lam_ref[0, :, states:]
    far_re, far_im = lam_ref[1, :, :states], lam_ref[1, :, states:]
    coef_re, coef_im = coef_ref[:, :states], coef_ref[:, states:]

    def retreat(step, carry):
        re, im, total_re, total_im = carry
        p = places - 1 - step
        rows = pl.ds(pl.multiple_of(p * group, group), group)
        near = cmul(get_step(work_ref, rows, 0), get_step(work_ref, rows, 1), lam_re, lam_im)
        begin = start_ref[rows, :states], start_ref[rows, states:]
        product = cmul(begin[0], begin[1], near[0], near[1])
        mixed = cmul(re, im, coef_re, coef_im)
        put_step(work_ref, rows, 0, mixed[0])
        put_step(work_ref, rows, 1, -mixed[1])
        keep = follows_ref[p]
        far = cmul(re, im, far_re, far_im)
        return (
            (near[0] + far[0]) * keep,
            (near[1] + far[1]) * keep,
            total_re + product[0],
            total_im + product[1],
        )

    zero = jnp.zeros((group, states), jnp.float32)
    _, _, total_re, total_im = lax.fori_loop(0, places, retreat, (zero, zero, zero, zero), unroll=4)
    sum_ref[:, :states] = sum_ref[:, :states] + total_re
    sum_ref[:, states:] = -(sum_ref[:, states:] + total_im)
    near = [nt(grads[c], taps_ref[c]) for c in each]
    results = []
    for c in each:
        mixed = get_rows(work_ref, c, places, group).astype(jnp.bfloat16)
        results.append(nt(mixed, down_ref[c, 0]) + near[c])
    for c in each:
        scatter_rows(pick, out_ref, c, results[c], mask)


def whole(shape):
    return pl.BlockSpec(shape, lambda i: (0,) * len(shape))


def part(shape, place, dim=0):
    index = tuple(place if k == dim else 0 for k in range(len(shape)))
    return pl.BlockSpec(shape, lambda i: index)


class Parts:
    def __init__(self, kernel, name, inputs, results, scratch, parts, flops):
        self.kernel, self.name, self.inputs, self.results = kernel, name, inputs, results
        self.scratch, self.parts, self.flops = scratch, parts, flops
        rows = scratch[-1].shape
        self.room = 20 * 2**20 + 14 * rows[0] * rows[1] * rows[2]
        self.done, self.outs, self.waits = 0, [], []

    def run(self, *waits):
        self.waits += waits
        if self.done < self.parts - 1:
            return self.call()
        return None

    def last(self, *waits):
        self.waits += waits
        return self.call()

    def call(self):
        k = self.done
        operands = [array for array, _ in self.inputs]
        specs = [spec(k) for _, spec in self.inputs]
        count, waits, before = len(operands), self.waits, list(self.outs)

        def body(*refs):
            self.kernel(*refs[:count], *refs[count + len(waits) + len(before) :])

        token = jax.ShapeDtypeStruct((8, 128), jnp.float32)
        *self.outs, token = pl.pallas_call(
            body,
            grid=(1,),
            in_specs=specs + [pl.BlockSpec(memory_space=pl.ANY)] * (len(waits) + len(before)),
            out_specs=[spec(k) for _, spec in self.results] + [whole((8, 128))],
            out_shape=[shape for shape, _ in self.results] + [token],
            input_output_aliases={count + len(waits) + n: n for n in range(len(before))},
            scratch_shapes=self.scratch,
            compiler_params=pltpu.CompilerParams(vmem_limit_bytes=self.room),
            cost_estimate=pl.CostEstimate(
                flops=self.flops, bytes_accessed=4 * 2**20, transcendentals=0
            ),
            name=self.name,
        )(*operands, *waits, *before)
        self.done, self.waits = k + 1, []
        return token


def scratches(active, group, places, states, tables):
    return [
        pltpu.VMEM((active, tables, BLOCK, 2 * states), jnp.bfloat16),
        pltpu.VMEM((active, tables, BLOCK, 2 * states), jnp.bfloat16),
        pltpu.VMEM((2 * states // 128, places * group, 128), jnp.float32),
    ]


def padded(values, lams, coefs):
    channels = values.shape[0]
    group, active = 8, min(8, channels)
    spare = max(0, group - channels)
    lams = jnp.pad(lams, ((0, 0), (0, spare), (0, 0)))
    coefs = jnp.pad(coefs, ((0, spare), (0, 0)))
    return group, active, spare, lams, coefs


def mix_forward(values, pieces, powers, lams, coefs):
    channels, shares, width = values.shape
    pick, mask, follows = pieces
    places, states = pick.shape[1], coefs.shape[1] // 2
    group, active, spare, lams, coefs = padded(values, lams, coefs)
    full = lambda shape: lambda k: whole(shape)
    inputs = [
        (follows, lambda k: pl.BlockSpec(memory_space=pltpu.SMEM)),
        (pick, full(pick.shape)),
        (mask, full((places, BLOCK))),
        (values, lambda k: part((active, shares, width), k)),
        (powers, lambda k: part((active, 16, 2 * states), k)),
        (lams, lambda k: part((2, group, 2 * states), k, 1)),
        (coefs, lambda k: part((group, 2 * states), k)),
    ]
    f32 = jnp.float32
    results = [
        (
            jax.ShapeDtypeStruct(values.shape, jnp.bfloat16),
            lambda k: part((active, shares, width), k),
        ),
        (
            jax.ShapeDtypeStruct((places * (channels + spare), 2 * states), f32),
            lambda k: part((places * group, 2 * states), k),
        ),
        (
            jax.ShapeDtypeStruct((channels, BLOCK, BLOCK), jnp.bfloat16),
            lambda k: part((active, BLOCK, BLOCK), k),
        ),
    ]
    return Parts(
        functools.partial(forward_kernel, active),
        "mix_forward",
        inputs,
        results,
        scratches(active, group, places, states, 2),
        channels // active,
        8 * 10**9,
    )


def mix_backward(values, grads, pieces, powers, lams, coefs, starts, taps):
    channels, shares, width = values.shape
    pick, mask, follows = pieces
    places, states = pick.shape[1], coefs.shape[1] // 2
    group, active, spare, lams, coefs = padded(values, lams, coefs)
    full = lambda shape: lambda k: whole(shape)
    inputs = [
        (follows, lambda k: pl.BlockSpec(memory_space=pltpu.SMEM)),
        (pick, full(pick.shape)),
        (mask, full((places, BLOCK))),
        (values, lambda k: part((active, shares, width), k)),
        (grads, lambda k: part((active, shares, width), k)),
        (powers, lambda k: part((active, 16, 2 * states), k)),
        (lams, lambda k: part((2, group, 2 * states), k, 1)),
        (coefs, lambda k: part((group, 2 * states), k)),
        (starts, lambda k: part((places * group, 2 * states), k)),
        (taps, lambda k: part((active, BLOCK, BLOCK), k)),
    ]
    results = [
        (
            jax.ShapeDtypeStruct(values.shape, jnp.bfloat16),
            lambda k: part((active, shares, width), k),
        ),
        (
            jax.ShapeDtypeStruct((channels + spare, 2 * states), jnp.float32),
            lambda k: part((group, 2 * states), k),
        ),
    ]
    return Parts(
        functools.partial(backward_kernel, active),
        "mix_backward",
        inputs,
        results,
        scratches(active, group, places, states, 1),
        channels // active,
        107 * 10**8,
    )


def mixer_inputs(poles, params):
    table = powers_of(poles)
    lams = jnp.stack([table[:, 1], table[:, 12]])
    coefs = jnp.concatenate([params[0], params[1]], axis=1)
    return table, lams, coefs


def adam_step(weight, gradient, first_moment, second, step_value, step_rate, decay_rate):
    first_new = beta_first * first_moment + (1.0 - beta_first) * gradient
    second_new = beta_second * second + (1.0 - beta_second) * gradient * gradient
    first_hat = first_new / (1.0 - jnp.power(beta_first, step_value))
    second_hat = second_new / (1.0 - jnp.power(beta_second, step_value))
    weight_new = weight - step_rate * (
        first_hat / (jnp.sqrt(second_hat) + epsilon_adam) + decay_rate * weight
    )
    return (weight_new, first_new, second_new)


class Cube:
    def __init__(self, tok_size):
        self.size = 2 * tok_size
        bits = tok_size.bit_length() - 1
        across = bits // 3
        self.xs = [1 + k for k in range(across)]
        self.ys = [1 + across + k for k in range(across)]
        self.zs = [1 + k for k in range(2 * across, bits)]
        self.place = lax.axis_index("tok") * 2 + lax.axis_index("rep")

    def bit(self, b):
        return lax.rem(lax.div(self.place, 1 << b), 2)

    def swap(self, block, b):
        return self.trade(block, 1 << b)

    def trade(self, block, mask):
        pairs = [(i, i ^ mask) for i in range(self.size)]
        return lax.ppermute(block, ("tok", "rep"), pairs)

    def halves(self, block, have, b):
        above = 1 << sum(1 for k in have if k > b)
        split = block.reshape((above, 2, -1) + block.shape[1:])
        index = self.bit(b)
        mine = lax.dynamic_index_in_dim(split, index, 1, keepdims=False)
        other = lax.dynamic_index_in_dim(split, 1 - index, 1, keepdims=False)
        shape = (-1,) + block.shape[1:]
        return mine.reshape(shape), other.reshape(shape)

    def split(self, block):
        stack = block.reshape((self.size, -1) + block.shape[1:])
        return self.halves(stack, range(self.size.bit_length() - 1), 0)

    def merge(self, mine, other):
        swapped = self.bit(0) == 1
        first, second = jnp.where(swapped, other, mine), jnp.where(swapped, mine, other)
        pair = jnp.stack([first, second], axis=1)
        return pair.reshape((-1,) + pair.shape[3:])


class Gather:
    def __init__(self, cube, shard, order):
        self.cube, self.order, self.have = cube, list(order), []
        self.block, self.going = shard[None], False

    def send(self, *waits):
        if self.order and not self.going:
            self.arriving = self.cube.swap(after(self.block, *waits), self.order[0])
            self.going = True

    def join(self, mine, other, b):
        above = 1 << sum(1 for k in self.have if k > b)
        shape = (above, 1, -1) + mine.shape[1:]
        first, second = mine.reshape(shape), other.reshape(shape)
        joined = jnp.where(
            self.cube.bit(b) == 1,
            jnp.concatenate([second, first], axis=1),
            jnp.concatenate([first, second], axis=1),
        )
        return joined.reshape((2 * mine.shape[0],) + mine.shape[1:])

    def take(self, *waits):
        self.send()
        if self.order:
            b, self.going = self.order.pop(0), False
            self.block = self.join(self.block, after(self.arriving, *waits), b)
            self.have.append(b)

    def direct(self, bits):
        masks = [sum(1 << b for k, b in enumerate(bits) if n >> k & 1) for n in range(1 << len(bits))]
        blocks = {m: self.cube.trade(self.block, m) if m else self.block for m in masks}
        for b in bits:
            blocks = {
                m: self.join(blocks[m], blocks[m | 1 << b], b) for m in blocks if not m >> b & 1
            }
            self.have.append(b)
        self.block = blocks[0]

    def rest(self):
        while self.order:
            self.take()

    def both(self):
        return self.block, self.cube.swap(self.block, 0)


class Scatter:
    def __init__(self, cube, keep, send, order, have, wide=()):
        self.cube, self.order, self.have = cube, list(order), list(have)
        self.keep, self.sent, self.wide = keep, send, wide
        self.going = False

    def send(self, *waits):
        if self.order and not self.going:
            self.arriving = self.cube.swap(after(self.sent, *waits), self.order[0])
            self.going = True

    def take(self, *waits):
        self.send()
        if not self.order:
            return
        b, self.going = self.order.pop(0), False
        self.have.remove(b)
        total = self.keep + after(self.arriving, *waits).astype(jnp.float32)
        if not self.order:
            self.keep, self.sent = total, total
            return
        self.keep, sent = self.cube.halves(total, self.have, self.order[0])
        self.sent = sent if self.order[0] in self.wide else sent.astype(jnp.bfloat16)

    def rest(self):
        while self.order:
            self.take()
        return self.keep[0]


def direct_sum(cube, total, have, bits, kind):
    have, parts = list(have), {0: total}
    for b in bits:
        halves = {m: cube.halves(part, have, b) for m, part in parts.items()}
        have.remove(b)
        parts = {m | k << b: halves[m][k] for m in halves for k in range(2)}
    keep = parts.pop(0)
    return keep + sum(cube.trade(p.astype(kind), m).astype(jnp.float32) for m, p in parts.items())


def after(block, *waits):
    return lax.optimization_barrier((block, *waits))[0] if waits else block


def gelu_parts(a):
    root = 0.7978845608028654
    square = a * a
    t = jnp.tanh(root * a * (1.0 + 0.044715 * square))
    half = 0.5 * (1.0 + t)
    slope = half + 0.5 * a * (1.0 - t * t) * root * (1.0 + 3.0 * 0.044715 * square)
    return a * half, slope


def gate_kernel(
    split, core_ref, normed_ref, state_refs, grad_ref, up_refs, expand_refs, down_refs,
    grad_out, up_out, gated_refs, state_outs, norm_outs, state_scratch, sum_scratch, norm_scratch,
):
    step, last = pl.program_id(0), pl.num_programs(0) - 1
    channels = state_refs[0].shape[0]
    swapped = core_ref[0] == 1

    @pl.when(step == 0)
    def _():
        for k in range(2):
            turned = state_refs[k][...].astype(jnp.float32).T
            state_scratch[:, channels * k : channels * (k + 1)] = turned.astype(jnp.bfloat16)
        sum_scratch[...] = jnp.zeros_like(sum_scratch)
        norm_scratch[...] = jnp.zeros_like(norm_scratch)

    def pair(mine, other):
        return jnp.where(swapped, other, mine), jnp.where(swapped, mine, other)

    rows = normed_ref.shape[1] // 2
    up_pre = nn(normed_ref[:, :rows], up_refs[0][...]) + nn(normed_ref[:, rows:], up_refs[1][...])
    if split:
        down = []
        for s in range(down_refs[0].shape[0]):
            down += pair(down_refs[0][s], down_refs[1][s])
        down = jnp.concatenate(down, axis=0)
    else:
        down = down_refs[0][...]
    gated_grad = nt(grad_ref[...], down)
    expanded = nn(state_scratch[:, :channels], expand_refs[0][...]) + nn(
        state_scratch[:, channels:], expand_refs[1][...]
    )
    upper, slope = gelu_parts(up_pre)
    expanded_grad = (gated_grad * upper).astype(jnp.bfloat16)
    grad_out[...] = expanded_grad
    up_pre_grad = (gated_grad * expanded * slope).astype(jnp.bfloat16)
    up_out[...] = up_pre_grad
    gated = (upper * expanded).T.astype(jnp.bfloat16)
    if split:
        size = gated_refs[0].shape[1]
        for s in range(gated_refs[0].shape[0]):
            first = gated[2 * s * size : (2 * s + 1) * size]
            second = gated[(2 * s + 1) * size : (2 * s + 2) * size]
            mine, other = pair(first, second)
            gated_refs[0][s] = mine
            gated_refs[1][s] = other
    else:
        gated_refs[0][...] = gated
    for k in range(2):
        sum_scratch[:, channels * k : channels * (k + 1)] += nt(expanded_grad, expand_refs[k][...])
        norm_scratch[:, rows * k : rows * (k + 1)] += nt(up_pre_grad, up_refs[k][...])

    @pl.when(step == last)
    def _():
        for k in range(2):
            total = sum_scratch[:, channels * k : channels * (k + 1)].T
            state_outs[k][...] = total.astype(jnp.bfloat16)
            norm_outs[k][...] = norm_scratch[:, rows * k : rows * (k + 1)].T


def gate(cube, normed, states, grad_rows, ups, expands, downs):
    tokens, width = grad_rows.shape
    hidden = ups[0].shape[1]
    split = downs[0].shape[1] % 16 == 0
    block = 2 * downs[0].shape[1] * max(1, 192 // downs[0].shape[1]) if split else 384
    low, f32 = jnp.bfloat16, jnp.float32
    full = lambda array: pl.BlockSpec(array.shape, lambda i: (0,) * array.ndim)
    if split:
        shards = block // (2 * downs[0].shape[1])
        down_spec = pl.BlockSpec((shards,) + downs[0].shape[1:], lambda i: (i, 0, 0))
        gated_shape = jax.ShapeDtypeStruct(downs[0].shape[:2] + (tokens,), low)
        gated_spec = pl.BlockSpec((shards, downs[0].shape[1], tokens), lambda i: (i, 0, 0))
        count = 2
    else:
        downs = [cube.merge(*downs)]
        down_spec = pl.BlockSpec((block, width), lambda i: (i, 0))
        gated_shape = jax.ShapeDtypeStruct((hidden, tokens), low)
        gated_spec = pl.BlockSpec((block, tokens), lambda i: (i, 0))
        count = 1
    columns = lambda array: pl.BlockSpec((array.shape[0], block), lambda i: (0, i))
    channels = states[0].shape[0]
    row_spec = pl.BlockSpec((tokens, block), lambda i: (0, i))
    state_shape = jax.ShapeDtypeStruct((channels, tokens), low)
    norm_shape = jax.ShapeDtypeStruct((width // 2, tokens), f32)

    def body(core, normed, s0, s1, grad, u0, u1, e0, e1, *refs):
        down_refs, refs = refs[:count], refs[count:]
        grad_out, up_out, gated_refs, refs = refs[0], refs[1], refs[2 : 2 + count], refs[2 + count :]
        gate_kernel(
            split, core, normed, (s0, s1), grad, (u0, u1), (e0, e1), down_refs,
            grad_out, up_out, gated_refs, refs[:2], refs[2:4], *refs[4:],
        )

    outs = pl.pallas_call(
        body,
        grid=(hidden // block,),
        in_specs=[pl.BlockSpec(memory_space=pltpu.SMEM), full(normed)]
        + [full(s) for s in states]
        + [full(grad_rows)]
        + [columns(u) for u in ups]
        + [columns(e) for e in expands]
        + [down_spec] * count,
        out_specs=[row_spec, row_spec]
        + [gated_spec] * count
        + [full(state_shape)] * 2
        + [full(norm_shape)] * 2,
        out_shape=[jax.ShapeDtypeStruct((tokens, hidden), low)] * 2
        + [gated_shape] * count
        + [state_shape] * 2
        + [norm_shape] * 2,
        scratch_shapes=[
            pltpu.VMEM((tokens, 2 * channels), low),
            pltpu.VMEM((tokens, 2 * channels), f32),
            pltpu.VMEM((tokens, width), f32),
        ],
        compiler_params=pltpu.CompilerParams(vmem_limit_bytes=48 * 2**20),
        cost_estimate=pl.CostEstimate(
            flops=10**6, bytes_accessed=2**10, transcendentals=0
        ),
        name="gate",
    )(cube.bit(0).reshape(1), normed, *states, grad_rows, *ups, *expands, *downs)
    grad_out, up_out = outs[:2]
    gated = outs[2 : 2 + count]
    gated = gated if split else cube.split(gated[0])
    return grad_out, up_out, gated, outs[2 + count : 4 + count], outs[4 + count :]


def value_kernel(
    width, grad_ref, pre_ref, value_refs, normed_refs, hat_refs, part_refs, keep_ref, send_ref, out_refs
):
    slope = gelu_parts(pre_ref[...])[1]
    grad = (grad_ref[...].astype(jnp.float32) * slope).astype(jnp.bfloat16)
    for k, ref in ((1, send_ref), (0, keep_ref)):
        total = part_refs[k][...] + nn(value_refs[k][:, :width], grad)
        out_refs[k][...] = total
        ref[:, :width] = nt(normed_refs[k][...], grad).astype(ref.dtype)
        lane = lax.broadcasted_iota(jnp.int32, (total.shape[0], 128), 1)
        gain = jnp.sum(total * hat_refs[k][...], axis=1, keepdims=True)
        shift = jnp.sum(total, axis=1, keepdims=True)
        columns = jnp.where(lane == 0, gain, jnp.where(lane == 1, shift, 0.0))
        ref[:, width:] = columns.astype(ref.dtype)


def value_grads(width, value_grad, value_pre, packs, normed, hats, parts):
    rows, tokens = normed[0].shape
    columns = packs[0].shape[1]

    def body(grad, pre, p0, p1, n0, n1, h0, h1, a0, a1, keep, send, g0, g1):
        value_kernel(
            width, grad, pre, (p0, p1), (n0, n1), (h0, h1), (a0, a1), keep, send, (g0, g1)
        )

    operands = (value_grad, value_pre, *packs, *normed, *hats, *parts)
    results = [((rows, columns), jnp.float32), ((rows, columns), jnp.bfloat16)]
    results += [((rows, tokens), jnp.float32)] * 2
    keep, send, first, second = pl.pallas_call(
        body,
        grid=(1,),
        in_specs=[whole(a.shape) for a in operands],
        out_specs=[whole(shape) for shape, _ in results],
        out_shape=[jax.ShapeDtypeStruct(shape, kind) for shape, kind in results],
        compiler_params=pltpu.CompilerParams(vmem_limit_bytes=48 * 2**20),
        cost_estimate=pl.CostEstimate(flops=10**6, bytes_accessed=2**10, transcendentals=0),
        name="value_grads",
    )(*operands)
    return keep, send, (first, second)


def products_kernel(bit_ref, own_send, own_keep, got_send, got_keep, own, got, send_ref, keep_ref):
    def product(a, b):
        flat = lambda ref: ref[...].reshape((-1, ref.shape[3]))
        return nn(flat(a), own[...]) + nn(flat(b), got[...])

    send_ref[...] = product(own_send, got_send).astype(jnp.bfloat16)
    keep_ref[...] = product(own_keep, got_keep)


def products(cube, lefts, rights, first, have):
    shards, rows, tokens = lefts[0].shape
    columns = rights[0].shape[1]
    above = 1 << sum(1 for k in have if k > first)
    shape = (shards // 2, rows, columns)
    if rows % 16:
        sides = [cube.halves(left, have, first) for left in lefts]
        keep, send = [
            sum(
                dot(pair[k].reshape((-1, tokens)), right, 1, 0)
                for pair, right in zip(sides, rights)
            ).reshape(shape)
            for k in range(2)
        ]
        return keep, send.astype(jnp.bfloat16)
    lefts = [left.reshape((above, 2, -1, tokens)) for left in lefts]
    side = (above, 1) + lefts[0].shape[2:]
    send_spec = pl.BlockSpec(side, lambda j, bit: (0, 1 - bit[0], 0, 0))
    keep_spec = pl.BlockSpec(side, lambda j, bit: (0, bit[0], 0, 0))
    block = min(columns, 1024)
    count = shards * rows // 2
    right_spec = pl.BlockSpec((tokens, block), lambda j, bit: (0, j))
    out_spec = pl.BlockSpec((count, block), lambda j, bit: (0, j))
    send, keep = pl.pallas_call(
        products_kernel,
        grid_spec=pltpu.PrefetchScalarGridSpec(
            num_scalar_prefetch=1,
            grid=(columns // block,),
            in_specs=[send_spec, keep_spec] * 2 + [right_spec] * 2,
            out_specs=[out_spec] * 2,
        ),
        out_shape=[
            jax.ShapeDtypeStruct((count, columns), jnp.bfloat16),
            jax.ShapeDtypeStruct((count, columns), jnp.float32),
        ],
        compiler_params=pltpu.CompilerParams(vmem_limit_bytes=48 * 2**20),
        cost_estimate=pl.CostEstimate(
            flops=10**6, bytes_accessed=2**10, transcendentals=0
        ),
        name="weight_grad",
    )(cube.bit(first).reshape(1), lefts[0], lefts[0], lefts[1], lefts[1], *rights)
    return keep.reshape(shape), send.reshape(shape)


def dot(a, b, a_dim, b_dim):
    return lax.dot_general(
        a, b, (((a_dim,), (b_dim,)), ((), ())), preferred_element_type=jnp.float32
    )


def per_device(
    tok_size,
    tokens,
    cotangent,
    lengths,
    up_weight,
    value_weight,
    expand_weight,
    down_weight,
    norm_params,
    state_params,
    state_poles,
    up_mean,
    up_square,
    value_mean,
    value_square,
    expand_mean,
    expand_square,
    down_mean,
    down_square,
    norm_mean,
    norm_square,
    state_mean,
    state_square,
):
    low = jnp.bfloat16
    cube = Cube(tok_size)
    xs, ys, zs = cube.xs, cube.ys, cube.zs
    down_zs, tok_bits = zs[::-1], xs + ys + zs
    nz, nx = len(zs), len(xs)

    def flat(block):
        return block.reshape((-1,) + block.shape[2:])

    def dots(lefts, rights, left_dim, right_dim):
        return dot(flat(lefts[0]), flat(rights[0]), left_dim, right_dim) + dot(
            flat(lefts[1]), flat(rights[1]), left_dim, right_dim
        )

    inner = value_weight.shape[1]
    norm_columns = jnp.pad(norm_params.T, ((0, 0), (0, 126)))
    packed = jnp.concatenate([value_weight, norm_columns], axis=1).astype(low)
    pack = Gather(cube, packed, xs + ys + down_zs)
    up = Gather(cube, up_weight.astype(low), down_zs + xs + ys)
    down = Gather(cube, down_weight.astype(low), down_zs + ys + xs)
    expand = Gather(cube, expand_weight.astype(low), xs + ys + down_zs)

    grad_rows = cotangent[0]
    token_rows = tokens[0].astype(jnp.float32)
    width = token_rows.shape[1]
    average = jnp.mean(token_rows, axis=1)
    centered = token_rows - average[:, None]
    scale = lax.rsqrt(jnp.mean(centered * centered, axis=1) + epsilon_norm)
    hats = [
        (part.astype(jnp.float32) - average) * scale for part in cube.split(tokens[0].T)
    ]

    expand.send()
    pack.direct(zs)
    up.send(pack.block)
    down.send(pack.block)
    if expand.order[1:]:
        expand.take(pack.block)
        expand.send()
    pack.direct(xs + ys)
    packs = pack.both()
    up.take()
    down.take()
    up.send()
    down.send()
    values = [pack[:, :, :inner] for pack in packs]
    gains = [pack[:, :, inner : inner + 1].astype(jnp.float32) for pack in packs]
    shifts = [pack[:, :, inner + 1 : inner + 2].astype(jnp.float32) for pack in packs]
    normed = [(h * g + b).astype(low) for h, g, b in zip(hats, gains, shifts)]
    value_preactivation = dots(values, normed, 0, 0)
    value_act = gelu_curve(value_preactivation)
    value_low = after(value_act.astype(low), up.block, down.block)
    channel_values = lax.all_to_all(value_low, "tok", split_axis=0, concat_axis=1, tiled=True)

    for _ in range(nz - 2):
        up.take(value_low)
        down.take(value_low)
        up.send()
        down.send()
    for _ in range(2 * nx - 2):
        expand.take(value_low)
        expand.send()
    poles, coefs = lax.optimization_barrier((state_poles, state_params, value_low))[:2]
    channels, length = channel_values.shape
    blocked = (channels, tok_size, length // tok_size)
    pieces = pieces_of(lengths[0], length, tok_size)
    powers, lams, coefs = mixer_inputs(poles, coefs)
    channel_values = channel_values.reshape(blocked)
    normed_rows = jnp.concatenate([flat(side).T for side in normed], axis=1)
    normed_swapped = cube.swap(normed[1], 0)
    columns_swapped = cube.swap(grad_rows, 0)
    mixer = mix_forward(channel_values, pieces, powers, lams, coefs)

    def run(*waits):
        token = mixer.run(*waits)
        return [] if token is None else [token]

    up.take(powers)
    down.take(powers)
    expand.take(powers)
    up.send()
    down.send()
    expand.send()
    token = run(up.block, down.block, expand.block)
    for _ in range(nx):
        up.take(*token)
        down.take(*token)
        up.send()
        down.send()
    expand.take(*token)
    if expand.order:
        expand.send()
    token = run(up.block, down.block, expand.block)
    token = run(*token)
    if expand.order:
        expand.take(*token)
    mixer.last(*token, expand.block, normed_swapped, columns_swapped, normed_rows)
    state_out, starts, taps = mixer.outs
    for part in (up, down):
        part.arriving = after(part.arriving, state_out)
    token_states = lax.all_to_all(
        state_out.reshape(channels, length), "tok", split_axis=1, concat_axis=0, tiled=True
    )
    state_sides = cube.split(token_states)
    expand.rest()
    up.rest()
    down.rest()
    ups, downs, expands = up.both(), down.both(), expand.both()

    expanded_grad, up_pre_grad, gated_sides, state_grads, ups_grads = gate(
        cube,
        normed_rows,
        [flat(side) for side in state_sides],
        grad_rows,
        [flat(side) for side in ups],
        [flat(side) for side in expands],
        downs,
    )
    state_grad = cube.merge(*[g.reshape(state_sides[0].shape) for g in state_grads])
    gated_swapped = cube.swap(gated_sides[1], 0)
    expanded_swapped = cube.swap(expanded_grad, 0)
    up_pre_swapped = cube.swap(after(up_pre_grad, gated_swapped), 0)
    state_swapped = cube.swap(state_sides[1], 0)

    def scatter(lefts, rights, order):
        keep, send = products(cube, lefts, rights, order[0], tok_bits)
        return Scatter(cube, keep, send, order, tok_bits)

    down_sums = scatter(
        (gated_sides[0], gated_swapped),
        (grad_rows, columns_swapped),
        xs + ys + zs,
    )
    up_sums = scatter((normed[0], normed_swapped), (up_pre_grad, up_pre_swapped), ys + xs + zs)
    expand_sums = scatter(
        (state_sides[0], state_swapped), (expanded_grad, expanded_swapped), zs + ys + xs
    )
    channel_grad = lax.all_to_all(state_grad, "tok", split_axis=0, concat_axis=1, tiled=True)
    channel_grad = channel_grad.reshape(blocked)
    down_sums.send()
    up_sums.send()
    expand_sums.send(channel_grad)
    mixer = mix_backward(
        channel_values, channel_grad, pieces, powers, lams, coefs, starts, taps
    )
    token = run(up_sums.sent, down_sums.sent, expand_sums.sent)
    token = run(*token)
    token = run(*token)
    expand_sums.take(*token)
    expand_sums.send()
    mixer.last(*token, expand_sums.sent)
    value_grad_channels, param_grad = mixer.outs
    states = param_grad.shape[1] // 2
    param_grad = jnp.stack([param_grad[:channels, :states], param_grad[:channels, states:]])
    param_sum = param_grad + cube.swap(param_grad, 0)
    mixed = value_grad_channels
    for _ in range(nx):
        for sums in (down_sums, up_sums):
            sums.take(mixed)
            sums.send()
    value_grad_channels = after(value_grad_channels, down_sums.sent, up_sums.sent)
    value_grad = lax.all_to_all(
        value_grad_channels.reshape(channels, length),
        "tok",
        split_axis=1,
        concat_axis=0,
        tiled=True,
    )
    for _ in range(nx):
        down_sums.take(value_grad_channels)
        down_sums.send()
    value_grad = after(value_grad, down_sums.sent)
    keep, send, normed_grads = value_grads(
        inner,
        value_grad,
        value_preactivation,
        [flat(part) for part in packs],
        [flat(part) for part in normed],
        [flat(part) for part in hats],
        ups_grads,
    )
    normed_grads = [g.reshape(h.shape) for g, h in zip(normed_grads, hats)]
    keep, send = [part.reshape(hats[0].shape[:2] + (-1,)) for part in (keep, send)]
    packed_sum = keep + cube.swap(send, 0).astype(jnp.float32)
    core_sum = packed_sum
    for _ in range(nx):
        for sums in (up_sums, expand_sums):
            sums.take(send)
            sums.send()
    packed_sum = after(packed_sum, up_sums.sent, down_sums.sent)
    packed_sum = direct_sum(cube, packed_sum, tok_bits, xs + ys, low)
    gated_late = after(gated_sides[0], packed_sum), gated_sides[1]
    layer_out = (token_rows + dots(gated_late, downs, 0, 0)).astype(low)[None]
    normed_grads = [after(g, packed_sum) for g in normed_grads]
    down_sums.take(core_sum)
    down_sums.send()
    for sums in (up_sums, expand_sums):
        sums.take(packed_sum)
        sums.send()
    packed_sum = direct_sum(cube, packed_sum, zs, zs, jnp.float32)[0]
    up_sum, down_sum, expand_sum = [
        sums.rest() for sums in (up_sums, down_sums, expand_sums)
    ]
    value_sum = packed_sum[:, :inner]
    norm_sum = packed_sum[:, inner : inner + 2].T
    hat_grads = [g * gain for g, gain in zip(normed_grads, gains)]
    hat_mean = sum(jnp.sum(d, axis=(0, 1)) for d in hat_grads) / width
    hat_product = sum(jnp.sum(d * h, axis=(0, 1)) for d, h in zip(hat_grads, hats)) / width
    row_grads = [(d - hat_mean - h * hat_product) * scale for d, h in zip(hat_grads, hats)]
    token_grad = (cube.merge(*row_grads).T + grad_rows.astype(jnp.float32))[None]
    step_value = jnp.float32(STEP)
    up_next, up_mean_next, up_square_next = adam_step(
        up_weight, up_sum, up_mean, up_square, step_value, 0.08, 0.1
    )
    value_next, value_mean_next, value_square_next = adam_step(
        value_weight, value_sum, value_mean, value_square, step_value, 0.08, 0.1
    )
    expand_next, expand_mean_next, expand_square_next = adam_step(
        expand_weight, expand_sum, expand_mean, expand_square, step_value, 0.08, 0.1
    )
    down_next, down_mean_next, down_square_next = adam_step(
        down_weight, down_sum, down_mean, down_square, step_value, 0.08, 0.1
    )
    norm_params, norm_mean, norm_square = lax.optimization_barrier(
        (norm_params, norm_mean, norm_square, core_sum)
    )[:3]
    norm_next, norm_mean_next, norm_square_next = adam_step(
        norm_params, norm_sum, norm_mean, norm_square, step_value, 1.0, 0.0
    )
    state_next, state_mean_next, state_square_next = adam_step(
        state_params, param_sum, state_mean, state_square, step_value, 0.006, 0.0
    )
    return (
        layer_out,
        token_grad,
        up_next,
        up_mean_next,
        up_square_next,
        value_next,
        value_mean_next,
        value_square_next,
        expand_next,
        expand_mean_next,
        expand_square_next,
        down_next,
        down_mean_next,
        down_square_next,
        norm_next,
        norm_mean_next,
        norm_square_next,
        state_next,
        state_mean_next,
        state_square_next,
    )


def solution(mesh):
    placed = (
        P("rep", "tok", None),
        P("rep", "tok", None),
        P("rep", None),
        P(("tok", "rep"), None),
        P(("tok", "rep"), None),
        P(("tok", "rep"), None),
        P(("tok", "rep"), None),
        P(None, ("tok", "rep")),
        P(None, "tok", None),
        P(None, "tok", None),
        P(("tok", "rep"), None),
        P(("tok", "rep"), None),
        P(("tok", "rep"), None),
        P(("tok", "rep"), None),
        P(("tok", "rep"), None),
        P(("tok", "rep"), None),
        P(("tok", "rep"), None),
        P(("tok", "rep"), None),
        P(None, ("tok", "rep")),
        P(None, ("tok", "rep")),
        P(None, "tok", None),
        P(None, "tok", None),
    )
    return jax.shard_map(
        functools.partial(per_device, mesh.shape["tok"]),
        mesh=mesh,
        in_specs=placed,
        out_specs=(
            P("rep", "tok", None),
            P("rep", "tok", None),
            P(("tok", "rep"), None),
            P(("tok", "rep"), None),
            P(("tok", "rep"), None),
            P(("tok", "rep"), None),
            P(("tok", "rep"), None),
            P(("tok", "rep"), None),
            P(("tok", "rep"), None),
            P(("tok", "rep"), None),
            P(("tok", "rep"), None),
            P(("tok", "rep"), None),
            P(("tok", "rep"), None),
            P(("tok", "rep"), None),
            P(None, ("tok", "rep")),
            P(None, ("tok", "rep")),
            P(None, ("tok", "rep")),
            P(None, "tok", None),
            P(None, "tok", None),
            P(None, "tok", None),
        ),
        check_vma=False,
    )
```
